32 devices in a mesh: dp: 16 (over z, x, core), mp: 2 (over y).
Axes of the slice: x: 2, y: 2, z: 4, core: 2. Of those that a mesh axis runs over, the one named last changes fastest.
Arguments:
- tokens: bfloat16 [8192, 8192], P('dp', 'mp'), may hold values from -6 to 6
- upstream: bfloat16 [8192, 8192], P('dp', 'mp'), may hold values from -6 to 6
- first_factor: bfloat16 [32, 256, 256], P('mp', 'dp'), may hold values from -0.375 to 0.375
- second_factor: bfloat16 [32, 256, 256], P('mp', 'dp'), may hold values from -0.375 to 0.375
Outputs:
- mixed: bfloat16 [8192, 8192], P('dp', 'mp')
- grad_tokens: bfloat16 [8192, 8192], P('dp', 'mp')
- grad_first: float32 [32, 256, 256], P('mp', 'dp')
- grad_second: float32 [32, 256, 256], P('mp', 'dp')
The draws below stay inside these ranges and needn't reach their ends.
All inputs are finite; a program needn't handle non-finite values.
Results may differ from the reference program's by a relative error of at most 0.0056.
Values may be sent and summed in bfloat16 or wider, within the bound.
No kernel may reach another device: no remote copies, remote signals or barrier semaphores. Data moves between devices by JAX's collectives and lax.ppermute only.
A program may use at most 128 MiB of HBM per device.

```python
import math
import jax
import jax.numpy as jnp
from jax import lax

BLOCKS = 32
BLK = 256
TOK_DEV = 512
D = 8192
TOKENS = 8192


def shard_levels(own_key, shape, cuts, smallest, largest):
    def one(axis_at, shards_of):
        draws = jax.random.uniform(jax.random.fold_in(jax.random.fold_in(own_key, 6), axis_at), (shards_of,), jnp.float32, smallest / len(cuts), largest / len(cuts))
        return jnp.repeat(jnp.exp(draws), shape[axis_at] // shards_of).reshape((-1,) + (1,) * (len(shape) - axis_at - 1))

    factor_of = one(*cuts[0])
    for cut in cuts[1:]:
        factor_of = factor_of * one(*cut)
    return factor_of


def noise(stream_key, extent, deviation, limit, cuts=(), kind=jnp.bfloat16):
    values = deviation * jax.random.normal(stream_key, extent, jnp.float32)
    if cuts:
        values = values * shard_levels(stream_key, extent, cuts, -0.22, 0.18)
    return jnp.clip(values, -limit, limit).astype(kind)


def setup_inputs(seed: int = 0) -> dict:
    key_list = jax.random.split(jax.random.key(seed), 5)
    tokens = noise(key_list[0], (TOKENS, D), 1.0, 6.0, ((0, 16), (1, 2)))
    upstream = noise(key_list[1], (TOKENS, D), 1.0, 6.0, ((0, 16), (1, 2)))
    first_factor = noise(key_list[2], (BLOCKS, BLK, BLK), BLK ** -0.5, 0.375, ((0, 2), (1, 16)))
    second_factor = noise(key_list[3], (BLOCKS, BLK, BLK), BLK ** -0.5, 0.375, ((0, 2), (1, 16)))
    return {"tokens": tokens, "upstream": upstream, "first_factor": first_factor, "second_factor": second_factor}


def gelu_exact(value):
    return jax.nn.gelu(value, approximate=False)

def reference(tokens, upstream, first_factor, second_factor):
    left_blocks = first_factor.astype(jnp.float32)
    right_blocks = second_factor.astype(jnp.float32)

    def block_step(carry, paired):
        grad_left, grad_right = carry
        row_block, cotangent = paired
        tok_count = row_block.shape[0]
        shaped = row_block.reshape(tok_count, BLOCKS, BLK).astype(jnp.float32)
        first_out = jnp.einsum('tbi,bio->tbo', shaped, left_blocks).astype(jnp.bfloat16)
        moved_in = jnp.transpose(first_out, (0, 2, 1)).reshape(tok_count, BLOCKS, BLK).astype(jnp.float32)
        second_out = jnp.einsum('tjc,jck->tjk', moved_in, right_blocks)
        activated, pullback = jax.vjp(gelu_exact, second_out)
        mixed_rows = (row_block.astype(jnp.float32) + activated.reshape(tok_count, D)).astype(jnp.bfloat16)
        upstream_rows = cotangent.astype(jnp.float32)
        grad_out = pullback(upstream_rows.reshape(tok_count, BLOCKS, BLK))[0].astype(jnp.bfloat16)
        grad_out = lax.optimization_barrier(grad_out).astype(jnp.float32)
        grad_right = grad_right + jnp.einsum('tjc,tjk->jck', moved_in, grad_out)
        grad_moved = jnp.einsum('tjk,jck->tjc', grad_out, right_blocks).astype(jnp.bfloat16)
        grad_moved = lax.optimization_barrier(grad_moved)
        grad_inner = jnp.transpose(grad_moved.reshape(tok_count, BLK, BLOCKS), (0, 2, 1)).astype(jnp.float32)
        grad_left = grad_left + jnp.einsum('tbi,tbo->bio', shaped, grad_inner)
        back_proj = jnp.einsum('tbo,bio->tbi', grad_inner, left_blocks).reshape(tok_count, D)
        grad_rows = (upstream_rows + back_proj).astype(jnp.bfloat16)
        return ((grad_left, grad_right), (mixed_rows, grad_rows))
    blocked = tokens.reshape(TOKENS // TOK_DEV, TOK_DEV, D)
    blocked_up = upstream.reshape(TOKENS // TOK_DEV, TOK_DEV, D)
    zeros_left = jnp.zeros((BLOCKS, BLK, BLK), jnp.float32)
    zeros_right = jnp.zeros((BLOCKS, BLK, BLK), jnp.float32)
    carried, outputs = lax.scan(block_step, (zeros_left, zeros_right), (blocked, blocked_up))
    scale = 1.0 / math.sqrt(TOKENS)
    mixed = outputs[0].reshape(TOKENS, D)
    grad_tokens = outputs[1].reshape(TOKENS, D)
    return (mixed, grad_tokens, carried[0] * scale, carried[1] * scale)
```

```python
import functools
import math

import jax
import jax.numpy as jnp
from jax import lax
from jax.experimental import pallas as pl
from jax.experimental.pallas import tpu as pltpu
from jax.sharding import PartitionSpec as P

BF16 = jnp.bfloat16
F32 = jnp.float32
ROOT_HALF = math.sqrt(0.5)
DENSITY = 1.0 / math.sqrt(2.0 * math.pi)
VMEM = 48 * 1024 * 1024


def split_even(count, parts):
    parts = min(count, parts)
    edges = [count * step // parts for step in range(parts + 1)]
    return list(zip(edges[:-1], edges[1:]))


def dot(left, right, left_dim, right_dim):
    return lax.dot_general(
        left, right, (((left_dim,), (right_dim,)), ((), ())), preferred_element_type=F32
    )


def params(dims=1):
    return pltpu.CompilerParams(
        dimension_semantics=("arbitrary",) * dims, vmem_limit_bytes=VMEM
    )


def expand_kernel(dims, me_ref, x_ref, w_ref, own_ref, *rest):
    group, spans, inner, blk = dims
    sends, full = rest[:-1], rest[-1]
    me = me_ref[0]
    width = blk // group
    for half in range(2):
        weight = w_ref[:, half].reshape(blk, blk)
        acts = x_ref[:, half * blk : (half + 1) * blk]
        full[half] = dot(weight.T, acts, 1, 1)
    for shift in range(group):
        peer = lax.rem(me + shift, group)
        rows = pl.ds(pl.multiple_of(peer * width, width), width)
        parts = [full[half, rows, :].reshape(width // inner, inner, -1) for half in range(2)]
        piece = jnp.concatenate(parts, axis=1).astype(BF16)
        if shift == 0:
            own_ref[...] = piece
        else:
            for at, (start, stop) in enumerate(spans):
                sends[(shift - 1) * len(spans) + at][...] = piece[start:stop]


def expand(me, tokens, weights, group, spans):
    shards, local, rows, blk = weights.shape
    tok = tokens.shape[0]
    inner = blk // (local * group)
    lane = lambda pair, _: (0, pair, 0)
    shapes = [local] + [stop - start for start, stop in spans] * (group - 1)
    return pl.pallas_call(
        functools.partial(expand_kernel, (group, spans, inner, blk)),
        grid_spec=pltpu.PrefetchScalarGridSpec(
            num_scalar_prefetch=1,
            grid=(local // 2,),
            in_specs=[
                pl.BlockSpec((tok, 2 * blk), lambda pair, _: (0, pair)),
                pl.BlockSpec((shards, 2, rows, blk), lambda pair, _: (0, pair, 0, 0)),
            ],
            out_specs=[pl.BlockSpec((count, 2 * inner, tok), lane) for count in shapes],
            scratch_shapes=[pltpu.VMEM((2, blk, tok), F32)],
        ),
        out_shape=[jax.ShapeDtypeStruct((count, local * inner, tok), BF16) for count in shapes],
        compiler_params=params(),
        cost_estimate=pl.CostEstimate(
            flops=2 * tok * local * blk * blk, bytes_accessed=4 * tok * local * blk, transcendentals=0
        ),
        name="expand",
    )(me, tokens, weights)


def order_matrix(blk, blocks, flip):
    inner = blk // blocks
    out = lax.broadcasted_iota(jnp.int32, (blk, blk), 1 if flip else 0)
    held = lax.broadcasted_iota(jnp.int32, (blk, blk), 0 if flip else 1)
    return (held == lax.rem(out, blocks) * inner + lax.div(out, blocks)).astype(F32).astype(BF16)


def mix_kernel(dims, me_ref, own_ref, *rest):
    group, blk, blocks, groups, held_count = dims
    arrived, rest = rest[: group - 1], rest[group - 1 :]
    w_ref, x_ref, up_ref = rest[:3]
    rest = rest[3 + held_count :]
    mixed_ref, grad_ref, back_own_ref = rest[:3]
    backs, (moved, back) = rest[3:-2], rest[-2:]
    me = me_ref[0]
    rows = blk // group
    span = lambda source: pl.ds(pl.multiple_of(source * rows, rows), rows)
    moved[span(me), :] = own_ref[0]
    for shift in range(1, group):
        moved[span(lax.rem(me - shift + group, group)), :] = arrived[shift - 1][0]
    ordered = dot(order_matrix(blk, blocks, False), moved[...], 1, 0).astype(BF16)
    weight = w_ref[:, 0].reshape(blk, blk)
    inner_out = dot(ordered.T, weight, 1, 0)
    cdf = 0.5 + 0.5 * lax.erf(inner_out * ROOT_HALF)
    mixed_ref[...] = (x_ref[...].astype(F32) + inner_out * cdf).astype(BF16)
    slope = cdf + inner_out * (DENSITY * jnp.exp(-0.5 * inner_out * inner_out))
    grad_out = (up_ref[...].astype(F32) * slope).astype(BF16)
    grad_ref[:, 0] = dot(ordered, grad_out, 1, 0).reshape(grad_ref.shape[0], -1, blk).astype(grad_ref.dtype)
    returned = dot(weight, grad_out, 1, 1).astype(BF16)
    back[...] = dot(order_matrix(blk, blocks, True), returned, 1, 0).astype(BF16)
    back_own_ref[0] = back[span(me), :]
    per = rows // sum(groups)
    for shift in range(1, group):
        piece = back[span(lax.rem(me + shift, group)), :]
        start = 0
        for at, count in enumerate(groups):
            backs[(shift - 1) * len(groups) + at][0] = piece[start * per : (start + count) * per]
            start += count


def mix(me, own, arrived, weights, tokens, upstream, held, span, group, groups, term_dtype):
    shards, local, rows, blk = weights.shape
    tok = tokens.shape[0]
    blocks = local * group
    first, last = span
    count = last - first
    feat = blk // group
    per = feat // local
    at = lambda j, _: (first + j, 0, 0)
    lane = lambda j, _: (0, first + j)
    back_shapes = [(local, n * per, tok) for n in groups] * (group - 1)
    out_shape = [
        jax.ShapeDtypeStruct(tokens.shape, BF16),
        jax.ShapeDtypeStruct((shards, count, rows, blk), term_dtype),
        jax.ShapeDtypeStruct((local, feat, tok), BF16),
    ] + [jax.ShapeDtypeStruct(shape, BF16) for shape in back_shapes]
    out_specs = [
        pl.BlockSpec((tok, blk), lane),
        pl.BlockSpec((shards, 1, rows, blk), lambda j, _: (0, j, 0, 0)),
        pl.BlockSpec((1, feat, tok), at),
    ] + [pl.BlockSpec((1,) + shape[1:], at) for shape in back_shapes]
    held_at = 1 + 1 + (group - 1) + 3
    kept = [0] + list(range(2, len(out_shape)))
    aliases = {held_at + k: kept[k] for k in range(len(held))}
    return pl.pallas_call(
        functools.partial(mix_kernel, (group, blk, blocks, groups, len(held))),
        grid_spec=pltpu.PrefetchScalarGridSpec(
            num_scalar_prefetch=1,
            grid=(count,),
            in_specs=[pl.BlockSpec((1, feat, tok), at)]
            + [pl.BlockSpec((1, feat, tok), lambda j, _: (j, 0, 0))] * (group - 1)
            + [
                pl.BlockSpec((shards, 1, rows, blk), lambda j, _: (0, first + j, 0, 0)),
                pl.BlockSpec((tok, blk), lane),
                pl.BlockSpec((tok, blk), lane),
            ]
            + [pl.BlockSpec(memory_space=pl.ANY)] * len(held),
            out_specs=out_specs,
            scratch_shapes=[pltpu.VMEM((blk, tok), BF16), pltpu.VMEM((blk, tok), BF16)],
        ),
        out_shape=out_shape,
        input_output_aliases=aliases,
        compiler_params=params(),
        cost_estimate=pl.CostEstimate(
            flops=10 * tok * count * blk * blk,
            bytes_accessed=12 * tok * count * blk,
            transcendentals=2 * tok * count * blk,
        ),
        name="mix",
    )(me, own, *arrived, weights, tokens, upstream, *held)


def fold_kernel(dims, me_ref, own_ref, *rest):
    group, inner, blk, held_count = dims
    arrived, rest = rest[: group - 1], rest[group - 1 :]
    x_ref, up_ref, w_ref = rest[:3]
    out_ref, grad_ref, inner_grad = rest[3 + held_count :]
    me = me_ref[0]
    width = blk // group
    for shift in range(group):
        ref = own_ref if shift == 0 else arrived[shift - 1]
        source = lax.rem(me - shift + group, group)
        piece = ref[...].astype(F32)
        for half in range(2):
            part = piece[:, half * inner : (half + 1) * inner].reshape(width, -1)
            inner_grad[half, pl.ds(pl.multiple_of(source * width, width), width), :] = part.astype(BF16)
    for half in range(2):
        cols = slice(half * blk, (half + 1) * blk)
        weight = w_ref[:, half].reshape(blk, blk)
        du = inner_grad[half].T
        term = dot(x_ref[:, cols].T, du, 1, 0)
        grad_ref[:, half] = term.reshape(grad_ref.shape[0], -1, blk).astype(grad_ref.dtype)
        out_ref[:, cols] = (up_ref[:, cols].astype(F32) + dot(du, weight, 1, 1)).astype(BF16)


def fold(me, own, arrived, tokens, upstream, weights, held, span, group, term_dtype):
    shards, local, rows, blk = weights.shape
    tok = tokens.shape[0]
    inner = blk // (local * group)
    first, last = span
    count = last - first
    lane = lambda pair, _: (0, first // 2 + pair)
    return pl.pallas_call(
        functools.partial(fold_kernel, (group, inner, blk, len(held))),
        grid_spec=pltpu.PrefetchScalarGridSpec(
            num_scalar_prefetch=1,
            grid=(count // 2,),
            in_specs=[pl.BlockSpec((local, 2 * inner, tok), lambda pair, _: (0, first // 2 + pair, 0))]
            + [pl.BlockSpec((local, 2 * inner, tok), lambda pair, _: (0, pair, 0))] * (group - 1)
            + [
                pl.BlockSpec((tok, 2 * blk), lane),
                pl.BlockSpec((tok, 2 * blk), lane),
                pl.BlockSpec((shards, 2, rows, blk), lambda pair, _: (0, first // 2 + pair, 0, 0)),
            ]
            + [pl.BlockSpec(memory_space=pl.ANY)] * len(held),
            out_specs=[
                pl.BlockSpec((tok, 2 * blk), lane),
                pl.BlockSpec((shards, 2, rows, blk), lambda pair, _: (0, pair, 0, 0)),
            ],
            scratch_shapes=[pltpu.VMEM((2, blk, tok), BF16)],
        ),
        out_shape=[
            jax.ShapeDtypeStruct(tokens.shape, BF16),
            jax.ShapeDtypeStruct((shards, count, rows, blk), term_dtype),
        ],
        input_output_aliases={1 + 1 + (group - 1) + 3: 0} if held else {},
        compiler_params=params(),
        cost_estimate=pl.CostEstimate(
            flops=4 * tok * count * blk * blk, bytes_accessed=10 * tok * count * blk, transcendentals=0
        ),
        name="fold",
    )(me, own, *arrived, tokens, upstream, weights, *held)


def exchange(pieces, group):
    if group == 1:
        return []
    return [
        lax.ppermute(piece, "mp", [(at, (at + shift) % group) for at in range(group)])
        for shift, piece in enumerate(pieces, 1)
    ]


def gather_rows(shard):
    local, rows, blk = shard.shape
    whole = lax.all_gather(shard, "dp", axis=0, tiled=False)
    if rows % 16:
        shards = whole.shape[0]
        whole = jnp.transpose(whole, (1, 0, 2, 3)).reshape(1, local, shards * rows, blk)
    return whole


def scatter_rows(term, rows):
    if term.shape[2] != rows:
        _, local, whole, blk = term.shape
        term = jnp.transpose(term.reshape(local, whole // rows, rows, blk), (1, 0, 2, 3))
    return lax.psum_scatter(term, "dp", scatter_dimension=0, tiled=False).astype(F32)


def on_device(tokens, upstream, first_factor, second_factor):
    local, rows, blk = first_factor.shape
    group = lax.axis_size("mp")
    scale = 1.0 / math.sqrt(tokens.shape[0] * lax.axis_size("dp"))
    me = lax.axis_index("mp").astype(jnp.int32).reshape(1)
    j_spans = split_even(local, 4)
    b_spans = [(2 * start, 2 * stop) for start, stop in split_even(local // 2, 4)]
    groups = tuple(stop - start for start, stop in b_spans)
    first_whole = gather_rows(first_factor)
    second_whole = gather_rows(second_factor)
    own, *sends = expand(me, tokens, first_whole, group, j_spans)
    arrived = [exchange(sends[at :: len(j_spans)], group) for at in range(len(j_spans))]
    held, second_terms = [], []
    for at, span in enumerate(j_spans):
        mixed, term, *backs = mix(
            me, own, arrived[at], second_whole, tokens, upstream, held, span, group, groups, F32
        )
        second_terms.append(scatter_rows(term, rows))
        held = [mixed] + backs
    back_own, backs = backs[0], backs[1:]
    returned = [exchange(backs[at :: len(groups)], group) for at in range(len(groups))]
    held, first_terms = [], []
    for at, span in enumerate(b_spans):
        grad_tokens, term = fold(
            me, back_own, returned[at], tokens, upstream, first_whole, held, span, group, F32
        )
        first_terms.append(scatter_rows(term, rows))
        held = [grad_tokens]
    grad_first = jnp.concatenate(first_terms, axis=0) * scale
    grad_second = jnp.concatenate(second_terms, axis=0) * scale
    return mixed, grad_tokens, grad_first, grad_second


def solution(mesh):
    placed = (P("dp", "mp"), P("dp", "mp"), P("mp", "dp", None), P("mp", "dp", None))
    return jax.shard_map(
        on_device, mesh=mesh, in_specs=placed, out_specs=placed, check_vma=False
    )
```

```python
import functools
import math

import jax
import jax.numpy as jnp
from jax import lax
from jax.experimental import pallas as pl
from jax.experimental.pallas import tpu as pltpu
from jax.sharding import PartitionSpec as P

BF16 = jnp.bfloat16
F32 = jnp.float32
ROOT_HALF = math.sqrt(0.5)
DENSITY = 1.0 / math.sqrt(2.0 * math.pi)
VMEM = 60 * 1024 * 1024


def split_even(count, parts):
    parts = min(count, parts)
    edges = [count * step // parts for step in range(parts + 1)]
    return list(zip(edges[:-1], edges[1:]))


def split_by(count, weights):
    total, edges, run = sum(weights), [0], 0
    for weight in weights:
        run += weight
        edges.append(count * run // total)
    return [(lo, hi) for lo, hi in zip(edges[:-1], edges[1:]) if hi > lo]


def dot(left, right, left_dim, right_dim):
    return lax.dot_general(
        left, right, (((left_dim,), (right_dim,)), ((), ())), preferred_element_type=F32
    )


def aligned(index, size):
    return pl.ds(pl.multiple_of(index * size, size), size)


def call(kernel, name, ids, grid, inputs, held, outputs, scratch=(), cost=1):
    places = sorted(held)
    return pl.pallas_call(
        kernel,
        grid_spec=pltpu.PrefetchScalarGridSpec(
            num_scalar_prefetch=1,
            grid=grid,
            in_specs=[spec for _, spec in inputs]
            + [pl.BlockSpec(memory_space=pl.ANY)] * len(places),
            out_specs=[spec for _, _, spec in outputs],
            scratch_shapes=list(scratch),
        ),
        out_shape=[jax.ShapeDtypeStruct(shape, dtype) for shape, dtype, _ in outputs],
        input_output_aliases={1 + len(inputs) + at: place for at, place in enumerate(places)},
        compiler_params=pltpu.CompilerParams(
            dimension_semantics=("arbitrary",) * len(grid), vmem_limit_bytes=VMEM
        ),
        cost_estimate=pl.CostEstimate(flops=cost, bytes_accessed=cost, transcendentals=0),
        name=name,
    )(ids, *[array for array, _ in inputs], *[held[place] for place in places])


class Whole:
    def __init__(self, arrays, slots, relative):
        self.arrays, self.slots, self.relative = arrays, slots, relative

    def specs(self, count, at):
        return [
            (array, pl.BlockSpec((array.shape[0], count) + array.shape[2:], lambda step, _: (0, at(step), 0, 0)))
            for array in self.arrays
        ]

    def load(self, refs, block, target, device):
        for ref, slots in zip(refs, self.slots):
            rows = ref.shape[2]
            for place, slot in enumerate(slots):
                owner = lax.bitwise_xor(device, slot) if self.relative else slot
                target[aligned(owner, rows) if self.relative else pl.ds(owner * rows, rows), :] = ref[place, block]


def combos(bits):
    found = [0]
    for bit in bits:
        found += [value | bit for value in found]
    return found


class Network:
    def __init__(self, size):
        bits = [1 << k for k in range(size.bit_length() - 1)]
        self.size = size
        self.rounds = [tuple(bits[:1]), tuple(bits[1:2]), tuple(bits[2:])]
        self.rounds = [bits for bits in self.rounds if bits]

    def swap(self, array, mask):
        return lax.ppermute(array, "dp", [(at, at ^ mask) for at in range(self.size)])

    def gather(self, shard):
        have = [(shard[None], [0])]
        for bits in reversed(self.rounds):
            if len(bits) > 1 and len(have) == 1:
                got = []
                for mask in combos(bits)[1:]:
                    got.append((self.swap(have[0][0], mask), [mask]))
                have = [
                    (
                        jnp.concatenate([have[0][0]] + [array for array, _ in got], axis=0),
                        sum([slots for _, slots in have + got], []),
                    )
                ]
            else:
                for mask in combos(bits)[1:]:
                    have = have + [
                        (self.swap(array, mask), [slot | mask for slot in slots]) for array, slots in have
                    ]
        return Whole([array for array, _ in have], [slots for _, slots in have], True)

    def cut(self, slots, step):
        bits = self.rounds[step]
        mask = sum(bits)
        return [[slot for slot in slots if slot & mask == value] for value in combos(bits)]

    def first_cut(self):
        return self.cut(list(range(self.size)), 0)

    def scatter(self, parts, ids, scale, held, shape, first):
        slots = self.first_cut()[0]
        for step, bits in enumerate(self.rounds):
            keep, sends = parts[0], parts[1:]
            got = [self.swap(send, mask) for send, mask in zip(sends, combos(bits)[1:])]
            last = step == len(self.rounds) - 1
            lists = None if last else self.cut(slots, step + 1)
            count = keep.shape[1]
            block = math.gcd(count, first) if last else count
            if block > 4 and not last:
                block = count // 2
            specs = [
                (
                    array,
                    pl.BlockSpec((array.shape[0], block) + array.shape[2:], lambda at, _: (0, at, 0, 0)),
                )
                for array in [keep] + got
            ]
            if last:
                outs = [
                    (
                        shape,
                        F32,
                        pl.BlockSpec((block,) + shape[1:], lambda at, _: (first // block + at, 0, 0)),
                    )
                ]
            else:
                outs = [
                    (
                        (len(members),) + keep.shape[1:],
                        F32 if place == 0 else BF16,
                        pl.BlockSpec((len(members), block) + keep.shape[2:], lambda at, _: (0, at, 0, 0)),
                    )
                    for place, members in enumerate(lists)
                ]
            kernel = functools.partial(
                join_kernel, len(got), slots, lists, scale, 1 if last and held is not None else 0
            )
            parts = call(
                kernel,
                "join",
                ids,
                (count // block,),
                specs,
                {0: held} if last and held is not None else {},
                outs,
            )
            if not last:
                slots = lists[0]
        return parts[0]


def join_kernel(arrivals, slots, lists, scale, held_count, ids, keep, *rest):
    got, outs = rest[:arrivals], rest[arrivals + held_count :]
    for place, slot in enumerate(slots):
        total = keep[place]
        for ref in got:
            total = total + ref[place].astype(F32)
        if lists is None:
            outs[0][...] = total * scale
        else:
            for out, members in zip(outs, lists):
                if slot in members:
                    out[members.index(slot)] = total.astype(out.dtype)


def expand_kernel(weights, shifts, spans, group, inner, ids, x_ref, *rest):
    w_refs, rest = rest[: len(weights.arrays)], rest[len(weights.arrays) :]
    outs, held = rest[:-1], rest[-1]
    blk = held.shape[1]
    halves = []
    for half in range(2):
        weights.load(w_refs, half, held.at[half], ids[1])
        acts = x_ref[:, half * blk : (half + 1) * blk]
        halves.append(dot(held[half].T, acts, 1, 1))
    width = blk // group
    for at, _ in enumerate(shifts):
        parts = [
            full[at * width : (at + 1) * width].reshape(width // inner, inner, -1) for full in halves
        ]
        piece = jnp.concatenate(parts, axis=1).astype(BF16)
        for place, (start, stop) in enumerate(spans):
            outs[at * len(spans) + place][...] = piece[start:stop]


def expand(ids, tokens, weights, shifts, spans, group, local):
    tok = tokens.shape[0]
    blk = tokens.shape[1] // local
    inner = blk // (local * group)
    cols = len(shifts) * (blk // group)
    shapes = [stop - start for _ in shifts for start, stop in spans]
    return call(
        functools.partial(expand_kernel, weights, shifts, spans, group, inner),
        "expand",
        ids,
        (local // 2,),
        [(tokens, pl.BlockSpec((tok, 2 * blk), lambda pair, _: (0, pair)))]
        + weights.specs(2, lambda pair: pair),
        {},
        [
            (
                (count, local * inner, tok),
                BF16,
                pl.BlockSpec((count, 2 * inner, tok), lambda pair, _: (0, pair, 0)),
            )
            for count in shapes
        ],
        [pltpu.VMEM((2, blk, cols), BF16)],
    )


def order_matrix(blk, blocks, flip):
    inner = blk // blocks
    out = lax.broadcasted_iota(jnp.int32, (blk, blk), 1 if flip else 0)
    held = lax.broadcasted_iota(jnp.int32, (blk, blk), 0 if flip else 1)
    return (held == lax.rem(out, blocks) * inner + lax.div(out, blocks)).astype(F32).astype(BF16)


def store_term(term, slots_lists, relative, outs, scratch, device, block):
    scratch[...] = term
    for out, slots in zip(outs, slots_lists):
        rows = out.shape[2]
        for place, slot in enumerate(slots):
            owner = lax.bitwise_xor(device, slot) if relative else slot
            out[place, block] = scratch[aligned(owner, rows), :].astype(out.dtype)


def mix_kernel(weights, cut, relative, group, blocks, backs, held_count, ids, own_ref, *rest):
    arrived, rest = rest[: group - 1], rest[group - 1 :]
    w_refs, rest = rest[: len(weights.arrays)], rest[len(weights.arrays) :]
    x_ref, up_ref = rest[:2]
    rest = rest[2 + held_count :]
    mixed_ref, back_own_ref = rest[:2]
    term_refs, rest = rest[2 : 2 + len(cut)], rest[2 + len(cut) :]
    back_refs, (moved, back, held, term) = rest[:-4], rest[-4:]
    me = ids[0]
    blk = held.shape[0]
    rows = blk // group
    moved[aligned(me, rows), :] = own_ref[0]
    for shift in range(1, group):
        moved[aligned(lax.rem(me - shift + group, group), rows), :] = arrived[shift - 1][0]
    weights.load(w_refs, 0, held, ids[1])
    weight = held[...]
    ordered = dot(order_matrix(blk, blocks, False), moved[...], 1, 0).astype(BF16)
    inner_out = dot(ordered.T, weight, 1, 0)
    cdf = 0.5 + 0.5 * lax.erf(inner_out * ROOT_HALF)
    mixed_ref[...] = (x_ref[...].astype(F32) + inner_out * cdf).astype(BF16)
    slope = cdf + inner_out * (DENSITY * jnp.exp(-0.5 * inner_out * inner_out))
    grad_out = (up_ref[...].astype(F32) * slope).astype(BF16)
    store_term(dot(ordered, grad_out, 1, 0), cut, relative, term_refs, term, ids[1], 0)
    returned = dot(weight, grad_out, 1, 1).astype(BF16)
    back[...] = dot(order_matrix(blk, blocks, True), returned, 1, 0).astype(BF16)
    back_own_ref[0] = back[aligned(me, rows), :]
    for shift in range(1, group):
        piece = back[aligned(lax.rem(me + shift, group), rows), :]
        for at, (start, stop) in enumerate(backs):
            back_refs[(shift - 1) * len(backs) + at][0] = piece[start:stop]


def mix(ids, own, arrived, weights, tokens, upstream, held, span, group, local, cut, relative, term, backs):
    tok = tokens.shape[0]
    blk = tokens.shape[1] // local
    feat = blk // group
    per = feat // local
    first, last = span
    rows = blk // sum(len(slots) for slots in cut)
    lane = pl.BlockSpec((tok, blk), lambda j, _: (0, first + j))
    at = pl.BlockSpec((1, feat, tok), lambda j, _: (first + j, 0, 0))
    keys = ["mixed", "own"]
    outs = [(tokens.shape, BF16, lane), ((local, feat, tok), BF16, at)]
    term_key, (term_first, term_last) = term
    for place, slots in enumerate(cut):
        keys.append((term_key, place))
        outs.append(
            (
                (len(slots), term_last - term_first, rows, blk),
                F32 if place == 0 else BF16,
                pl.BlockSpec((len(slots), 1, rows, blk), lambda j, _: (0, first - term_first + j, 0, 0)),
            )
        )
    for shift in range(1, group):
        for key, (b_first, b_last), (j_first, j_last) in backs:
            keys.append((key, shift))
            outs.append(
                (
                    (j_last - j_first, (b_last - b_first) * per, tok),
                    BF16,
                    pl.BlockSpec(
                        (1, (b_last - b_first) * per, tok),
                        functools.partial(lambda start, j, _: (start + j, 0, 0), first - j_first),
                    ),
                )
            )
    kept = {place: held[key] for place, key in enumerate(keys) if key in held}
    cuts = [(b_first * per, b_last * per) for _, (b_first, b_last), _ in backs]
    got = call(
        functools.partial(mix_kernel, weights, cut, relative, group, local * group, cuts, len(kept)),
        "mix",
        ids,
        (last - first,),
        [(own, at)]
        + [(array, pl.BlockSpec((1, feat, tok), lambda j, _: (j, 0, 0))) for array in arrived]
        + weights.specs(1, lambda j: first + j)
        + [(tokens, lane), (upstream, lane)],
        kept,
        outs,
        [
            pltpu.VMEM((blk, tok), BF16),
            pltpu.VMEM((blk, tok), BF16),
            pltpu.VMEM((blk, blk), BF16),
            pltpu.VMEM((blk, blk), F32),
        ],
    )
    held.update(zip(keys, got))


def fold_kernel(columns, cut, relative, group, inner, pieces, held_count, ids, own_ref, *rest):
    arrived, rest = rest[: pieces * (group - 1)], rest[pieces * (group - 1) :]
    x_ref, up_ref = rest[:2]
    rest = rest[2:]
    w_refs = []
    for weights in columns:
        w_refs.append(rest[: len(weights.arrays)])
        rest = rest[len(weights.arrays) :]
    rest = rest[held_count:]
    out_ref, term_refs = rest[0], rest[1:-4]
    inner_grad, held, sorted_term, term = rest[-4:]
    me = ids[0]
    blk = held.shape[1]
    width = blk // group
    for shift in range(group):
        if shift == 0:
            piece = own_ref[...]
        else:
            refs = arrived[(shift - 1) * pieces : shift * pieces]
            piece = jnp.concatenate([ref[...] for ref in refs], axis=0)
        piece = piece.astype(F32)
        for half in range(2):
            part = piece[:, half * inner : (half + 1) * inner].reshape(width, -1)
            inner_grad[half, shift * width : (shift + 1) * width, :] = part.astype(BF16)
    for half in range(2):
        cols = slice(half * blk, (half + 1) * blk)
        start = 0
        for weights, refs in zip(columns, w_refs):
            size = refs[0].shape[3]
            weights.load(refs, half, held.at[:, start : start + size], ids[1])
            start += size
        du = inner_grad[half]
        unsorted = dot(du, x_ref[:, cols], 1, 0)
        for shift in range(group):
            source = lax.rem(me - shift + group, group)
            sorted_term[aligned(source, width), :] = unsorted[shift * width : (shift + 1) * width]
        store_term(sorted_term[...].T, cut, relative, term_refs, term, ids[1], half)
        back = dot(du.T, held[...], 1, 1)
        out_ref[:, cols] = (up_ref[:, cols].astype(F32) + back).astype(BF16)


def fold(ids, own, arrived, pieces, tokens, upstream, columns, grad_tokens, span, group, local, cut, relative):
    tok = tokens.shape[0]
    blk = tokens.shape[1] // local
    inner = blk // (local * group)
    first, last = span
    rows = blk // sum(len(slots) for slots in cut)
    start = first // 2
    lane = pl.BlockSpec((tok, 2 * blk), lambda pair, _: (0, start + pair))
    inputs = [(own, pl.BlockSpec((local, 2 * inner, tok), lambda pair, _: (0, start + pair, 0)))]
    inputs += [
        (array, pl.BlockSpec((array.shape[0], 2 * inner, tok), lambda pair, _: (0, pair, 0)))
        for array in arrived
    ]
    inputs += [(tokens, lane), (upstream, lane)]
    for weights in columns:
        inputs += weights.specs(2, lambda pair: start + pair)
    outs = [(tokens.shape, BF16, lane)] + [
        (
            (len(slots), last - first, rows, blk),
            F32 if place == 0 else BF16,
            pl.BlockSpec((len(slots), 2, rows, blk), lambda pair, _: (0, pair, 0, 0)),
        )
        for place, slots in enumerate(cut)
    ]
    held = {} if grad_tokens is None else {0: grad_tokens}
    return call(
        functools.partial(fold_kernel, columns, cut, relative, group, inner, pieces, len(held)),
        "fold",
        ids,
        ((last - first) // 2,),
        inputs,
        held,
        outs,
        [
            pltpu.VMEM((2, blk, tok), BF16),
            pltpu.VMEM((blk, blk), BF16),
            pltpu.VMEM((blk, blk), F32),
            pltpu.VMEM((blk, blk), F32),
        ],
    )


def send(array, shift, group):
    return lax.ppermute(array, "mp", [(at, (at + shift) % group) for at in range(group)])


def gather_plain(shard):
    local, rows, blk = shard.shape
    whole = lax.all_gather(shard, "dp", axis=0, tiled=False)
    if rows % 16:
        whole = jnp.transpose(whole, (1, 0, 2, 3)).reshape(1, local, whole.shape[0] * rows, blk)
    return Whole([whole], [list(range(whole.shape[0]))], False)


def scatter_plain(term, rows, scale):
    _, local, whole, blk = term.shape
    term = jnp.transpose(term.reshape(local, whole // rows, rows, blk), (1, 0, 2, 3))
    return lax.psum_scatter(term, "dp", scatter_dimension=0, tiled=False) * scale


def on_device(tokens, upstream, first_factor, second_factor):
    local, rows, blk = first_factor.shape
    group, size = lax.axis_size("mp"), lax.axis_size("dp")
    width = blk // group
    scale = 1.0 / math.sqrt(tokens.shape[0] * size)
    me, device = lax.axis_index("mp"), lax.axis_index("dp")
    ids = jnp.stack([me, device]).astype(jnp.int32)
    cube = group == 2 and size >= 8 and size & (size - 1) == 0 and rows % 16 == 0 and width % 128 == 0
    net = Network(size) if cube else None
    cut = net.first_cut() if cube else [[0]]
    j_spans = split_even(local, 4)
    term_spans = split_even(local, 2)
    b_spans = [(2 * lo, 2 * hi) for lo, hi in split_by(local // 2, (4, 3, 1))]

    second_whole = gather_plain(second_factor)
    if cube:
        near, far = [
            net.gather(lax.dynamic_slice_in_dim(first_factor, lax.rem(me + shift, group) * width, width, 2))
            for shift in range(2)
        ]
        columns = [near, far]
    else:
        whole = gather_plain(first_factor).arrays[0]
        if whole.shape[0] > 1:
            whole = jnp.transpose(whole, (1, 0, 2, 3)).reshape(1, local, blk, blk)
        turned = jnp.roll(whole, -me * width, axis=3)
        near, far, turned = [
            Whole([array], [[0]], False) for array in (turned[..., :width], turned[..., width:], turned)
        ]
        columns = [turned]
    shifts = list(range(1, group))
    sends = expand(ids, tokens, far, shifts, j_spans, group, local)
    arrived = [
        [send(sends[(shift - 1) * len(j_spans) + at], shift, group) for shift in shifts]
        for at in range(len(j_spans))
    ]
    own = expand(ids, tokens, near, [0], [(0, local)], group, local)[0]

    held, returned, grad_second = {}, {}, None
    for at, span in enumerate(j_spans):
        backs = []
        for place, b_span in enumerate(b_spans):
            for j_span in term_spans if place == 0 else [(0, local)]:
                if j_span[0] <= span[0] and span[1] <= j_span[1]:
                    backs.append((("back", place, j_span), b_span, j_span))
        term_span = [known for known in term_spans if known[0] <= span[0] and span[1] <= known[1]][0]
        mix(
            ids, own, arrived[at], second_whole, tokens, upstream, held, span, group, local, cut, cube,
            (("term", term_span), term_span), backs,
        )
        for key, _, j_span in backs:
            if j_span[1] == span[1]:
                for shift in shifts:
                    returned[(key, shift)] = send(held[(key, shift)], shift, group)
        if cube and term_span[1] == span[1]:
            parts = [held[(("term", term_span), place)] for place in range(len(cut))]
            grad_second = net.scatter(parts, ids, scale, grad_second, first_factor.shape, term_span[0])
    if not cube:
        terms = [held[(("term", span), 0)] for span in term_spans]
        grad_second = scatter_plain(jnp.concatenate(terms, axis=1), rows, scale)

    grad_tokens, grad_first, terms = None, None, []
    for place, b_span in enumerate(b_spans):
        j_parts = term_spans if place == 0 else [(0, local)]
        pieces = [returned[(("back", place, j_span), shift)] for shift in shifts for j_span in j_parts]
        grad_tokens, *parts = fold(
            ids, held["own"], pieces, len(j_parts), tokens, upstream, columns, grad_tokens, b_span, group,
            local, cut, cube,
        )
        if cube:
            grad_first = net.scatter(parts, ids, scale, grad_first, first_factor.shape, b_span[0])
        else:
            terms.append(parts[0])
    if not cube:
        grad_first = scatter_plain(jnp.concatenate(terms, axis=1), rows, scale)
    return held["mixed"], grad_tokens, grad_first, grad_second


def solution(mesh):
    placed = (P("dp", "mp"), P("dp", "mp"), P("mp", "dp", None), P("mp", "dp", None))
    return jax.shard_map(
        on_device, mesh=mesh, in_specs=placed, out_specs=placed, check_vma=False
    )
```

```python
import functools
import math

import jax
import jax.numpy as jnp
from jax import lax
from jax.experimental import pallas as pl
from jax.experimental.pallas import tpu as pltpu
from jax.sharding import PartitionSpec as P

BF16 = jnp.bfloat16
F32 = jnp.float32
ROOT_HALF = math.sqrt(0.5)
DENSITY = 1.0 / math.sqrt(2.0 * math.pi)
TIES = {0: ((0, 1),), 1: ((1, 1),), 2: ((0, 2), (2, 1))}
VMEM = 20 * 1024 * 1024


def split_even(count, parts):
    parts = min(count, parts)
    edges = [count * step // parts for step in range(parts + 1)]
    return list(zip(edges[:-1], edges[1:]))


def split_by(count, weights):
    total, edges, run = sum(weights), [0], 0
    for weight in weights:
        run += weight
        edges.append(count * run // total)
    return [(lo, hi) for lo, hi in zip(edges[:-1], edges[1:]) if hi > lo]


def dot(left, right, left_dim, right_dim):
    return lax.dot_general(
        left, right, (((left_dim,), (right_dim,)), ((), ())), preferred_element_type=F32
    )


def aligned(index, size):
    return pl.ds(pl.multiple_of(index * size, size), size)


def call(kernel, name, ids, grid, inputs, held, outputs, scratch=(), after=()):
    places = sorted(held)
    extra = [held[place] for place in places] + list(after)
    taken = len(inputs)

    def body(ids_ref, *refs):
        kernel(ids_ref, *refs[:taken], *refs[taken + len(extra) :])

    return pl.pallas_call(
        body,
        grid_spec=pltpu.PrefetchScalarGridSpec(
            num_scalar_prefetch=1,
            grid=grid,
            in_specs=[spec for _, spec in inputs] + [pl.BlockSpec(memory_space=pl.ANY)] * len(extra),
            out_specs=[spec for _, _, spec in outputs],
            scratch_shapes=list(scratch),
        ),
        out_shape=[jax.ShapeDtypeStruct(shape, dtype) for shape, dtype, _ in outputs],
        input_output_aliases={1 + taken + at: place for at, place in enumerate(places)},
        compiler_params=pltpu.CompilerParams(
            dimension_semantics=("arbitrary",) * len(grid), vmem_limit_bytes=VMEM
        ),
        cost_estimate=pl.CostEstimate(flops=1, bytes_accessed=1, transcendentals=0),
        name=name,
    )(ids, *[array for array, _ in inputs], *extra)


class Whole:
    def __init__(self, arrays, slots, relative):
        self.arrays, self.slots, self.relative = arrays, slots, relative

    def specs(self, count, at):
        return [
            (array, pl.BlockSpec((array.shape[0], count) + array.shape[2:], lambda step, _: (0, at(step), 0, 0)))
            for array in self.arrays
        ]

    def load(self, refs, block, target, device):
        if not self.relative:
            return refs[0][:, block].reshape(target.shape)
        for ref, slots in zip(refs, self.slots):
            rows = ref.shape[2]
            for place, slot in enumerate(slots):
                target[aligned(lax.bitwise_xor(device, slot), rows), :] = ref[place, block]
        return target[...]


def combos(bits):
    found = [0]
    for bit in bits:
        found += [value | bit for value in found]
    return found


class Network:
    def __init__(self, size):
        bits = [1 << k for k in range(size.bit_length() - 1)]
        self.size = size
        self.rounds = [tuple(bits[:1]), tuple(bits[1:2]), tuple(bits[2:])]
        self.rounds = [bits for bits in self.rounds if bits]
        self.order = [0]
        for bits in reversed(self.rounds):
            self.order = [slot | mask for mask in combos(bits) for slot in self.order]

    def swap(self, array, mask):
        return lax.ppermute(array, "dp", [(at, at ^ mask) for at in range(self.size)])

    def gather(self, shard, until=None):
        have = [(shard[None], [0])]
        for bits in reversed(self.rounds):
            if len(bits) > 1 and len(have) == 1:
                got = []
                for mask in combos(bits)[1:]:
                    got.append((self.swap(have[0][0], mask), [mask]))
                self.first_got = [array for array, _ in got]
                if until is not None:
                    tied, _ = lax.optimization_barrier((self.first_got, until))
                    got = [(array, slots) for array, (_, slots) in zip(tied, got)]
                have = [
                    (
                        jnp.concatenate([have[0][0]] + [array for array, _ in got], axis=0),
                        sum([slots for _, slots in have + got], []),
                    )
                ]
            else:
                for mask in combos(bits)[1:]:
                    have = have + [
                        (self.swap(array, mask), [slot | mask for slot in slots]) for array, slots in have
                    ]
        return Whole([array for array, _ in have], [slots for _, slots in have], True)

    def cut(self, slots, step):
        bits = self.rounds[step]
        mask = sum(bits)
        return [[slot for slot in slots if slot & mask == value] for value in combos(bits)]

    def first_cut(self):
        return self.cut(self.order, 0)

    def scatter(self, parts, scale):
        slots = self.first_cut()[0]
        total, sends, marks = parts[0], parts[1:], []
        for step, bits in enumerate(self.rounds):
            marks.append(sends)
            got = [self.swap(piece, mask) for piece, mask in zip(sends, combos(bits)[1:])]
            for piece in got:
                total = total + piece.astype(F32)
            if step + 1 < len(self.rounds):
                lists = self.cut(slots, step + 1)
                spans = [(slots.index(members[0]), slots.index(members[-1]) + 1) for members in lists]
                sends = [total[lo:hi].astype(BF16) for lo, hi in spans[1:]]
                total = total[spans[0][0] : spans[0][1]]
                slots = lists[0]
        return total[0] * scale, marks


def expand_kernel(weights, shifts, spans, group, inner, ids, x_ref, *rest):
    w_refs, rest = rest[: len(weights.arrays)], rest[len(weights.arrays) :]
    outs, held = rest[:-1], rest[-1]
    blk = held.shape[1]
    halves = []
    for half in range(2):
        weight = weights.load(w_refs, half, held.at[half], ids[1])
        acts = x_ref[:, half * blk : (half + 1) * blk]
        halves.append(dot(acts, weight, 1, 0).astype(BF16).T.astype(F32))
    width = blk // group
    for at, _ in enumerate(shifts):
        parts = [
            full[at * width : (at + 1) * width].reshape(width // inner, inner, -1) for full in halves
        ]
        piece = jnp.concatenate(parts, axis=1).astype(BF16)
        for place, (start, stop) in enumerate(spans):
            outs[at * len(spans) + place][...] = piece[start:stop]


def expand(ids, tokens, weights, shifts, spans, group, local):
    tok = tokens.shape[0]
    blk = tokens.shape[1] // local
    inner = blk // (local * group)
    cols = len(shifts) * (blk // group)
    shapes = [stop - start for _ in shifts for start, stop in spans]
    return call(
        functools.partial(expand_kernel, weights, shifts, spans, group, inner),
        "expand",
        ids,
        (local // 2,),
        [(tokens, pl.BlockSpec((tok, 2 * blk), lambda pair, _: (0, pair)))]
        + weights.specs(2, lambda pair: pair),
        {},
        [
            (
                (count, local * inner, tok),
                BF16,
                pl.BlockSpec((count, 2 * inner, tok), lambda pair, _: (0, pair, 0)),
            )
            for count in shapes
        ],
        [pltpu.VMEM((2, blk, cols), BF16)],
    )


def order_matrix(blk, blocks, flip):
    inner = blk // blocks
    out = lax.broadcasted_iota(jnp.int32, (blk, blk), 1 if flip else 0)
    held = lax.broadcasted_iota(jnp.int32, (blk, blk), 0 if flip else 1)
    return (held == lax.rem(out, blocks) * inner + lax.div(out, blocks)).astype(F32).astype(BF16)


def store_term(term, slots_lists, relative, outs, scratch, device, block):
    if not relative:
        out = outs[0]
        out[:, block] = term.reshape(out.shape[0], out.shape[2], out.shape[3])
        return
    scratch[...] = term
    for out, slots in zip(outs, slots_lists):
        rows = out.shape[2]
        for place, slot in enumerate(slots):
            out[place, block] = scratch[aligned(lax.bitwise_xor(device, slot), rows), :].astype(out.dtype)


def mix_kernel(weights, cut, relative, group, blocks, backs, ids, own_ref, *rest):
    arrived, rest = rest[: group - 1], rest[group - 1 :]
    w_refs, rest = rest[: len(weights.arrays)], rest[len(weights.arrays) :]
    x_ref, up_ref = rest[:2]
    rest = rest[2:]
    mixed_ref, back_own_ref = rest[:2]
    term_refs, rest = rest[2 : 2 + len(cut)], rest[2 + len(cut) :]
    back_refs, (moved, back, held, term) = rest[:-4], rest[-4:]
    me = ids[0]
    blk = held.shape[1]
    rows = blk // group
    there = order_matrix(blk, blocks, False)
    again = order_matrix(blk, blocks, True)
    for j in range(held.shape[0]):
        cols = slice(j * blk, (j + 1) * blk)
        moved[j, aligned(me, rows), :] = own_ref[j]
        for shift in range(1, group):
            moved[j, aligned(lax.rem(me - shift + group, group), rows), :] = arrived[shift - 1][j]
        weight = weights.load(w_refs, j, held.at[j], ids[1])
        ordered = dot(there, moved[j], 1, 0).astype(BF16)
        inner_out = dot(ordered.T, weight, 1, 0)
        cdf = 0.5 + 0.5 * lax.erf(inner_out * ROOT_HALF)
        mixed_ref[:, cols] = (x_ref[:, cols].astype(F32) + inner_out * cdf).astype(BF16)
        slope = cdf + inner_out * (DENSITY * jnp.exp(-0.5 * inner_out * inner_out))
        grad_out = (up_ref[:, cols].astype(F32) * slope).astype(BF16)
        store_term(dot(ordered, grad_out, 1, 0), cut, relative, term_refs, term.at[j], ids[1], j)
        returned = dot(weight, grad_out, 1, 1).astype(BF16)
        back[j] = dot(again, returned, 1, 0).astype(BF16)
        back_own_ref[j] = back[j, aligned(me, rows), :]
        for shift in range(1, group):
            piece = back[j, aligned(lax.rem(me + shift, group), rows), :]
            for at, (start, stop) in enumerate(backs):
                back_refs[(shift - 1) * len(backs) + at][j] = piece[start:stop]


def mix(ids, own, arrived, weights, tokens, upstream, held, span, group, local, cut, relative, term, backs):
    tok = tokens.shape[0]
    blk = tokens.shape[1] // local
    feat = blk // group
    per = feat // local
    first, last = span
    rows = blk // sum(len(slots) for slots in cut)
    step = math.gcd(2, math.gcd(first, last))
    lane = pl.BlockSpec((tok, step * blk), lambda j, _: (0, first // step + j))
    at = pl.BlockSpec((step, feat, tok), lambda j, _: (first // step + j, 0, 0))
    keys = ["mixed", "own"]
    outs = [(tokens.shape, BF16, lane), ((local, feat, tok), BF16, at)]
    term_key, (term_first, term_last) = term
    for place, slots in enumerate(cut):
        keys.append((term_key, place))
        outs.append(
            (
                (len(slots), term_last - term_first, rows, blk),
                F32 if place == 0 else BF16,
                pl.BlockSpec((len(slots), step, rows, blk), lambda j, _: (0, (first - term_first) // step + j, 0, 0)),
            )
        )
    for shift in range(1, group):
        for key, (b_first, b_last), (j_first, j_last) in backs:
            keys.append((key, shift))
            outs.append(
                (
                    (j_last - j_first, (b_last - b_first) * per, tok),
                    BF16,
                    pl.BlockSpec(
                        (step, (b_last - b_first) * per, tok),
                        functools.partial(lambda start, j, _: (start + j, 0, 0), (first - j_first) // step),
                    ),
                )
            )
    kept = {place: held[key] for place, key in enumerate(keys) if key in held}
    cuts = [(b_first * per, b_last * per) for _, (b_first, b_last), _ in backs]
    got = call(
        functools.partial(mix_kernel, weights, cut, relative, group, local * group, cuts),
        "mix",
        ids,
        ((last - first) // step,),
        [(own, at)]
        + [(array, pl.BlockSpec((step, feat, tok), lambda j, _: (j, 0, 0))) for array in arrived]
        + weights.specs(step, lambda j: first // step + j)
        + [(tokens, lane), (upstream, lane)],
        kept,
        outs,
        [
            pltpu.VMEM((step, blk, tok), BF16),
            pltpu.VMEM((step, blk, tok), BF16),
            pltpu.VMEM((step, blk, blk), BF16),
            pltpu.VMEM((step, blk, blk), F32),
        ],
    )
    held.update(zip(keys, got))


def fold_kernel(columns, cut, relative, group, inner, pieces, ids, own_ref, *rest):
    arrived, rest = rest[: pieces * (group - 1)], rest[pieces * (group - 1) :]
    x_ref, up_ref = rest[:2]
    rest = rest[2:]
    w_refs = []
    for weights in columns:
        w_refs.append(rest[: len(weights.arrays)])
        rest = rest[len(weights.arrays) :]
    out_ref, term_refs = rest[0], rest[1:-4]
    inner_grad, held, sorted_term, term = rest[-4:]
    me = ids[0]
    blk = held.shape[2]
    width = blk // group
    for shift in range(group):
        if shift == 0:
            piece = own_ref[...]
        else:
            refs = arrived[(shift - 1) * pieces : shift * pieces]
            piece = jnp.concatenate([ref[...] for ref in refs], axis=0)
        piece = piece.astype(F32)
        for half in range(2):
            part = piece[:, half * inner : (half + 1) * inner].reshape(width, -1)
            inner_grad[half, shift * width : (shift + 1) * width, :] = part.astype(BF16)
    for half in range(2):
        cols = slice(half * blk, (half + 1) * blk)
        if len(columns) == 1:
            weight = columns[0].load(w_refs[0], half, held.at[half], ids[1])
        else:
            start = 0
            for weights, refs in zip(columns, w_refs):
                size = refs[0].shape[3]
                weights.load(refs, half, held.at[half, :, start : start + size], ids[1])
                start += size
            weight = held[half]
        du = inner_grad[half]
        unsorted = dot(du, x_ref[:, cols], 1, 0)
        for shift in range(group):
            source = lax.rem(me - shift + group, group)
            sorted_term[half, aligned(source, width), :] = unsorted[shift * width : (shift + 1) * width]
        store_term(sorted_term[half].T, cut, relative, term_refs, term.at[half], ids[1], half)
        back = dot(du.T, weight, 1, 1)
        out_ref[:, cols] = (up_ref[:, cols].astype(F32) + back).astype(BF16)


def fold(ids, own, arrived, tokens, upstream, columns, grad_tokens, span, group, local, cut, relative, after):
    tok = tokens.shape[0]
    blk = tokens.shape[1] // local
    inner = blk // (local * group)
    first, last = span
    rows = blk // sum(len(slots) for slots in cut)
    start = first // 2
    lane = pl.BlockSpec((tok, 2 * blk), lambda pair, _: (0, start + pair))
    inputs = []
    for array, begin in [(own, 0)] + arrived:
        at = functools.partial(lambda skip, pair, _: (0, skip + pair, 0), start - begin // 2)
        inputs.append((array, pl.BlockSpec((array.shape[0], 2 * inner, tok), at)))
    inputs += [(tokens, lane), (upstream, lane)]
    for weights in columns:
        inputs += weights.specs(2, lambda pair: start + pair)
    outs = [(tokens.shape, BF16, lane)] + [
        (
            (len(slots), last - first, rows, blk),
            F32 if place == 0 else BF16,
            pl.BlockSpec((len(slots), 2, rows, blk), lambda pair, _: (0, pair, 0, 0)),
        )
        for place, slots in enumerate(cut)
    ]
    pieces = len(arrived) // (group - 1)
    held = {} if grad_tokens is None else {0: grad_tokens}
    return call(
        functools.partial(fold_kernel, columns, cut, relative, group, inner, pieces),
        "fold",
        ids,
        ((last - first) // 2,),
        inputs,
        held,
        outs,
        [
            pltpu.VMEM((2, blk, tok), BF16),
            pltpu.VMEM((2, blk, blk), BF16),
            pltpu.VMEM((2, blk, blk), F32),
            pltpu.VMEM((2, blk, blk), F32),
        ],
        after,
    )


def send(array, shift, group):
    return lax.ppermute(array, "mp", [(at, (at + shift) % group) for at in range(group)])


def gather_plain(shard):
    local, rows, blk = shard.shape
    whole = lax.all_gather(shard, "dp", axis=0, tiled=False)
    if rows % 16:
        whole = jnp.transpose(whole, (1, 0, 2, 3)).reshape(1, local, whole.shape[0] * rows, blk)
    return Whole([whole], [list(range(whole.shape[0]))], False)


def scatter_plain(term, rows, scale):
    if term.shape[2] != rows:
        _, count, whole, blk = term.shape
        term = jnp.transpose(term.reshape(count, whole // rows, rows, blk), (1, 0, 2, 3))
    return lax.psum_scatter(term, "dp", scatter_dimension=0, tiled=False) * scale


def on_device(tokens, upstream, first_factor, second_factor):
    local, rows, blk = first_factor.shape
    group, size = lax.axis_size("mp"), lax.axis_size("dp")
    width = blk // group
    scale = 1.0 / math.sqrt(tokens.shape[0] * size)
    me, device = lax.axis_index("mp"), lax.axis_index("dp")
    ids = jnp.stack([me, device]).astype(jnp.int32)
    cube = group == 2 and size >= 8 and size & (size - 1) == 0 and rows % 16 == 0 and width % 128 == 0
    net = Network(size) if cube else None
    cut = net.first_cut() if cube else [[0]]
    plain_cut = [list(range(size))] if cube else [[0]]
    j_spans = split_by(local, (6, 4, 4, 2)) if local % 8 == 0 else split_even(local, 4)
    b_spans = [(2 * lo, 2 * hi) for lo, hi in split_by(local // 2, (4, 3, 1))]
    shifts = list(range(1, group))

    second_whole = gather_plain(second_factor)
    if cube:
        shards = [
            lax.dynamic_slice_in_dim(first_factor, lax.rem(me + shift, group) * width, width, 2)
            for shift in range(2)
        ]
        far = net.gather(shards[1])
        shards[0], _ = lax.optimization_barrier((shards[0], net.first_got))
        columns = [far]
    else:
        whole = gather_plain(first_factor).arrays[0]
        if whole.shape[0] > 1:
            whole = jnp.transpose(whole, (1, 0, 2, 3)).reshape(1, local, blk, blk)
        turned = jnp.roll(whole, -me * width, axis=3)
        near, far, turned = [
            Whole([array], [[0]], False) for array in (turned[..., :width], turned[..., width:], turned)
        ]
        columns = [turned]
    sends = expand(ids, tokens, far, shifts, j_spans, group, local)
    arrived = [
        [send(sends[(shift - 1) * len(j_spans) + at], shift, group) for shift in shifts]
        for at in range(len(j_spans))
    ]
    if cube:
        near = net.gather(shards[0], sends)
        columns = [near, far]
    own = expand(ids, tokens, near, [0], [(0, local)], group, local)[0]

    held = {}
    backs = [(("back", place), b_span, (0, local)) for place, b_span in enumerate(b_spans)]
    for at, span in enumerate(j_spans):
        mix(
            ids, own, arrived[at], second_whole, tokens, upstream, held, span, group, local, cut, cube,
            ("term", (0, local)), backs,
        )
    returned = [[send(held[(key, shift)], shift, group) for shift in shifts] for key, _, _ in backs]
    parts = [held[("term", place)] for place in range(len(cut))]
    if cube:
        grad_second, marks = net.scatter(parts, scale)
    else:
        grad_second, marks = scatter_plain(parts[0], rows, scale), []

    grad_tokens, sums, terms, chains = None, [], [], [marks]
    tie = lambda place: [array for chain, step in TIES.get(place, ()) if cube for array in chains[chain][step]]
    for place, b_span in enumerate(b_spans):
        grad_tokens, *parts = fold(
            ids, held["own"], [(array, b_span[0]) for array in returned[place]], tokens, upstream, columns,
            grad_tokens, b_span, group, local, cut, cube, tie(place),
        )
        if cube:
            total, marks = net.scatter(parts, scale)
            chains.append(marks)
            sums.append(total)
        else:
            terms.append(parts[0])
    if not cube:
        sums = [scatter_plain(jnp.concatenate(terms, axis=1), rows, scale)]
    return held["mixed"], grad_tokens, jnp.concatenate(sums), grad_second


def solution(mesh):
    placed = (P("dp", "mp"), P("dp", "mp"), P("mp", "dp", None), P("mp", "dp", None))
    return jax.shard_map(
        on_device, mesh=mesh, in_specs=placed, out_specs=placed, check_vma=False
    )
```

```python
import functools
import math

import jax
import jax.numpy as jnp
from jax import lax
from jax.experimental import pallas as pl
from jax.experimental.pallas import tpu as pltpu
from jax.sharding import PartitionSpec as P

BF16 = jnp.bfloat16
F32 = jnp.float32
ROOT_HALF = math.sqrt(0.5)
DENSITY = 1.0 / math.sqrt(2.0 * math.pi)
TIES = {0: ((0, 1),), 1: ((1, 1), (0, 2)), 2: ((0, 3), (1, 2), (2, 1))}
VMEM = 20 * 1024 * 1024
LARGE = 1 << 20


def split_even(count, parts):
    parts = min(count, parts)
    edges = [count * step // parts for step in range(parts + 1)]
    return list(zip(edges[:-1], edges[1:]))


def split_by(count, weights):
    total, edges, run = sum(weights), [0], 0
    for weight in weights:
        run += weight
        edges.append(count * run // total)
    return [(lo, hi) for lo, hi in zip(edges[:-1], edges[1:]) if hi > lo]


def dot(left, right, left_dim, right_dim):
    return lax.dot_general(
        left, right, (((left_dim,), (right_dim,)), ((), ())), preferred_element_type=F32
    )


def aligned(index, size):
    return pl.ds(pl.multiple_of(index * size, size), size)


def far_off(array):
    return pltpu.with_memory_space_constraint(array, pltpu.HBM)


def call(kernel, name, ids, grid, inputs, held, outputs, scratch=(), after=()):
    places = sorted(held)
    extra = [held[place] for place in places] + list(after)
    taken = len(inputs)

    def body(ids_ref, *refs):
        kernel(ids_ref, *refs[:taken], *refs[taken + len(extra) :])

    return pl.pallas_call(
        body,
        grid_spec=pltpu.PrefetchScalarGridSpec(
            num_scalar_prefetch=1,
            grid=grid,
            in_specs=[spec for _, spec in inputs] + [pl.BlockSpec(memory_space=pl.ANY)] * len(extra),
            out_specs=[spec for _, _, spec in outputs],
            scratch_shapes=list(scratch),
        ),
        out_shape=[jax.ShapeDtypeStruct(shape, dtype) for shape, dtype, _ in outputs],
        input_output_aliases={1 + taken + at: place for at, place in enumerate(places)},
        compiler_params=pltpu.CompilerParams(
            dimension_semantics=("arbitrary",) * len(grid), vmem_limit_bytes=VMEM
        ),
        cost_estimate=pl.CostEstimate(flops=1, bytes_accessed=1, transcendentals=0),
        name=name,
    )(ids, *[far_off(array) if array.ndim != 3 and array.size >= LARGE else array for array, _ in inputs], *extra)


class Whole:
    def __init__(self, arrays, slots, relative):
        self.arrays, self.slots, self.relative = arrays, slots, relative

    def specs(self, count, at):
        return [
            (array, pl.BlockSpec((array.shape[0], count) + array.shape[2:], lambda step, _: (0, at(step), 0, 0)))
            for array in self.arrays
        ]

    def load(self, refs, block, target, device):
        if not self.relative:
            return refs[0][:, block].reshape(target.shape)
        for ref, slots in zip(refs, self.slots):
            rows = ref.shape[2]
            for place, slot in enumerate(slots):
                target[aligned(lax.bitwise_xor(device, slot), rows), :] = ref[place, block]
        return target[...]


def combos(bits):
    found = [0]
    for bit in bits:
        found += [value | bit for value in found]
    return found


class Network:
    def __init__(self, size):
        bits = [1 << k for k in range(size.bit_length() - 1)]
        self.size = size
        self.rounds = [tuple(bits[:1]), tuple(bits[1:2]), tuple(bits[2:])]
        self.rounds = [bits for bits in self.rounds if bits]
        self.order = [0]
        for bits in reversed(self.rounds):
            self.order = [slot | mask for mask in combos(bits) for slot in self.order]

    def swap(self, array, mask):
        return lax.ppermute(array, "dp", [(at, at ^ mask) for at in range(self.size)])

    def gather_first(self, shard):
        combo = combos(self.rounds[-1])
        return [shard[None]] + [self.swap(shard[None], mask) for mask in combo[1:]], combo

    def gather_rest(self, first):
        arrays, slots = first
        have = [(jnp.concatenate(arrays, axis=0), slots)]
        for bits in reversed(self.rounds[:-1]):
            for mask in combos(bits)[1:]:
                have = have + [(self.swap(array, mask), [slot | mask for slot in slots]) for array, slots in have]
        return Whole([array for array, _ in have], [slots for _, slots in have], True)

    def cut(self, slots, step):
        bits = self.rounds[step]
        mask = sum(bits)
        return [[slot for slot in slots if slot & mask == value] for value in combos(bits)]

    def first_cut(self):
        return self.cut(self.order, 0)

    def scatter(self, parts, scale):
        slots = self.first_cut()[0]
        total, sends, marks = parts[0], parts[1:], []
        for step, bits in enumerate(self.rounds):
            marks.append(sends)
            got = [self.swap(piece, mask) for piece, mask in zip(sends, combos(bits)[1:])]
            for piece in got:
                total = total + piece.astype(F32)
            if step + 1 < len(self.rounds):
                lists = self.cut(slots, step + 1)
                spans = [(slots.index(members[0]), slots.index(members[-1]) + 1) for members in lists]
                sends = [total[lo:hi].astype(BF16) for lo, hi in spans[1:]]
                total = total[spans[0][0] : spans[0][1]]
                slots = lists[0]
        result = total[0] * scale
        return result, marks + [[result]]


def expand_kernel(weights, shifts, spans, group, inner, ids, x_ref, *rest):
    w_refs, rest = rest[: len(weights.arrays)], rest[len(weights.arrays) :]
    outs, held = rest[:-1], rest[-1]
    blk = held.shape[1]
    halves = []
    for half in range(2):
        weight = weights.load(w_refs, half, held.at[half], ids[1])
        acts = x_ref[:, half * blk : (half + 1) * blk]
        halves.append(dot(acts, weight, 1, 0).astype(BF16).T.astype(F32))
    width = blk // group
    for at, _ in enumerate(shifts):
        parts = [
            full[at * width : (at + 1) * width].reshape(width // inner, inner, -1) for full in halves
        ]
        piece = jnp.concatenate(parts, axis=1).astype(BF16)
        for place, (start, stop) in enumerate(spans):
            outs[at * len(spans) + place][...] = piece[start:stop]


def expand(ids, tokens, weights, shifts, spans, group, local, after=()):
    tok = tokens.shape[0]
    blk = tokens.shape[1] // local
    inner = blk // (local * group)
    cols = len(shifts) * (blk // group)
    shapes = [stop - start for _ in shifts for start, stop in spans]
    return call(
        functools.partial(expand_kernel, weights, shifts, spans, group, inner),
        "expand",
        ids,
        (local // 2,),
        [(tokens, pl.BlockSpec((tok, 2 * blk), lambda pair, _: (0, pair)))]
        + weights.specs(2, lambda pair: pair),
        {},
        [
            (
                (count, local * inner, tok),
                BF16,
                pl.BlockSpec((count, 2 * inner, tok), lambda pair, _: (0, pair, 0)),
            )
            for count in shapes
        ],
        [pltpu.VMEM((2, blk, cols), BF16)],
        after,
    )


def order_matrix(blk, blocks, flip):
    inner = blk // blocks
    out = lax.broadcasted_iota(jnp.int32, (blk, blk), 1 if flip else 0)
    held = lax.broadcasted_iota(jnp.int32, (blk, blk), 0 if flip else 1)
    return (held == lax.rem(out, blocks) * inner + lax.div(out, blocks)).astype(F32).astype(BF16)


def store_term(term, slots_lists, relative, outs, scratch, device, block):
    if not relative:
        out = outs[0]
        out[:, block] = term.reshape(out.shape[0], out.shape[2], out.shape[3])
        return
    scratch[...] = term
    for out, slots in zip(outs, slots_lists):
        rows = out.shape[2]
        for place, slot in enumerate(slots):
            out[place, block] = scratch[aligned(lax.bitwise_xor(device, slot), rows), :].astype(out.dtype)


def mix_kernel(weights, cut, relative, group, blocks, backs, ids, own_ref, *rest):
    arrived, rest = rest[: group - 1], rest[group - 1 :]
    w_refs, rest = rest[: len(weights.arrays)], rest[len(weights.arrays) :]
    x_ref, up_ref = rest[:2]
    rest = rest[2:]
    mixed_ref, back_own_ref = rest[:2]
    term_refs, rest = rest[2 : 2 + len(cut)], rest[2 + len(cut) :]
    back_refs, (moved, back, held, term) = rest[:-4], rest[-4:]
    me = ids[0]
    blk = held.shape[1]
    rows = blk // group
    there = order_matrix(blk, blocks, False)
    again = order_matrix(blk, blocks, True)
    for j in range(held.shape[0]):
        cols = slice(j * blk, (j + 1) * blk)
        moved[j, aligned(me, rows), :] = own_ref[j]
        for shift in range(1, group):
            moved[j, aligned(lax.rem(me - shift + group, group), rows), :] = arrived[shift - 1][j]
        weight = weights.load(w_refs, j, held.at[j], ids[1])
        ordered = dot(there, moved[j], 1, 0).astype(BF16)
        inner_out = dot(ordered.T, weight, 1, 0)
        cdf = 0.5 + 0.5 * lax.erf(inner_out * ROOT_HALF)
        mixed_ref[:, cols] = (x_ref[:, cols].astype(F32) + inner_out * cdf).astype(BF16)
        slope = cdf + inner_out * (DENSITY * jnp.exp(-0.5 * inner_out * inner_out))
        grad_out = (up_ref[:, cols].astype(F32) * slope).astype(BF16)
        store_term(dot(ordered, grad_out, 1, 0), cut, relative, term_refs, term.at[j], ids[1], j)
        returned = dot(weight, grad_out, 1, 1).astype(BF16)
        back[j] = dot(again, returned, 1, 0).astype(BF16)
        back_own_ref[j] = back[j, aligned(me, rows), :]
        for shift in range(1, group):
            piece = back[j, aligned(lax.rem(me + shift, group), rows), :]
            for at, (start, stop) in enumerate(backs):
                back_refs[(shift - 1) * len(backs) + at][j] = piece[start:stop]


def mix(ids, own, arrived, weights, tokens, upstream, held, span, group, local, cut, relative, term, backs):
    tok = tokens.shape[0]
    blk = tokens.shape[1] // local
    feat = blk // group
    per = feat // local
    first, last = span
    rows = blk // sum(len(slots) for slots in cut)
    step = math.gcd(2, math.gcd(first, last))
    lane = pl.BlockSpec((tok, step * blk), lambda j, _: (0, first // step + j))
    at = pl.BlockSpec((step, feat, tok), lambda j, _: (first // step + j, 0, 0))
    keys = ["mixed", "own"]
    outs = [(tokens.shape, BF16, lane), ((local, feat, tok), BF16, at)]
    term_key, (term_first, term_last) = term
    for place, slots in enumerate(cut):
        keys.append((term_key, place))
        outs.append(
            (
                (len(slots), term_last - term_first, rows, blk),
                F32 if place == 0 else BF16,
                pl.BlockSpec((len(slots), step, rows, blk), lambda j, _: (0, (first - term_first) // step + j, 0, 0)),
            )
        )
    for shift in range(1, group):
        for key, (b_first, b_last), (j_first, j_last) in backs:
            keys.append((key, shift))
            outs.append(
                (
                    (j_last - j_first, (b_last - b_first) * per, tok),
                    BF16,
                    pl.BlockSpec(
                        (step, (b_last - b_first) * per, tok),
                        functools.partial(lambda start, j, _: (start + j, 0, 0), (first - j_first) // step),
                    ),
                )
            )
    kept = {place: held[key] for place, key in enumerate(keys) if key in held}
    cuts = [(b_first * per, b_last * per) for _, (b_first, b_last), _ in backs]
    got = call(
        functools.partial(mix_kernel, weights, cut, relative, group, local * group, cuts),
        "mix",
        ids,
        ((last - first) // step,),
        [(own, at)]
        + [(array, pl.BlockSpec((step, feat, tok), lambda j, _: (j, 0, 0))) for array in arrived]
        + weights.specs(step, lambda j: first // step + j)
        + [(tokens, lane), (upstream, lane)],
        kept,
        outs,
        [
            pltpu.VMEM((step, blk, tok), BF16),
            pltpu.VMEM((step, blk, tok), BF16),
            pltpu.VMEM((step, blk, blk), BF16),
            pltpu.VMEM((step, blk, blk), F32),
        ],
    )
    held.update(zip(keys, got))


def fold_kernel(columns, cut, relative, group, inner, pieces, ids, own_ref, *rest):
    arrived, rest = rest[: pieces * (group - 1)], rest[pieces * (group - 1) :]
    x_ref, up_ref = rest[:2]
    rest = rest[2:]
    w_refs = []
    for weights in columns:
        w_refs.append(rest[: len(weights.arrays)])
        rest = rest[len(weights.arrays) :]
    out_ref, term_refs = rest[0], rest[1:-4]
    inner_grad, held, sorted_term, term = rest[-4:]
    me = ids[0]
    blk = held.shape[2]
    width = blk // group
    for shift in range(group):
        if shift == 0:
            piece = own_ref[...]
        else:
            refs = arrived[(shift - 1) * pieces : shift * pieces]
            piece = jnp.concatenate([ref[...] for ref in refs], axis=0)
        piece = piece.astype(F32)
        for half in range(2):
            part = piece[:, half * inner : (half + 1) * inner].reshape(width, -1)
            inner_grad[half, shift * width : (shift + 1) * width, :] = part.astype(BF16)
    for half in range(2):
        cols = slice(half * blk, (half + 1) * blk)
        if len(columns) == 1:
            weight = columns[0].load(w_refs[0], half, held.at[half], ids[1])
        else:
            start = 0
            for weights, refs in zip(columns, w_refs):
                size = refs[0].shape[3]
                weights.load(refs, half, held.at[half, :, start : start + size], ids[1])
                start += size
            weight = held[half]
        du = inner_grad[half]
        unsorted = dot(du, x_ref[:, cols], 1, 0)
        for shift in range(group):
            source = lax.rem(me - shift + group, group)
            sorted_term[half, aligned(source, width), :] = unsorted[shift * width : (shift + 1) * width]
        store_term(sorted_term[half].T, cut, relative, term_refs, term.at[half], ids[1], half)
        back = dot(du.T, weight, 1, 1)
        out_ref[:, cols] = (up_ref[:, cols].astype(F32) + back).astype(BF16)


def fold(ids, own, arrived, tokens, upstream, columns, grad_tokens, span, group, local, cut, relative, after):
    tok = tokens.shape[0]
    blk = tokens.shape[1] // local
    inner = blk // (local * group)
    first, last = span
    rows = blk // sum(len(slots) for slots in cut)
    start = first // 2
    lane = pl.BlockSpec((tok, 2 * blk), lambda pair, _: (0, start + pair))
    inputs = []
    for array, begin in [(own, 0)] + arrived:
        at = functools.partial(lambda skip, pair, _: (0, skip + pair, 0), start - begin // 2)
        inputs.append((array, pl.BlockSpec((array.shape[0], 2 * inner, tok), at)))
    inputs += [(tokens, lane), (upstream, lane)]
    for weights in columns:
        inputs += weights.specs(2, lambda pair: start + pair)
    outs = [(tokens.shape, BF16, lane)] + [
        (
            (len(slots), last - first, rows, blk),
            F32 if place == 0 else BF16,
            pl.BlockSpec((len(slots), 2, rows, blk), lambda pair, _: (0, pair, 0, 0)),
        )
        for place, slots in enumerate(cut)
    ]
    pieces = len(arrived) // (group - 1)
    held = {} if grad_tokens is None else {0: grad_tokens}
    return call(
        functools.partial(fold_kernel, columns, cut, relative, group, inner, pieces),
        "fold",
        ids,
        ((last - first) // 2,),
        inputs,
        held,
        outs,
        [
            pltpu.VMEM((2, blk, tok), BF16),
            pltpu.VMEM((2, blk, blk), BF16),
            pltpu.VMEM((2, blk, blk), F32),
            pltpu.VMEM((2, blk, blk), F32),
        ],
        after,
    )


def send(array, shift, group):
    return lax.ppermute(array, "mp", [(at, (at + shift) % group) for at in range(group)])


def gather_plain(shard):
    local, rows, blk = shard.shape
    whole = lax.all_gather(shard, "dp", axis=0, tiled=False)
    if rows % 16:
        whole = jnp.transpose(whole, (1, 0, 2, 3)).reshape(1, local, whole.shape[0] * rows, blk)
    return Whole([whole], [list(range(whole.shape[0]))], False)


def scatter_plain(term, rows, scale):
    if term.shape[2] != rows:
        _, count, whole, blk = term.shape
        term = jnp.transpose(term.reshape(count, whole // rows, rows, blk), (1, 0, 2, 3))
    return lax.psum_scatter(term, "dp", scatter_dimension=0, tiled=False) * scale


def on_device(tokens, upstream, first_factor, second_factor):
    local, rows, blk = first_factor.shape
    group, size = lax.axis_size("mp"), lax.axis_size("dp")
    width = blk // group
    scale = 1.0 / math.sqrt(tokens.shape[0] * size)
    me, device = lax.axis_index("mp"), lax.axis_index("dp")
    ids = jnp.stack([me, device]).astype(jnp.int32)
    cube = group == 2 and size >= 8 and size & (size - 1) == 0 and rows % 16 == 0 and width % 128 == 0
    net = Network(size) if cube else None
    cut = net.first_cut() if cube else [[0]]
    plain_cut = [list(range(size))] if cube else [[0]]
    j_spans = split_by(local, (6, 4, 4, 2)) if local % 8 == 0 else split_even(local, 4)
    b_spans = [(2 * lo, 2 * hi) for lo, hi in split_by(local // 2, (4, 3, 1))]
    shifts = list(range(1, group))

    second_whole = gather_plain(second_factor)
    if cube:
        shards = [
            lax.dynamic_slice_in_dim(first_factor, lax.rem(me + shift, group) * width, width, 2)
            for shift in range(2)
        ]
        far_first = net.gather_first(shards[1])
        shards[0], _ = lax.optimization_barrier((shards[0], far_first[0]))
        near_first = net.gather_first(shards[0])
        far = net.gather_rest(far_first)
    else:
        whole = gather_plain(first_factor).arrays[0]
        if whole.shape[0] > 1:
            whole = jnp.transpose(whole, (1, 0, 2, 3)).reshape(1, local, blk, blk)
        turned = jnp.roll(whole, -me * width, axis=3)
        near, far, turned = [
            Whole([array], [[0]], False) for array in (turned[..., :width], turned[..., width:], turned)
        ]
        columns = [turned]
    sends = expand(ids, tokens, far, shifts, j_spans, group, local, near_first[0] if cube else ())
    arrived = [
        [send(sends[(shift - 1) * len(j_spans) + at], shift, group) for shift in shifts]
        for at in range(len(j_spans))
    ]
    if cube:
        near = net.gather_rest(near_first)
        columns = [near, far]
    own = expand(ids, tokens, near, [0], [(0, local)], group, local)[0]

    held = {}
    backs = [(("back", place), b_span, (0, local)) for place, b_span in enumerate(b_spans)]
    for at, span in enumerate(j_spans):
        mix(
            ids, own, arrived[at], second_whole, tokens, upstream, held, span, group, local, cut, cube,
            ("term", (0, local)), backs,
        )
    returned = [[send(held[(key, shift)], shift, group) for shift in shifts] for key, _, _ in backs]
    parts = [held[("term", place)] for place in range(len(cut))]
    if cube:
        grad_second, marks = net.scatter(parts, scale)
    else:
        grad_second, marks = scatter_plain(parts[0], rows, scale), []

    grad_tokens, sums, terms, chains = None, [], [], [marks]
    tie = lambda place: [array for chain, step in TIES.get(place, ()) if cube for array in chains[chain][step]]
    for place, b_span in enumerate(b_spans):
        grad_tokens, *parts = fold(
            ids, held["own"], [(array, b_span[0]) for array in returned[place]], tokens, upstream, columns,
            grad_tokens, b_span, group, local, cut, cube, tie(place),
        )
        if cube:
            total, marks = net.scatter(parts, scale)
            chains.append(marks)
            sums.append(total)
        else:
            terms.append(parts[0])
    if not cube:
        sums = [scatter_plain(jnp.concatenate(terms, axis=1), rows, scale)]
    return held["mixed"], grad_tokens, jnp.concatenate(sums), grad_second


def solution(mesh):
    placed = (P("dp", "mp"), P("dp", "mp"), P("mp", "dp", None), P("mp", "dp", None))
    return jax.shard_map(
        on_device, mesh=mesh, in_specs=placed, out_specs=placed, check_vma=False
    )
```

```python
import functools
import math

import jax
import jax.numpy as jnp
from jax import lax
from jax.experimental import pallas as pl
from jax.experimental.pallas import tpu as pltpu
from jax.sharding import PartitionSpec as P

BF16 = jnp.bfloat16
F32 = jnp.float32
ROOT_HALF = math.sqrt(0.5)
DENSITY = 1.0 / math.sqrt(2.0 * math.pi)
TIES = {0: ((0, 1),), 1: ((1, 1), (0, 2)), 2: ((0, 3), (1, 2), (2, 1))}
VMEM = 20 * 1024 * 1024


def split_even(count, parts):
    parts = min(count, parts)
    edges = [count * step // parts for step in range(parts + 1)]
    return list(zip(edges[:-1], edges[1:]))


def split_by(count, weights):
    total, edges, run = sum(weights), [0], 0
    for weight in weights:
        run += weight
        edges.append(count * run // total)
    return [(lo, hi) for lo, hi in zip(edges[:-1], edges[1:]) if hi > lo]


def dot(left, right, left_dim, right_dim):
    return lax.dot_general(
        left, right, (((left_dim,), (right_dim,)), ((), ())), preferred_element_type=F32
    )


def aligned(index, size):
    return pl.ds(pl.multiple_of(index * size, size), size)


def far_off(array):
    return pltpu.with_memory_space_constraint(array, pltpu.HBM)


def call(kernel, name, ids, grid, inputs, held, outputs, scratch=(), after=()):
    places = sorted(held)
    extra = [held[place] for place in places] + list(after)
    taken = len(inputs)

    def body(ids_ref, *refs):
        kernel(ids_ref, *refs[:taken], *refs[taken + len(extra) :])

    return pl.pallas_call(
        body,
        grid_spec=pltpu.PrefetchScalarGridSpec(
            num_scalar_prefetch=1,
            grid=grid,
            in_specs=[spec for _, spec in inputs] + [pl.BlockSpec(memory_space=pl.ANY)] * len(extra),
            out_specs=[spec for _, _, spec in outputs],
            scratch_shapes=list(scratch),
        ),
        out_shape=[jax.ShapeDtypeStruct(shape, dtype) for shape, dtype, _ in outputs],
        input_output_aliases={1 + taken + at: place for at, place in enumerate(places)},
        compiler_params=pltpu.CompilerParams(
            dimension_semantics=("arbitrary",) * len(grid), vmem_limit_bytes=VMEM
        ),
        cost_estimate=pl.CostEstimate(flops=1, bytes_accessed=1, transcendentals=0),
        name=name,
    )(ids, *[far_off(array) if array.ndim == 2 else array for array, _ in inputs], *extra)


class Whole:
    def __init__(self, arrays, slots, mask):
        self.arrays, self.slots, self.mask = arrays, slots, mask

    def specs(self, count, at):
        return [
            (array, pl.BlockSpec((array.shape[0], count) + array.shape[2:], lambda step, _: (0, at(step), 0, 0)))
            for array in self.arrays
        ]

    def load(self, refs, block, target, device):
        if not self.mask:
            return refs[0][:, block].reshape(target.shape)
        turn = lax.bitwise_and(device, self.mask)
        for ref, slots in zip(refs, self.slots):
            rows = ref.shape[2]
            for place, slot in enumerate(slots):
                target[aligned(lax.bitwise_xor(turn, slot), rows), :] = ref[place, block]
        return target[...]


def combos(bits):
    found = [0]
    for bit in bits:
        found += [value | bit for value in found]
    return found


class Network:
    def __init__(self, size):
        bits = [1 << k for k in range(size.bit_length() - 1)]
        self.size = size
        self.rounds = [tuple(bits[:1]), tuple(bits[1:2]), tuple(bits[2:])]
        self.rounds = [bits for bits in self.rounds if bits]
        self.order = [0]
        for bits in reversed(self.rounds):
            self.order = [slot | mask for mask in combos(bits) for slot in self.order]

    def swap(self, array, mask):
        return lax.ppermute(array, "dp", [(at, at ^ mask) for at in range(self.size)])

    def gather_first(self, shard):
        combo = combos(self.rounds[-1])
        return [shard[None]] + [self.swap(shard[None], mask) for mask in combo[1:]], combo

    def gather_rest(self, first, until=None):
        arrays, slots = first
        have = [(jnp.concatenate(arrays, axis=0), slots)]
        for bits in reversed(self.rounds[:-1]):
            for mask in combos(bits)[1:]:
                got = [self.swap(array, mask) for array, _ in have]
                if until is not None:
                    got, until = lax.optimization_barrier((got, until))[0], None
                have = have + [(array, [slot | mask for slot in slots]) for array, (_, slots) in zip(got, have)]
        return Whole([array for array, _ in have], [slots for _, slots in have], self.size - 1)

    def gather_aside(self, shard):
        groups = [list(range(low, self.size, 2)) for low in range(2)]
        return lax.all_gather(shard, "dp", axis=0, tiled=False, axis_index_groups=groups)

    def gather_both(self, mine, until):
        groups = [list(range(low, self.size, 2)) for low in range(2)]
        mine, _ = lax.optimization_barrier((mine, until))
        return Whole([mine, self.swap(mine, 1)], [groups[0], groups[1]], 1)

    def cut(self, slots, step):
        bits = self.rounds[step]
        mask = sum(bits)
        return [[slot for slot in slots if slot & mask == value] for value in combos(bits)]

    def first_cut(self):
        return self.cut(self.order, 0)

    def scatter(self, parts, scale):
        slots = self.first_cut()[0]
        total, sends, marks = parts[0], parts[1:], []
        for step, bits in enumerate(self.rounds):
            marks.append(sends)
            got = [self.swap(piece, mask) for piece, mask in zip(sends, combos(bits)[1:])]
            for piece in got:
                total = total + piece.astype(F32)
            if step + 1 < len(self.rounds):
                lists = self.cut(slots, step + 1)
                spans = [(slots.index(members[0]), slots.index(members[-1]) + 1) for members in lists]
                sends = [total[lo:hi].astype(BF16) for lo, hi in spans[1:]]
                total = total[spans[0][0] : spans[0][1]]
                slots = lists[0]
        result = total[0] * scale
        return result, marks + [[result]]


def expand_kernel(weights, shifts, spans, group, inner, ids, *rest):
    x_refs, rest = rest[:2], rest[2:]
    w_refs, rest = rest[: len(weights.arrays)], rest[len(weights.arrays) :]
    outs, held = rest[:-1], rest[-1]
    blk = held.shape[1]
    halves = []
    for half in range(2):
        weight = weights.load(w_refs, half, held.at[half], ids[1])
        halves.append(dot(x_refs[half][...], weight, 1, 0).astype(BF16).T.astype(F32))
    width = blk // group
    for at, _ in enumerate(shifts):
        parts = [
            full[at * width : (at + 1) * width].reshape(width // inner, inner, -1) for full in halves
        ]
        piece = jnp.concatenate(parts, axis=1).astype(BF16)
        for place, (start, stop) in enumerate(spans):
            outs[at * len(spans) + place][...] = piece[start:stop]


def expand(ids, tokens, weights, shifts, spans, group, local, after=()):
    tok = tokens.shape[0]
    blk = tokens.shape[1] // local
    inner = blk // (local * group)
    cols = len(shifts) * (blk // group)
    shapes = [stop - start for _ in shifts for start, stop in spans]
    return call(
        functools.partial(expand_kernel, weights, shifts, spans, group, inner),
        "expand",
        ids,
        (local // 2,),
        [
            (tokens, pl.BlockSpec((tok, blk), functools.partial(lambda half, pair, _: (0, 2 * pair + half), half)))
            for half in range(2)
        ]
        + weights.specs(2, lambda pair: pair),
        {},
        [
            (
                (count, local * inner, tok),
                BF16,
                pl.BlockSpec((count, 2 * inner, tok), lambda pair, _: (0, pair, 0)),
            )
            for count in shapes
        ],
        [pltpu.VMEM((2, blk, cols), BF16)],
        after,
    )


def order_matrix(blk, blocks, flip):
    inner = blk // blocks
    out = lax.broadcasted_iota(jnp.int32, (blk, blk), 1 if flip else 0)
    held = lax.broadcasted_iota(jnp.int32, (blk, blk), 0 if flip else 1)
    return (held == lax.rem(out, blocks) * inner + lax.div(out, blocks)).astype(F32).astype(BF16)


def store_term(term, slots_lists, relative, outs, scratch, device, block):
    if not relative:
        out = outs[0]
        out[:, block] = term.reshape(out.shape[0], out.shape[2], out.shape[3])
        return
    scratch[...] = term
    for out, slots in zip(outs, slots_lists):
        rows = out.shape[2]
        for place, slot in enumerate(slots):
            out[place, block] = scratch[aligned(lax.bitwise_xor(device, slot), rows), :].astype(out.dtype)


def mix_kernel(weights, cut, relative, group, blocks, backs, ids, own_ref, *rest):
    arrived, rest = rest[: group - 1], rest[group - 1 :]
    w_refs, rest = rest[: len(weights.arrays)], rest[len(weights.arrays) :]
    x_ref, up_ref = rest[:2]
    rest = rest[2:]
    mixed_ref, back_own_ref = rest[:2]
    term_refs, rest = rest[2 : 2 + len(cut)], rest[2 + len(cut) :]
    back_refs, (moved, back, held, term) = rest[:-4], rest[-4:]
    me = ids[0]
    blk = held.shape[1]
    rows = blk // group
    there = order_matrix(blk, blocks, False)
    again = order_matrix(blk, blocks, True)
    for j in range(held.shape[0]):
        cols = slice(j * blk, (j + 1) * blk)
        moved[j, aligned(me, rows), :] = own_ref[j]
        for shift in range(1, group):
            moved[j, aligned(lax.rem(me - shift + group, group), rows), :] = arrived[shift - 1][j]
        weight = weights.load(w_refs, j, held.at[j], ids[1])
        ordered = dot(there, moved[j], 1, 0).astype(BF16)
        inner_out = dot(ordered.T, weight, 1, 0)
        cdf = 0.5 + 0.5 * lax.erf(inner_out * ROOT_HALF)
        mixed_ref[:, cols] = (x_ref[:, cols].astype(F32) + inner_out * cdf).astype(BF16)
        slope = cdf + inner_out * (DENSITY * jnp.exp(-0.5 * inner_out * inner_out))
        grad_out = (up_ref[:, cols].astype(F32) * slope).astype(BF16)
        store_term(dot(ordered, grad_out, 1, 0), cut, relative, term_refs, term.at[j], ids[1], j)
        returned = dot(weight, grad_out, 1, 1).astype(BF16)
        back[j] = dot(again, returned, 1, 0).astype(BF16)
        back_own_ref[j] = back[j, aligned(me, rows), :]
        for shift in range(1, group):
            piece = back[j, aligned(lax.rem(me + shift, group), rows), :]
            for at, (start, stop) in enumerate(backs):
                back_refs[(shift - 1) * len(backs) + at][j] = piece[start:stop]


def mix(ids, own, arrived, weights, tokens, upstream, held, span, group, local, cut, relative, term, backs):
    tok = tokens.shape[0]
    blk = tokens.shape[1] // local
    feat = blk // group
    per = feat // local
    first, last = span
    rows = blk // sum(len(slots) for slots in cut)
    step = math.gcd(2, math.gcd(first, last))
    lane = pl.BlockSpec((tok, step * blk), lambda j, _: (0, first // step + j))
    at = pl.BlockSpec((step, feat, tok), lambda j, _: (first // step + j, 0, 0))
    keys = ["mixed", "own"]
    outs = [(tokens.shape, BF16, lane), ((local, feat, tok), BF16, at)]
    term_key, (term_first, term_last) = term
    for place, slots in enumerate(cut):
        keys.append((term_key, place))
        outs.append(
            (
                (len(slots), term_last - term_first, rows, blk),
                F32 if place == 0 else BF16,
                pl.BlockSpec((len(slots), step, rows, blk), lambda j, _: (0, (first - term_first) // step + j, 0, 0)),
            )
        )
    for shift in range(1, group):
        for key, (b_first, b_last), (j_first, j_last) in backs:
            keys.append((key, shift))
            outs.append(
                (
                    (j_last - j_first, (b_last - b_first) * per, tok),
                    BF16,
                    pl.BlockSpec(
                        (step, (b_last - b_first) * per, tok),
                        functools.partial(lambda start, j, _: (start + j, 0, 0), (first - j_first) // step),
                    ),
                )
            )
    kept = {place: held[key] for place, key in enumerate(keys) if key in held}
    cuts = [(b_first * per, b_last * per) for _, (b_first, b_last), _ in backs]
    got = call(
        functools.partial(mix_kernel, weights, cut, relative, group, local * group, cuts),
        "mix",
        ids,
        ((last - first) // step,),
        [(own, at)]
        + [(array, pl.BlockSpec((step, feat, tok), lambda j, _: (j, 0, 0))) for array in arrived]
        + weights.specs(step, lambda j: first // step + j)
        + [(tokens, lane), (upstream, lane)],
        kept,
        outs,
        [
            pltpu.VMEM((step, blk, tok), BF16),
            pltpu.VMEM((step, blk, tok), BF16),
            pltpu.VMEM((step, blk, blk), BF16),
            pltpu.VMEM((step, blk, blk), F32),
        ],
    )
    held.update(zip(keys, got))


def fold_kernel(columns, cut, relative, group, inner, pieces, ids, own_ref, *rest):
    arrived, rest = rest[: pieces * (group - 1)], rest[pieces * (group - 1) :]
    x_ref, up_ref = rest[:2]
    rest = rest[2:]
    w_refs = []
    for weights in columns:
        w_refs.append(rest[: len(weights.arrays)])
        rest = rest[len(weights.arrays) :]
    out_ref, term_refs = rest[0], rest[1:-4]
    inner_grad, held, sorted_term, term = rest[-4:]
    me = ids[0]
    blk = held.shape[2]
    width = blk // group
    for shift in range(group):
        if shift == 0:
            piece = own_ref[...]
        else:
            refs = arrived[(shift - 1) * pieces : shift * pieces]
            piece = jnp.concatenate([ref[...] for ref in refs], axis=0)
        piece = piece.astype(F32)
        for half in range(2):
            part = piece[:, half * inner : (half + 1) * inner].reshape(width, -1)
            inner_grad[half, shift * width : (shift + 1) * width, :] = part.astype(BF16)
    for half in range(2):
        cols = slice(half * blk, (half + 1) * blk)
        if len(columns) == 1:
            weight = columns[0].load(w_refs[0], half, held.at[half], ids[1])
        else:
            start = 0
            for weights, refs in zip(columns, w_refs):
                size = refs[0].shape[3]
                weights.load(refs, half, held.at[half, :, start : start + size], ids[1])
                start += size
            weight = held[half]
        du = inner_grad[half]
        unsorted = dot(du, x_ref[:, cols], 1, 0)
        for shift in range(group):
            source = lax.rem(me - shift + group, group)
            sorted_term[half, aligned(source, width), :] = unsorted[shift * width : (shift + 1) * width]
        store_term(sorted_term[half].T, cut, relative, term_refs, term.at[half], ids[1], half)
        back = dot(du.T, weight, 1, 1)
        out_ref[:, cols] = (up_ref[:, cols].astype(F32) + back).astype(BF16)


def fold(ids, own, arrived, tokens, upstream, columns, grad_tokens, span, group, local, cut, relative, after):
    tok = tokens.shape[0]
    blk = tokens.shape[1] // local
    inner = blk // (local * group)
    first, last = span
    rows = blk // sum(len(slots) for slots in cut)
    start = first // 2
    lane = pl.BlockSpec((tok, 2 * blk), lambda pair, _: (0, start + pair))
    inputs = []
    for array, begin in [(own, 0)] + arrived:
        at = functools.partial(lambda skip, pair, _: (0, skip + pair, 0), start - begin // 2)
        inputs.append((array, pl.BlockSpec((array.shape[0], 2 * inner, tok), at)))
    inputs += [(tokens, lane), (upstream, lane)]
    for weights in columns:
        inputs += weights.specs(2, lambda pair: start + pair)
    outs = [(tokens.shape, BF16, lane)] + [
        (
            (len(slots), last - first, rows, blk),
            F32 if place == 0 else BF16,
            pl.BlockSpec((len(slots), 2, rows, blk), lambda pair, _: (0, pair, 0, 0)),
        )
        for place, slots in enumerate(cut)
    ]
    pieces = len(arrived) // (group - 1)
    held = {} if grad_tokens is None else {0: grad_tokens}
    return call(
        functools.partial(fold_kernel, columns, cut, relative, group, inner, pieces),
        "fold",
        ids,
        ((last - first) // 2,),
        inputs,
        held,
        outs,
        [
            pltpu.VMEM((2, blk, tok), BF16),
            pltpu.VMEM((2, blk, blk), BF16),
            pltpu.VMEM((2, blk, blk), F32),
            pltpu.VMEM((2, blk, blk), F32),
        ],
        after,
    )


def send(array, shift, group):
    return lax.ppermute(array, "mp", [(at, (at + shift) % group) for at in range(group)])


def gather_plain(shard):
    local, rows, blk = shard.shape
    whole = lax.all_gather(shard, "dp", axis=0, tiled=False)
    if rows % 16:
        whole = jnp.transpose(whole, (1, 0, 2, 3)).reshape(1, local, whole.shape[0] * rows, blk)
    return Whole([whole], [list(range(whole.shape[0]))], 0)


def scatter_plain(term, rows, scale):
    if term.shape[2] != rows:
        _, count, whole, blk = term.shape
        term = jnp.transpose(term.reshape(count, whole // rows, rows, blk), (1, 0, 2, 3))
    return lax.psum_scatter(term, "dp", scatter_dimension=0, tiled=False) * scale


def on_device(tokens, upstream, first_factor, second_factor):
    local, rows, blk = first_factor.shape
    group, size = lax.axis_size("mp"), lax.axis_size("dp")
    width = blk // group
    scale = 1.0 / math.sqrt(tokens.shape[0] * size)
    me, device = lax.axis_index("mp"), lax.axis_index("dp")
    ids = jnp.stack([me, device]).astype(jnp.int32)
    cube = group == 2 and size >= 8 and size & (size - 1) == 0 and rows % 16 == 0 and width % 128 == 0
    net = Network(size) if cube else None
    cut = net.first_cut() if cube else [[0]]
    plain_cut = [list(range(size))] if cube else [[0]]
    j_spans = split_by(local, (6, 4, 4, 2)) if local % 8 == 0 else split_even(local, 4)
    b_spans = [(2 * lo, 2 * hi) for lo, hi in split_by(local // 2, (4, 3, 1))]
    shifts = list(range(1, group))

    second_whole = net.gather_aside(second_factor) if cube else gather_plain(second_factor)
    if cube:
        shards = [
            lax.dynamic_slice_in_dim(first_factor, lax.rem(me + shift, group) * width, width, 2)
            for shift in range(2)
        ]
        far_first = net.gather_first(shards[1])
        near_first = net.gather_first(shards[0])
        far = net.gather_rest(far_first, near_first[0])
    else:
        whole = gather_plain(first_factor).arrays[0]
        if whole.shape[0] > 1:
            whole = jnp.transpose(whole, (1, 0, 2, 3)).reshape(1, local, blk, blk)
        turned = jnp.roll(whole, -me * width, axis=3)
        near, far, turned = [
            Whole([array], [[0]], 0) for array in (turned[..., :width], turned[..., width:], turned)
        ]
        columns = [turned]
    sends = expand(ids, tokens, far, shifts, j_spans, group, local)
    arrived = [
        [send(sends[(shift - 1) * len(j_spans) + at], shift, group) for shift in shifts]
        for at in range(len(j_spans))
    ]
    if cube:
        near = net.gather_rest(near_first)
        columns = [near, far]
    if cube:
        second_whole = net.gather_both(second_whole, near.arrays[1])
    own = expand(ids, tokens, near, [0], [(0, local)], group, local)[0]

    held = {}
    backs = [(("back", place), b_span, (0, local)) for place, b_span in enumerate(b_spans)]
    for at, span in enumerate(j_spans):
        mix(
            ids, own, arrived[at], second_whole, tokens, upstream, held, span, group, local, cut, cube,
            ("term", (0, local)), backs,
        )
    returned = [[send(held[(key, shift)], shift, group) for shift in shifts] for key, _, _ in backs]
    parts = [held[("term", place)] for place in range(len(cut))]
    if cube:
        grad_second, marks = net.scatter(parts, scale)
    else:
        grad_second, marks = scatter_plain(parts[0], rows, scale), []

    grad_tokens, sums, terms, chains = None, [], [], [marks]
    tie = lambda place: [array for chain, step in TIES.get(place, ()) if cube for array in chains[chain][step]]
    for place, b_span in enumerate(b_spans):
        grad_tokens, *parts = fold(
            ids, held["own"], [(array, b_span[0]) for array in returned[place]], tokens, upstream, columns,
            grad_tokens, b_span, group, local, cut, cube, tie(place),
        )
        if cube:
            total, marks = net.scatter(parts, scale)
            chains.append(marks)
            sums.append(total)
        else:
            terms.append(parts[0])
    if not cube:
        sums = [scatter_plain(jnp.concatenate(terms, axis=1), rows, scale)]
    return held["mixed"], grad_tokens, jnp.concatenate(sums), grad_second


def solution(mesh):
    placed = (P("dp", "mp"), P("dp", "mp"), P("mp", "dp", None), P("mp", "dp", None))
    return jax.shard_map(
        on_device, mesh=mesh, in_specs=placed, out_specs=placed, check_vma=False
    )
```

```python
import functools
import math

import jax
import jax.numpy as jnp
from jax import lax
from jax.experimental import pallas as pl
from jax.experimental.pallas import tpu as pltpu
from jax.sharding import PartitionSpec as P

BF16 = jnp.bfloat16
F32 = jnp.float32
ROOT_HALF = math.sqrt(0.5)
DENSITY = 1.0 / math.sqrt(2.0 * math.pi)
TIES = {0: ((0, 1),), 1: ((1, 1), ), 2: ((0, 3), (1, 2), (2, 1))}
VMEM = 20 * 1024 * 1024


def split_by(count, weights):
    total, edges, run = sum(weights), [0], 0
    for weight in weights:
        run += weight
        edges.append(count * run // total)
    return [(lo, hi) for lo, hi in zip(edges[:-1], edges[1:]) if hi > lo]


def dot(left, right, left_dim, right_dim):
    return lax.dot_general(
        left, right, (((left_dim,), (right_dim,)), ((), ())), preferred_element_type=F32
    )


def aligned(index, size):
    return pl.ds(pl.multiple_of(index * size, size), size)


def far_off(array):
    return pltpu.with_memory_space_constraint(array, pltpu.HBM)


def call(kernel, name, ids, grid, inputs, held, outputs, scratch=(), after=()):
    places = sorted(held)
    extra = [held[place] for place in places] + list(after)
    taken = len(inputs)

    def body(ids_ref, *refs):
        kernel(ids_ref, *refs[:taken], *refs[taken + len(extra) :])

    return pl.pallas_call(
        body,
        grid_spec=pltpu.PrefetchScalarGridSpec(
            num_scalar_prefetch=1,
            grid=grid,
            in_specs=[spec for _, spec in inputs] + [pl.BlockSpec(memory_space=pl.ANY)] * len(extra),
            out_specs=[spec for _, _, spec in outputs],
            scratch_shapes=list(scratch),
        ),
        out_shape=[jax.ShapeDtypeStruct(shape, dtype) for shape, dtype, _ in outputs],
        input_output_aliases={1 + taken + at: place for at, place in enumerate(places)},
        compiler_params=pltpu.CompilerParams(
            dimension_semantics=("arbitrary",) * len(grid), vmem_limit_bytes=VMEM
        ),
        cost_estimate=pl.CostEstimate(flops=1, bytes_accessed=1, transcendentals=0),
        name=name,
    )(ids, *[far_off(array) if array.ndim == 2 else array for array, _ in inputs], *extra)


class Whole:
    def __init__(self, arrays, slots, relative, first=0):
        self.arrays, self.slots, self.relative, self.first = arrays, slots, relative, first

    def specs(self, count, at):
        skip = self.first // count
        return [
            (
                array,
                pl.BlockSpec(
                    (array.shape[0], count) + array.shape[2:], lambda step, _: (0, at(step) - skip, 0, 0)
                ),
            )
            for array in self.arrays
        ]

    def load(self, refs, block, target, device):
        if not self.relative:
            return refs[0][:, block].reshape(target.shape)
        for ref, slots in zip(refs, self.slots):
            rows = ref.shape[2]
            for place, slot in enumerate(slots):
                target[aligned(lax.bitwise_xor(device, slot), rows), :] = ref[place, block]
        return target[...]


def combos(bits):
    found = [0]
    for bit in bits:
        found += [value | bit for value in found]
    return found


class Network:
    def __init__(self, size):
        bits = [1 << k for k in range(size.bit_length() - 1)]
        self.size = size
        self.rounds = [tuple(bits[:1]), tuple(bits[1:2]), tuple(bits[2:])]
        self.rounds = [bits for bits in self.rounds if bits]
        self.order = [0]
        for bits in reversed(self.rounds):
            self.order = [slot | mask for mask in combos(bits) for slot in self.order]

    def swap(self, array, mask):
        return lax.ppermute(array, "dp", [(at, at ^ mask) for at in range(self.size)])

    def gather_first(self, shard):
        combo = combos(self.rounds[-1])
        return [shard[None]] + [self.swap(shard[None], mask) for mask in combo[1:]], combo

    def gather_rest(self, first, begin, until):
        arrays, slots = first
        joined = jnp.concatenate(arrays, axis=0)
        if until is not None:
            joined, _ = lax.optimization_barrier((joined, until))
        have = [(joined, slots)]
        for bits in reversed(self.rounds[:-1]):
            for mask in combos(bits)[1:]:
                have = have + [(self.swap(array, mask), [slot | mask for slot in slots]) for array, slots in have]
        return Whole([array for array, _ in have], [slots for _, slots in have], True, begin)

    def cut(self, slots, step):
        bits = self.rounds[step]
        mask = sum(bits)
        return [[slot for slot in slots if slot & mask == value] for value in combos(bits)]

    def first_cut(self):
        return self.cut(self.order, 0)

    def scatter(self, parts, scale):
        slots = self.first_cut()[0]
        total, sends, marks = parts[0], parts[1:], []
        for step, bits in enumerate(self.rounds):
            marks.append(sends)
            got = [self.swap(piece, mask) for piece, mask in zip(sends, combos(bits)[1:])]
            for piece in got:
                total = total + piece.astype(F32)
            if step + 1 < len(self.rounds):
                lists = self.cut(slots, step + 1)
                spans = [(slots.index(members[0]), slots.index(members[-1]) + 1) for members in lists]
                sends = [total[lo:hi].astype(BF16) for lo, hi in spans[1:]]
                total = total[spans[0][0] : spans[0][1]]
                slots = lists[0]
        result = total[0] * scale
        return result, marks + [[result]]


def expand_kernel(weights, spans, group, inner, ids, *rest):
    x_refs, rest = rest[:2], rest[2:]
    w_refs, rest = rest[: len(weights.arrays)], rest[len(weights.arrays) :]
    own_ref, outs, (held, full) = rest[0], rest[1:-2], rest[-2:]
    blk = held.shape[1]
    width = blk // group
    for half in range(2):
        weight = weights.load(w_refs, half, held.at[half], ids[1])
        full[half] = dot(x_refs[half][...], weight, 1, 0).astype(BF16).T.astype(F32)
    for shift in range(group):
        peer = lax.rem(ids[0] + shift, group)
        parts = [full[half, aligned(peer, width), :].reshape(width // inner, inner, -1) for half in range(2)]
        piece = jnp.concatenate(parts, axis=1).astype(BF16)
        if shift == 0:
            own_ref[...] = piece
        else:
            for place, (start, stop) in enumerate(spans):
                outs[(shift - 1) * len(spans) + place][...] = piece[start:stop]


def expand(ids, tokens, weights, b_span, spans, group, local):
    tok = tokens.shape[0]
    blk = tokens.shape[1] // local
    inner = blk // (local * group)
    first, last = b_span
    start = first // 2
    shapes = [local] + [hi - lo for _ in range(group - 1) for lo, hi in spans]
    return call(
        functools.partial(expand_kernel, weights, spans, group, inner),
        "expand",
        ids,
        ((last - first) // 2,),
        [
            (
                tokens,
                pl.BlockSpec(
                    (tok, blk), functools.partial(lambda half, pair, _: (0, 2 * (start + pair) + half), half)
                ),
            )
            for half in range(2)
        ]
        + weights.specs(2, lambda pair: start + pair),
        {},
        [
            (
                (count, (last - first) * inner, tok),
                BF16,
                pl.BlockSpec((count, 2 * inner, tok), lambda pair, _: (0, pair, 0)),
            )
            for count in shapes
        ],
        [pltpu.VMEM((2, blk, blk), BF16), pltpu.VMEM((2, blk, tok), F32)],
    )


def order_matrix(blk, blocks, flip):
    inner = blk // blocks
    out = lax.broadcasted_iota(jnp.int32, (blk, blk), 1 if flip else 0)
    held = lax.broadcasted_iota(jnp.int32, (blk, blk), 0 if flip else 1)
    return (held == lax.rem(out, blocks) * inner + lax.div(out, blocks)).astype(F32).astype(BF16)


def store_term(term, slots_lists, relative, outs, scratch, device, block):
    if not relative:
        out = outs[0]
        out[:, block] = term.reshape(out.shape[0], out.shape[2], out.shape[3])
        return
    scratch[...] = term
    for out, slots in zip(outs, slots_lists):
        rows = out.shape[2]
        for place, slot in enumerate(slots):
            out[place, block] = scratch[aligned(lax.bitwise_xor(device, slot), rows), :].astype(out.dtype)


def mix_kernel(weights, cut, relative, group, blocks, backs, parts, ids, *rest):
    count = group * len(parts)
    moves, rest = rest[:count], rest[count:]
    w_refs, rest = rest[: len(weights.arrays)], rest[len(weights.arrays) :]
    x_ref, up_ref = rest[:2]
    rest = rest[2:]
    mixed_ref, back_own_ref = rest[:2]
    term_refs, rest = rest[2 : 2 + len(cut)], rest[2 + len(cut) :]
    back_refs, (moved, back, held, term) = rest[:-4], rest[-4:]
    me = ids[0]
    blk = held.shape[1]
    rows = blk // group
    there = order_matrix(blk, blocks, False)
    again = order_matrix(blk, blocks, True)
    for j in range(held.shape[0]):
        cols = slice(j * blk, (j + 1) * blk)
        for shift in range(group):
            source = lax.rem(me - shift + group, group) * rows
            for place, (start, stop) in enumerate(parts):
                span = pl.ds(pl.multiple_of(source + start, math.gcd(rows, start)), stop - start)
                moved[j, span, :] = moves[shift * len(parts) + place][j]
        weight = weights.load(w_refs, j, held.at[j], ids[1])
        ordered = dot(there, moved[j], 1, 0).astype(BF16)
        inner_out = dot(ordered.T, weight, 1, 0)
        cdf = 0.5 + 0.5 * lax.erf(inner_out * ROOT_HALF)
        mixed_ref[:, cols] = (x_ref[:, cols].astype(F32) + inner_out * cdf).astype(BF16)
        slope = cdf + inner_out * (DENSITY * jnp.exp(-0.5 * inner_out * inner_out))
        grad_out = (up_ref[:, cols].astype(F32) * slope).astype(BF16)
        store_term(dot(ordered, grad_out, 1, 0), cut, relative, term_refs, term.at[j], ids[1], j)
        returned = dot(weight, grad_out, 1, 1).astype(BF16)
        back[j] = dot(again, returned, 1, 0).astype(BF16)
        back_own_ref[j] = back[j, aligned(me, rows), :]
        for shift in range(1, group):
            piece = back[j, aligned(lax.rem(me + shift, group), rows), :]
            for at, (start, stop) in enumerate(backs):
                back_refs[(shift - 1) * len(backs) + at][j] = piece[start:stop]


def mix(ids, moves, parts, weights, tokens, upstream, held, span, group, local, cut, relative, term, backs):
    tok = tokens.shape[0]
    blk = tokens.shape[1] // local
    feat = blk // group
    per = feat // local
    first, last = span
    rows = blk // sum(len(slots) for slots in cut)
    step = math.gcd(2, math.gcd(first, last))
    lane = pl.BlockSpec((tok, step * blk), lambda j, _: (0, first // step + j))
    at = pl.BlockSpec((step, feat, tok), lambda j, _: (first // step + j, 0, 0))
    keys = ["mixed", "own"]
    outs = [(tokens.shape, BF16, lane), ((local, feat, tok), BF16, at)]
    term_key, (term_first, term_last) = term
    for place, slots in enumerate(cut):
        keys.append((term_key, place))
        outs.append(
            (
                (len(slots), term_last - term_first, rows, blk),
                F32 if place == 0 else BF16,
                pl.BlockSpec((len(slots), step, rows, blk), lambda j, _: (0, (first - term_first) // step + j, 0, 0)),
            )
        )
    for shift in range(1, group):
        for key, (b_first, b_last), (j_first, j_last) in backs:
            keys.append((key, shift))
            outs.append(
                (
                    (j_last - j_first, (b_last - b_first) * per, tok),
                    BF16,
                    pl.BlockSpec(
                        (step, (b_last - b_first) * per, tok),
                        functools.partial(lambda start, j, _: (start + j, 0, 0), (first - j_first) // step),
                    ),
                )
            )
    kept = {place: held[key] for place, key in enumerate(keys) if key in held}
    cuts = [(b_first * per, b_last * per) for _, (b_first, b_last), _ in backs]
    got = call(
        functools.partial(
            mix_kernel, weights, cut, relative, group, local * group, cuts,
            [(lo * per, hi * per) for lo, hi in parts],
        ),
        "mix",
        ids,
        ((last - first) // step,),
        [
            (
                array,
                pl.BlockSpec(
                    (step,) + array.shape[1:],
                    functools.partial(lambda start, j, _: (start + j, 0, 0), (first - begin) // step),
                ),
            )
            for array, begin in moves
        ]
        + weights.specs(step, lambda j: first // step + j)
        + [(tokens, lane), (upstream, lane)],
        kept,
        outs,
        [
            pltpu.VMEM((step, blk, tok), BF16),
            pltpu.VMEM((step, blk, tok), BF16),
            pltpu.VMEM((step, blk, blk), BF16),
            pltpu.VMEM((step, blk, blk), F32),
        ],
    )
    held.update(zip(keys, got))


def fold_kernel(weights, cut, relative, group, inner, pieces, ids, own_ref, *rest):
    arrived, rest = rest[: pieces * (group - 1)], rest[pieces * (group - 1) :]
    x_ref, up_ref = rest[:2]
    rest = rest[2:]
    w_refs, rest = rest[: len(weights.arrays)], rest[len(weights.arrays) :]
    out_ref, term_refs = rest[0], rest[1:-3]
    inner_grad, held, term = rest[-3:]
    me = ids[0]
    blk = held.shape[2]
    width = blk // group
    for shift in range(group):
        if shift == 0:
            piece = own_ref[...]
        else:
            refs = arrived[(shift - 1) * pieces : shift * pieces]
            piece = jnp.concatenate([ref[...] for ref in refs], axis=0)
        piece = piece.astype(F32)
        source = lax.rem(me - shift + group, group)
        for half in range(2):
            part = piece[:, half * inner : (half + 1) * inner].reshape(width, -1)
            inner_grad[half, aligned(source, width), :] = part.astype(BF16)
    for half in range(2):
        cols = slice(half * blk, (half + 1) * blk)
        weight = weights.load(w_refs, half, held.at[half], ids[1])
        du = inner_grad[half]
        store_term(dot(du, x_ref[:, cols], 1, 0).T, cut, relative, term_refs, term.at[half], ids[1], half)
        back = dot(du.T, weight, 1, 1)
        out_ref[:, cols] = (up_ref[:, cols].astype(F32) + back).astype(BF16)


def fold(ids, own, arrived, tokens, upstream, weights, grad_tokens, span, group, local, cut, relative, after):
    tok = tokens.shape[0]
    blk = tokens.shape[1] // local
    inner = blk // (local * group)
    first, last = span
    rows = blk // sum(len(slots) for slots in cut)
    start = first // 2
    lane = pl.BlockSpec((tok, 2 * blk), lambda pair, _: (0, start + pair))
    inputs = []
    for array, begin in [(own, 0)] + arrived:
        at = functools.partial(lambda skip, pair, _: (0, skip + pair, 0), start - begin // 2)
        inputs.append((array, pl.BlockSpec((array.shape[0], 2 * inner, tok), at)))
    inputs += [(tokens, lane), (upstream, lane)]
    inputs += weights.specs(2, lambda pair: start + pair)
    outs = [(tokens.shape, BF16, lane)] + [
        (
            (len(slots), last - first, rows, blk),
            F32 if place == 0 else BF16,
            pl.BlockSpec((len(slots), 2, rows, blk), lambda pair, _: (0, pair, 0, 0)),
        )
        for place, slots in enumerate(cut)
    ]
    pieces = len(arrived) // (group - 1)
    held = {} if grad_tokens is None else {0: grad_tokens}
    return call(
        functools.partial(fold_kernel, weights, cut, relative, group, inner, pieces),
        "fold",
        ids,
        ((last - first) // 2,),
        inputs,
        held,
        outs,
        [
            pltpu.VMEM((2, blk, tok), BF16),
            pltpu.VMEM((2, blk, blk), BF16),
            pltpu.VMEM((2, blk, blk), F32),
        ],
        after,
    )


def send(array, shift, group):
    return lax.ppermute(array, "mp", [(at, (at + shift) % group) for at in range(group)])


def gather_plain(shard):
    local, rows, blk = shard.shape
    whole = lax.all_gather(shard, "dp", axis=0, tiled=False)
    if rows % 16:
        whole = jnp.transpose(whole, (1, 0, 2, 3)).reshape(1, local, whole.shape[0] * rows, blk)
    return Whole([whole], [list(range(whole.shape[0]))], False)


def scatter_plain(term, rows, scale):
    if term.shape[2] != rows:
        _, count, whole, blk = term.shape
        term = jnp.transpose(term.reshape(count, whole // rows, rows, blk), (1, 0, 2, 3))
    return lax.psum_scatter(term, "dp", scatter_dimension=0, tiled=False) * scale


def on_device(tokens, upstream, first_factor, second_factor):
    local, rows, blk = first_factor.shape
    group, size = lax.axis_size("mp"), lax.axis_size("dp")
    width = blk // group
    scale = 1.0 / math.sqrt(tokens.shape[0] * size)
    me, device = lax.axis_index("mp"), lax.axis_index("dp")
    ids = jnp.stack([me, device]).astype(jnp.int32)
    cube = group == 2 and size >= 8 and size & (size - 1) == 0 and rows % 16 == 0 and local % 16 == 0
    net = Network(size) if cube else None
    cut = net.first_cut() if cube else [[0]]
    plain_cut = [list(range(size))] if cube else [[0]]
    j_spans = split_by(local, (3, 3, 2)) if cube else [(0, local)]
    parts = split_by(local, (3, 5)) if cube else [(0, local)]
    b_spans = split_by(local, (3, 3, 2)) if cube else [(0, local)]
    shifts = list(range(1, group))

    second_whole = gather_plain(second_factor)
    firsts = []
    if cube:
        for lo, hi in parts:
            shard = first_factor[lo:hi]
            if firsts:
                shard, _ = lax.optimization_barrier((shard, brought))
            brought, slots = net.gather_first(shard)
            firsts.append(net.gather_rest((brought, slots), lo, firsts[-1].arrays[-1] if firsts else None))
    else:
        whole = gather_plain(first_factor).arrays[0]
        if whole.shape[0] > 1:
            whole = jnp.transpose(whole, (1, 0, 2, 3)).reshape(1, local, blk, blk)
        firsts = [Whole([whole], [[0]], False) for _ in parts]
    owns, arrived = [], []
    for place, (part, weights) in enumerate(zip(parts, firsts)):
        spans = j_spans if place + 1 == len(parts) else [(0, local)]
        own, *sends = expand(ids, tokens, weights, part, spans, group, local)
        owns.append(own)
        got = [send(piece, shift, group) for shift in shifts for piece in sends[(shift - 1) * len(spans) : shift * len(spans)]]
        arrived.append({(shift, span): got[(shift - 1) * len(spans) + at] for shift in shifts for at, span in enumerate(spans)})

    held = {}
    backs = [(("back", place), b_span, (0, local)) for place, b_span in enumerate(b_spans)]
    for at, span in enumerate(j_spans):
        moves = [(own, 0) for own in owns]
        for shift in shifts:
            for pieces in arrived:
                key = [known for known in pieces if known[0] == shift and known[1][0] <= span[0] and span[1] <= known[1][1]][0]
                moves.append((pieces[key], key[1][0]))
        mix(
            ids, moves, parts, second_whole, tokens, upstream, held, span, group, local, cut, cube,
            ("term", (0, local)), backs,
        )
    returned = [[send(held[(key, shift)], shift, group) for shift in shifts] for key, _, _ in backs]
    sums = [held[("term", place)] for place in range(len(cut))]
    if cube:
        grad_second, marks = net.scatter(sums, scale)
    else:
        grad_second, marks = scatter_plain(sums[0], rows, scale), []

    grad_tokens, sums, terms, chains = None, [], [], [marks]
    tie = lambda place: [array for chain, step in TIES.get(place, ()) if cube for array in chains[chain][step]]
    for place, b_span in enumerate(b_spans):
        grad_tokens, *pieces = fold(
            ids, held["own"], [(array, b_span[0]) for array in returned[place]], tokens, upstream,
            [weights for part, weights in zip(parts, firsts) if part[0] <= b_span[0] < part[1]][0],
            grad_tokens, b_span, group, local, cut, cube, tie(place),
        )
        if cube:
            total, marks = net.scatter(pieces, scale)
            chains.append(marks)
            sums.append(total)
        else:
            terms.append(pieces[0])
    if not cube:
        sums = [scatter_plain(jnp.concatenate(terms, axis=1), rows, scale)]
    return held["mixed"], grad_tokens, jnp.concatenate(sums), grad_second


def solution(mesh):
    placed = (P("dp", "mp"), P("dp", "mp"), P("mp", "dp", None), P("mp", "dp", None))
    return jax.shard_map(
        on_device, mesh=mesh, in_specs=placed, out_specs=placed, check_vma=False
    )
```

```python
import functools
import math

import jax
import jax.numpy as jnp
from jax import lax
from jax.experimental import pallas as pl
from jax.experimental.pallas import tpu as pltpu
from jax.sharding import PartitionSpec as P

BF16 = jnp.bfloat16
F32 = jnp.float32
ROOT_HALF = math.sqrt(0.5)
DENSITY = 1.0 / math.sqrt(2.0 * math.pi)
TIES = {0: ((0, 1),), 1: ((1, 1),), 2: ((0, 2), (2, 1))}
VMEM = 20 * 1024 * 1024
LARGE = 1 << 20


def split_even(count, parts):
    parts = min(count, parts)
    edges = [count * step // parts for step in range(parts + 1)]
    return list(zip(edges[:-1], edges[1:]))


def split_by(count, weights):
    total, edges, run = sum(weights), [0], 0
    for weight in weights:
        run += weight
        edges.append(count * run // total)
    return [(lo, hi) for lo, hi in zip(edges[:-1], edges[1:]) if hi > lo]


def dot(left, right, left_dim, right_dim):
    return lax.dot_general(
        left, right, (((left_dim,), (right_dim,)), ((), ())), preferred_element_type=F32
    )


def aligned(index, size):
    return pl.ds(pl.multiple_of(index * size, size), size)


def far_off(array):
    return pltpu.with_memory_space_constraint(array, pltpu.HBM)


def call(kernel, name, ids, grid, inputs, held, outputs, scratch=(), after=()):
    places = sorted(held)
    extra = [held[place] for place in places] + list(after)
    taken = len(inputs)

    def body(ids_ref, *refs):
        kernel(ids_ref, *refs[:taken], *refs[taken + len(extra) :])

    return pl.pallas_call(
        body,
        grid_spec=pltpu.PrefetchScalarGridSpec(
            num_scalar_prefetch=1,
            grid=grid,
            in_specs=[spec for _, spec in inputs] + [pl.BlockSpec(memory_space=pl.ANY)] * len(extra),
            out_specs=[spec for _, _, spec in outputs],
            scratch_shapes=list(scratch),
        ),
        out_shape=[jax.ShapeDtypeStruct(shape, dtype) for shape, dtype, _ in outputs],
        input_output_aliases={1 + taken + at: place for at, place in enumerate(places)},
        compiler_params=pltpu.CompilerParams(
            dimension_semantics=("arbitrary",) * len(grid), vmem_limit_bytes=VMEM
        ),
        cost_estimate=pl.CostEstimate(flops=1, bytes_accessed=1, transcendentals=0),
        name=name,
    )(ids, *[far_off(array) if array.ndim != 3 and array.size > LARGE else array for array, _ in inputs], *extra)


class Whole:
    def __init__(self, arrays, slots, relative, lanes=None):
        self.arrays, self.slots, self.relative = arrays, slots, relative
        self.cols, self.lane = lanes or (arrays[0].shape[3], 0)

    def specs(self, count, at):
        return [
            (
                array,
                pl.BlockSpec(
                    (array.shape[0], count, array.shape[2], self.cols),
                    lambda step, _: (0, at(step), 0, self.lane),
                ),
            )
            for array in self.arrays
        ]

    def load(self, refs, block, target, device):
        if not self.relative:
            return refs[0][:, block].reshape(target.shape)
        for ref, slots in zip(refs, self.slots):
            rows = ref.shape[2]
            for place, slot in enumerate(slots):
                target[aligned(lax.bitwise_xor(device, slot), rows), :] = ref[place, block]
        return target[...]


def combos(bits):
    found = [0]
    for bit in bits:
        found += [value | bit for value in found]
    return found


class Network:
    def __init__(self, size):
        bits = [1 << k for k in range(size.bit_length() - 1)]
        self.size = size
        self.near, self.far = bits[:2], bits[2:]
        self.rounds = [(bit,) for bit in bits]
        self.order = [0]
        for bits in reversed(self.rounds):
            self.order = [slot | mask for mask in combos(bits) for slot in self.order]

    def swap(self, array, mask):
        return lax.ppermute(array, "dp", [(at, at ^ mask) for at in range(self.size)])

    def gather(self, shard):
        combo = combos(self.far)
        first = [shard[None]] + [self.swap(shard[None], mask) for mask in combo[1:]]
        have = [(jnp.concatenate(first, axis=0), combo)]
        for mask in reversed(self.near):
            have = have + [(self.swap(array, mask), [slot | mask for slot in slots]) for array, slots in have]
        return Whole([array for array, _ in have], [slots for _, slots in have], True)

    def cut(self, slots, step):
        bits = self.rounds[step]
        mask = sum(bits)
        return [[slot for slot in slots if slot & mask == value] for value in combos(bits)]

    def first_cut(self):
        return self.cut(self.order, 0)

    def scatter(self, parts, scale):
        slots = self.first_cut()[0]
        total, sends, marks = parts[0], parts[1:], []
        for step, bits in enumerate(self.rounds):
            marks.append(sends)
            got = [self.swap(piece, mask) for piece, mask in zip(sends, combos(bits)[1:])]
            for piece in got:
                total = total + piece.astype(F32)
            if step + 1 < len(self.rounds):
                lists = self.cut(slots, step + 1)
                spans = [(slots.index(members[0]), slots.index(members[-1]) + 1) for members in lists]
                sends = [total[lo:hi].astype(BF16) for lo, hi in spans[1:]]
                total = total[spans[0][0] : spans[0][1]]
                slots = lists[0]
        result = total[0] * scale
        return result, marks + [[result]]


def expand_kernel(weights, shifts, spans, group, inner, ids, x_ref, *rest):
    w_refs, rest = rest[: len(weights.arrays)], rest[len(weights.arrays) :]
    outs, held = rest[:-1], rest[-1]
    blk = held.shape[1]
    halves = []
    for half in range(2):
        weight = weights.load(w_refs, half, held.at[half], ids[1])
        acts = x_ref[:, half * blk : (half + 1) * blk]
        halves.append(dot(acts, weight, 1, 0).astype(BF16).T.astype(F32))
    width = blk // group
    for at, _ in enumerate(shifts):
        parts = [
            full[at * width : (at + 1) * width].reshape(width // inner, inner, -1) for full in halves
        ]
        piece = jnp.concatenate(parts, axis=1).astype(BF16)
        for place, (start, stop) in enumerate(spans):
            outs[at * len(spans) + place][...] = piece[start:stop]


def expand(ids, tokens, weights, shifts, spans, group, local, after=()):
    tok = tokens.shape[0]
    blk = tokens.shape[1] // local
    inner = blk // (local * group)
    cols = len(shifts) * (blk // group)
    shapes = [stop - start for _ in shifts for start, stop in spans]
    return call(
        functools.partial(expand_kernel, weights, shifts, spans, group, inner),
        "expand",
        ids,
        (local // 2,),
        [(tokens, pl.BlockSpec((tok, 2 * blk), lambda pair, _: (0, pair)))]
        + weights.specs(2, lambda pair: pair),
        {},
        [
            (
                (count, local * inner, tok),
                BF16,
                pl.BlockSpec((count, 2 * inner, tok), lambda pair, _: (0, pair, 0)),
            )
            for count in shapes
        ],
        [pltpu.VMEM((2, blk, cols), BF16)],
        after,
    )


def order_matrix(blk, blocks, flip):
    inner = blk // blocks
    out = lax.broadcasted_iota(jnp.int32, (blk, blk), 1 if flip else 0)
    held = lax.broadcasted_iota(jnp.int32, (blk, blk), 0 if flip else 1)
    return (held == lax.rem(out, blocks) * inner + lax.div(out, blocks)).astype(F32).astype(BF16)


def store_term(term, slots_lists, relative, outs, scratch, device, block):
    if not relative:
        out = outs[0]
        out[:, block] = term.reshape(out.shape[0], out.shape[2], out.shape[3])
        return
    scratch[...] = term
    for out, slots in zip(outs, slots_lists):
        rows = out.shape[2]
        for place, slot in enumerate(slots):
            out[place, block] = scratch[aligned(lax.bitwise_xor(device, slot), rows), :].astype(out.dtype)


def mix_kernel(weights, cut, relative, group, blocks, backs, ids, own_ref, *rest):
    arrived, rest = rest[: group - 1], rest[group - 1 :]
    w_refs, rest = rest[: len(weights.arrays)], rest[len(weights.arrays) :]
    x_ref, up_ref = rest[:2]
    rest = rest[2:]
    mixed_ref, back_own_ref = rest[:2]
    term_refs, rest = rest[2 : 2 + len(cut)], rest[2 + len(cut) :]
    back_refs, (moved, back, held, term) = rest[:-4], rest[-4:]
    me = ids[0]
    blk = held.shape[1]
    rows = blk // group
    there = order_matrix(blk, blocks, False)
    again = order_matrix(blk, blocks, True)
    for j in range(held.shape[0]):
        cols = slice(j * blk, (j + 1) * blk)
        moved[j, aligned(me, rows), :] = own_ref[j]
        for shift in range(1, group):
            moved[j, aligned(lax.rem(me - shift + group, group), rows), :] = arrived[shift - 1][j]
        weight = weights.load(w_refs, j, held.at[j], ids[1])
        ordered = dot(there, moved[j], 1, 0).astype(BF16)
        inner_out = dot(ordered.T, weight, 1, 0)
        cdf = 0.5 + 0.5 * lax.erf(inner_out * ROOT_HALF)
        mixed_ref[:, cols] = (x_ref[:, cols].astype(F32) + inner_out * cdf).astype(BF16)
        slope = cdf + inner_out * (DENSITY * jnp.exp(-0.5 * inner_out * inner_out))
        grad_out = (up_ref[:, cols].astype(F32) * slope).astype(BF16)
        store_term(dot(ordered, grad_out, 1, 0), cut, relative, term_refs, term.at[j], ids[1], j)
        returned = dot(weight, grad_out, 1, 1).astype(BF16)
        back[j] = dot(again, returned, 1, 0).astype(BF16)
        back_own_ref[j] = back[j, aligned(me, rows), :]
        for shift in range(1, group):
            piece = back[j, aligned(lax.rem(me + shift, group), rows), :]
            for at, (start, stop) in enumerate(backs):
                back_refs[(shift - 1) * len(backs) + at][j] = piece[start:stop]


def mix(ids, own, arrived, weights, tokens, upstream, held, span, group, local, cut, relative, term, backs):
    tok = tokens.shape[0]
    blk = tokens.shape[1] // local
    feat = blk // group
    per = feat // local
    first, last = span
    rows = blk // sum(len(slots) for slots in cut)
    step = math.gcd(2, math.gcd(first, last))
    lane = pl.BlockSpec((tok, step * blk), lambda j, _: (0, first // step + j))
    at = pl.BlockSpec((step, feat, tok), lambda j, _: (first // step + j, 0, 0))
    keys = ["mixed", "own"]
    outs = [(tokens.shape, BF16, lane), ((local, feat, tok), BF16, at)]
    term_key, (term_first, term_last) = term
    for place, slots in enumerate(cut):
        keys.append((term_key, place))
        outs.append(
            (
                (len(slots), term_last - term_first, rows, blk),
                F32 if place == 0 else BF16,
                pl.BlockSpec((len(slots), step, rows, blk), lambda j, _: (0, (first - term_first) // step + j, 0, 0)),
            )
        )
    for shift in range(1, group):
        for key, (b_first, b_last), (j_first, j_last) in backs:
            keys.append((key, shift))
            outs.append(
                (
                    (j_last - j_first, (b_last - b_first) * per, tok),
                    BF16,
                    pl.BlockSpec(
                        (step, (b_last - b_first) * per, tok),
                        functools.partial(lambda start, j, _: (start + j, 0, 0), (first - j_first) // step),
                    ),
                )
            )
    kept = {place: held[key] for place, key in enumerate(keys) if key in held}
    cuts = [(b_first * per, b_last * per) for _, (b_first, b_last), _ in backs]
    got = call(
        functools.partial(mix_kernel, weights, cut, relative, group, local * group, cuts),
        "mix",
        ids,
        ((last - first) // step,),
        [(own, at)]
        + [(array, pl.BlockSpec((step, feat, tok), lambda j, _: (j, 0, 0))) for array in arrived]
        + weights.specs(step, lambda j: first // step + j)
        + [(tokens, lane), (upstream, lane)],
        kept,
        outs,
        [
            pltpu.VMEM((step, blk, tok), BF16),
            pltpu.VMEM((step, blk, tok), BF16),
            pltpu.VMEM((step, blk, blk), BF16),
            pltpu.VMEM((step, blk, blk), F32),
        ],
    )
    held.update(zip(keys, got))


def fold_kernel(columns, cut, relative, group, inner, pieces, ids, own_ref, *rest):
    arrived, rest = rest[: pieces * (group - 1)], rest[pieces * (group - 1) :]
    x_ref, up_ref = rest[:2]
    rest = rest[2:]
    w_refs = []
    for weights in columns:
        w_refs.append(rest[: len(weights.arrays)])
        rest = rest[len(weights.arrays) :]
    out_ref, term_refs = rest[0], rest[1:-4]
    inner_grad, held, sorted_term, term = rest[-4:]
    me = ids[0]
    blk = held.shape[2]
    width = blk // group
    for shift in range(group):
        if shift == 0:
            piece = own_ref[...]
        else:
            refs = arrived[(shift - 1) * pieces : shift * pieces]
            piece = jnp.concatenate([ref[...] for ref in refs], axis=0)
        piece = piece.astype(F32)
        for half in range(2):
            part = piece[:, half * inner : (half + 1) * inner].reshape(width, -1)
            inner_grad[half, shift * width : (shift + 1) * width, :] = part.astype(BF16)
    for half in range(2):
        cols = slice(half * blk, (half + 1) * blk)
        if len(columns) == 1:
            weight = columns[0].load(w_refs[0], half, held.at[half], ids[1])
        else:
            start = 0
            for weights, refs in zip(columns, w_refs):
                size = weights.cols
                part = held.at[half, :, start : start + size]
                part[...] = weights.load(refs, half, part, ids[1])
                start += size
            weight = held[half]
        du = inner_grad[half]
        unsorted = dot(du, x_ref[:, cols], 1, 0)
        for shift in range(group):
            source = lax.rem(me - shift + group, group)
            sorted_term[half, aligned(source, width), :] = unsorted[shift * width : (shift + 1) * width]
        store_term(sorted_term[half].T, cut, relative, term_refs, term.at[half], ids[1], half)
        back = dot(du.T, weight, 1, 1)
        out_ref[:, cols] = (up_ref[:, cols].astype(F32) + back).astype(BF16)


def fold(ids, own, arrived, tokens, upstream, columns, grad_tokens, span, group, local, cut, relative, after):
    tok = tokens.shape[0]
    blk = tokens.shape[1] // local
    inner = blk // (local * group)
    first, last = span
    rows = blk // sum(len(slots) for slots in cut)
    start = first // 2
    lane = pl.BlockSpec((tok, 2 * blk), lambda pair, _: (0, start + pair))
    inputs = []
    for array, begin in [(own, 0)] + arrived:
        at = functools.partial(lambda skip, pair, _: (0, skip + pair, 0), start - begin // 2)
        inputs.append((array, pl.BlockSpec((array.shape[0], 2 * inner, tok), at)))
    inputs += [(tokens, lane), (upstream, lane)]
    for weights in columns:
        inputs += weights.specs(2, lambda pair: start + pair)
    outs = [(tokens.shape, BF16, lane)] + [
        (
            (len(slots), last - first, rows, blk),
            F32 if place == 0 else BF16,
            pl.BlockSpec((len(slots), 2, rows, blk), lambda pair, _: (0, pair, 0, 0)),
        )
        for place, slots in enumerate(cut)
    ]
    pieces = len(arrived) // (group - 1)
    held = {} if grad_tokens is None else {0: grad_tokens}
    return call(
        functools.partial(fold_kernel, columns, cut, relative, group, inner, pieces),
        "fold",
        ids,
        ((last - first) // 2,),
        inputs,
        held,
        outs,
        [
            pltpu.VMEM((2, blk, tok), BF16),
            pltpu.VMEM((2, blk, blk), BF16),
            pltpu.VMEM((2, blk, blk), F32),
            pltpu.VMEM((2, blk, blk), F32),
        ],
        after,
    )


def send(array, shift, group):
    return lax.ppermute(array, "mp", [(at, (at + shift) % group) for at in range(group)])


def gather_plain(shard):
    local, rows, blk = shard.shape
    whole = lax.all_gather(shard, "dp", axis=0, tiled=False)
    if rows % 16:
        whole = jnp.transpose(whole, (1, 0, 2, 3)).reshape(1, local, whole.shape[0] * rows, blk)
    return Whole([whole], [list(range(whole.shape[0]))], False)


def scatter_plain(term, rows, scale):
    if term.shape[2] != rows:
        _, count, whole, blk = term.shape
        term = jnp.transpose(term.reshape(count, whole // rows, rows, blk), (1, 0, 2, 3))
    return lax.psum_scatter(term, "dp", scatter_dimension=0, tiled=False) * scale


def on_device(tokens, upstream, first_factor, second_factor):
    local, rows, blk = first_factor.shape
    group, size = lax.axis_size("mp"), lax.axis_size("dp")
    width = blk // group
    scale = 1.0 / math.sqrt(tokens.shape[0] * size)
    me, device = lax.axis_index("mp"), lax.axis_index("dp")
    ids = jnp.stack([me, device]).astype(jnp.int32)
    cube = group == 2 and size >= 8 and size & (size - 1) == 0 and rows % 16 == 0 and width % 128 == 0
    net = Network(size) if cube else None
    cut = net.first_cut() if cube else [[0]]
    plain_cut = [list(range(size))] if cube else [[0]]
    j_spans = split_by(local, (3, 3, 2)) if cube else split_even(local, 4)
    b_spans = [(2 * lo, 2 * hi) for lo, hi in split_by(local // 2, (4, 3, 1))]
    shifts = list(range(1, group))

    if cube:
        cols = [
            lax.dynamic_slice_in_dim(first_factor, lax.rem(me + shift, group) * width, width, 2)
            for shift in range(2)
        ]
        far = net.gather(cols[1])
        both = gather_plain(jnp.concatenate([second_factor, cols[0]], axis=2))
        second_whole = Whole(both.arrays, both.slots, False, (blk, 0))
        near = Whole(both.arrays, both.slots, False, (width, group))
        columns = [near, far]
    else:
        second_whole = gather_plain(second_factor)
        whole = gather_plain(first_factor).arrays[0]
        if whole.shape[0] > 1:
            whole = jnp.transpose(whole, (1, 0, 2, 3)).reshape(1, local, blk, blk)
        turned = jnp.roll(whole, -me * width, axis=3)
        near, far, turned = [
            Whole([array], [[0]], False) for array in (turned[..., :width], turned[..., width:], turned)
        ]
        columns = [turned]
    sends = expand(ids, tokens, far, shifts, j_spans, group, local)
    arrived = [
        [send(sends[(shift - 1) * len(j_spans) + at], shift, group) for shift in shifts]
        for at in range(len(j_spans))
    ]
    own = expand(ids, tokens, near, [0], [(0, local)], group, local)[0]

    held = {}
    backs = [(("back", place), b_span, (0, local)) for place, b_span in enumerate(b_spans)]
    for at, span in enumerate(j_spans):
        mix(
            ids, own, arrived[at], second_whole, tokens, upstream, held, span, group, local, cut, cube,
            ("term", (0, local)), backs,
        )
    returned = [[send(held[(key, shift)], shift, group) for shift in shifts] for key, _, _ in backs]
    parts = [held[("term", place)] for place in range(len(cut))]
    if cube:
        grad_second, marks = net.scatter(parts, scale)
    else:
        grad_second, marks = scatter_plain(parts[0], rows, scale), []

    grad_tokens, sums, terms, chains = None, [], [], [marks]
    tie = lambda place: [array for chain, step in TIES.get(place, ()) if cube for array in chains[chain][step]]
    for place, b_span in enumerate(b_spans):
        grad_tokens, *parts = fold(
            ids, held["own"], [(array, b_span[0]) for array in returned[place]], tokens, upstream, columns,
            grad_tokens, b_span, group, local, cut, cube, tie(place),
        )
        if cube:
            total, marks = net.scatter(parts, scale)
            chains.append(marks)
            sums.append(total)
        else:
            terms.append(parts[0])
    if not cube:
        sums = [scatter_plain(jnp.concatenate(terms, axis=1), rows, scale)]
    return held["mixed"], grad_tokens, jnp.concatenate(sums), grad_second


def solution(mesh):
    placed = (P("dp", "mp"), P("dp", "mp"), P("mp", "dp", None), P("mp", "dp", None))
    return jax.shard_map(
        on_device, mesh=mesh, in_specs=placed, out_specs=placed, check_vma=False
    )
```

```python
import functools
import math

import jax
import jax.numpy as jnp
from jax import lax
from jax.experimental import pallas as pl
from jax.experimental.pallas import tpu as pltpu
from jax.sharding import PartitionSpec as P

BF16 = jnp.bfloat16
F32 = jnp.float32
ROOT_HALF = math.sqrt(0.5)
DENSITY = 1.0 / math.sqrt(2.0 * math.pi)
TIES = {2: ((1, 2), (0, 2))}
VMEM = 20 * 1024 * 1024
LARGE = 1 << 20


def split_even(count, parts):
    parts = min(count, parts)
    edges = [count * step // parts for step in range(parts + 1)]
    return list(zip(edges[:-1], edges[1:]))


def split_by(count, weights):
    total, edges, run = sum(weights), [0], 0
    for weight in weights:
        run += weight
        edges.append(count * run // total)
    return [(lo, hi) for lo, hi in zip(edges[:-1], edges[1:]) if hi > lo]


def dot(left, right, left_dim, right_dim):
    return lax.dot_general(
        left, right, (((left_dim,), (right_dim,)), ((), ())), preferred_element_type=F32
    )


def aligned(index, size):
    return pl.ds(pl.multiple_of(index * size, size), size)


def far_off(array):
    return pltpu.with_memory_space_constraint(array, pltpu.HBM)


def call(kernel, name, ids, grid, inputs, held, outputs, scratch=(), after=()):
    places = sorted(held)
    extra = [held[place] for place in places] + list(after)
    taken = len(inputs)

    def body(ids_ref, *refs):
        kernel(ids_ref, *refs[:taken], *refs[taken + len(extra) :])

    return pl.pallas_call(
        body,
        grid_spec=pltpu.PrefetchScalarGridSpec(
            num_scalar_prefetch=1,
            grid=grid,
            in_specs=[spec for _, spec in inputs] + [pl.BlockSpec(memory_space=pl.ANY)] * len(extra),
            out_specs=[spec for _, _, spec in outputs],
            scratch_shapes=list(scratch),
        ),
        out_shape=[jax.ShapeDtypeStruct(shape, dtype) for shape, dtype, _ in outputs],
        input_output_aliases={1 + taken + at: place for at, place in enumerate(places)},
        compiler_params=pltpu.CompilerParams(
            dimension_semantics=("arbitrary",) * len(grid), vmem_limit_bytes=VMEM
        ),
        cost_estimate=pl.CostEstimate(flops=1, bytes_accessed=1, transcendentals=0),
        name=name,
    )(ids, *[far_off(array) if array.ndim != 3 and array.size > LARGE else array for array, _ in inputs], *extra)


class Whole:
    def __init__(self, arrays, slots, relative, lanes=None):
        self.arrays, self.slots, self.relative = arrays, slots, relative
        self.cols, self.lane = lanes or (arrays[0].shape[3], 0)

    def specs(self, count, at):
        return [
            (
                array,
                pl.BlockSpec(
                    (array.shape[0], count, array.shape[2], self.cols),
                    lambda step, _: (0, at(step), 0, self.lane),
                ),
            )
            for array in self.arrays
        ]

    def load(self, refs, block, target, device):
        if not self.relative:
            return refs[0][:, block].reshape(target.shape)
        for ref, slots in zip(refs, self.slots):
            rows = ref.shape[2]
            for place, slot in enumerate(slots):
                target[aligned(lax.bitwise_xor(device, slot), rows), :] = ref[place, block]
        return target[...]


def combos(bits):
    found = [0]
    for bit in bits:
        found += [value | bit for value in found]
    return found


class Network:
    def __init__(self, size):
        bits = [1 << k for k in range(size.bit_length() - 1)]
        self.size = size
        self.near, self.far = bits[:2], bits[2:]
        self.rounds = [(bit,) for bit in bits]
        self.order = [0]
        for bits in reversed(self.rounds):
            self.order = [slot | mask for mask in combos(bits) for slot in self.order]

    def swap(self, array, mask):
        return lax.ppermute(array, "dp", [(at, at ^ mask) for at in range(self.size)])

    def gather(self, shard):
        combo = combos(self.far)
        first = [shard[None]] + [self.swap(shard[None], mask) for mask in combo[1:]]
        have = [(jnp.concatenate(first, axis=0), combo)]
        for mask in reversed(self.near):
            have = have + [(self.swap(array, mask), [slot | mask for slot in slots]) for array, slots in have]
        return Whole([array for array, _ in have], [slots for _, slots in have], True)

    def cut(self, slots, step):
        bits = self.rounds[step]
        mask = sum(bits)
        return [[slot for slot in slots if slot & mask == value] for value in combos(bits)]

    def first_cut(self):
        return self.cut(self.order, 0)

    def scatter(self, parts, scale):
        slots = self.first_cut()[0]
        total, sends, marks = parts[0], parts[1:], []
        for step, bits in enumerate(self.rounds):
            marks.append(sends)
            got = [self.swap(piece, mask) for piece, mask in zip(sends, combos(bits)[1:])]
            for piece in got:
                total = total + piece.astype(F32)
            if step + 1 < len(self.rounds):
                lists = self.cut(slots, step + 1)
                spans = [(slots.index(members[0]), slots.index(members[-1]) + 1) for members in lists]
                sends = [total[lo:hi].astype(BF16) for lo, hi in spans[1:]]
                total = total[spans[0][0] : spans[0][1]]
                slots = lists[0]
        result = total[0] * scale
        return result, marks + [[result]]


def expand_kernel(weights, shifts, spans, group, inner, ids, x_ref, *rest):
    w_refs, rest = rest[: len(weights.arrays)], rest[len(weights.arrays) :]
    outs, held = rest[:-1], rest[-1]
    blk = held.shape[1]
    halves = []
    for half in range(2):
        weight = weights.load(w_refs, half, held.at[half], ids[1])
        acts = x_ref[:, half * blk : (half + 1) * blk]
        halves.append(dot(acts, weight, 1, 0).astype(BF16).T.astype(F32))
    width = blk // group
    for at, _ in enumerate(shifts):
        parts = [
            full[at * width : (at + 1) * width].reshape(width // inner, inner, -1) for full in halves
        ]
        piece = jnp.concatenate(parts, axis=1).astype(BF16)
        for place, (start, stop) in enumerate(spans):
            outs[at * len(spans) + place][...] = piece[start:stop]


def expand(ids, tokens, weights, shifts, spans, group, local, after=()):
    tok = tokens.shape[0]
    blk = tokens.shape[1] // local
    inner = blk // (local * group)
    cols = len(shifts) * (blk // group)
    shapes = [stop - start for _ in shifts for start, stop in spans]
    return call(
        functools.partial(expand_kernel, weights, shifts, spans, group, inner),
        "expand",
        ids,
        (local // 2,),
        [(tokens, pl.BlockSpec((tok, 2 * blk), lambda pair, _: (0, pair)))]
        + weights.specs(2, lambda pair: pair),
        {},
        [
            (
                (count, local * inner, tok),
                BF16,
                pl.BlockSpec((count, 2 * inner, tok), lambda pair, _: (0, pair, 0)),
            )
            for count in shapes
        ],
        [pltpu.VMEM((2, blk, cols), BF16)],
        after,
    )


def order_matrix(blk, blocks, flip):
    inner = blk // blocks
    out = lax.broadcasted_iota(jnp.int32, (blk, blk), 1 if flip else 0)
    held = lax.broadcasted_iota(jnp.int32, (blk, blk), 0 if flip else 1)
    return (held == lax.rem(out, blocks) * inner + lax.div(out, blocks)).astype(F32).astype(BF16)


def store_term(term, slots_lists, relative, outs, scratch, device, block):
    if not relative:
        out = outs[0]
        out[:, block] = term.reshape(out.shape[0], out.shape[2], out.shape[3])
        return
    scratch[...] = term
    for out, slots in zip(outs, slots_lists):
        rows = out.shape[2]
        for place, slot in enumerate(slots):
            out[place, block] = scratch[aligned(lax.bitwise_xor(device, slot), rows), :].astype(out.dtype)


def mix_kernel(weights, cut, relative, group, blocks, backs, ids, own_ref, *rest):
    arrived, rest = rest[: group - 1], rest[group - 1 :]
    w_refs, rest = rest[: len(weights.arrays)], rest[len(weights.arrays) :]
    x_ref, up_ref = rest[:2]
    rest = rest[2:]
    mixed_ref, back_own_ref = rest[:2]
    term_refs, rest = rest[2 : 2 + len(cut)], rest[2 + len(cut) :]
    back_refs, (moved, back, held, term) = rest[:-4], rest[-4:]
    me = ids[0]
    blk = held.shape[1]
    rows = blk // group
    there = order_matrix(blk, blocks, False)
    again = order_matrix(blk, blocks, True)
    for j in range(held.shape[0]):
        cols = slice(j * blk, (j + 1) * blk)
        moved[j, aligned(me, rows), :] = own_ref[j]
        for shift in range(1, group):
            moved[j, aligned(lax.rem(me - shift + group, group), rows), :] = arrived[shift - 1][j]
        weight = weights.load(w_refs, j, held.at[j], ids[1])
        ordered = dot(there, moved[j], 1, 0).astype(BF16)
        inner_out = dot(ordered.T, weight, 1, 0)
        cdf = 0.5 + 0.5 * lax.erf(inner_out * ROOT_HALF)
        mixed_ref[:, cols] = (x_ref[:, cols].astype(F32) + inner_out * cdf).astype(BF16)
        slope = cdf + inner_out * (DENSITY * jnp.exp(-0.5 * inner_out * inner_out))
        grad_out = (up_ref[:, cols].astype(F32) * slope).astype(BF16)
        store_term(dot(ordered, grad_out, 1, 0), cut, relative, term_refs, term.at[j], ids[1], j)
        returned = dot(weight, grad_out, 1, 1).astype(BF16)
        back[j] = dot(again, returned, 1, 0).astype(BF16)
        back_own_ref[j] = back[j, aligned(me, rows), :]
        for shift in range(1, group):
            piece = back[j, aligned(lax.rem(me + shift, group), rows), :]
            for at, (start, stop) in enumerate(backs):
                back_refs[(shift - 1) * len(backs) + at][j] = piece[start:stop]


def mix(ids, own, arrived, weights, tokens, upstream, held, span, group, local, cut, relative, term, backs):
    tok = tokens.shape[0]
    blk = tokens.shape[1] // local
    feat = blk // group
    per = feat // local
    first, last = span
    rows = blk // sum(len(slots) for slots in cut)
    step = math.gcd(2, math.gcd(first, last))
    lane = pl.BlockSpec((tok, step * blk), lambda j, _: (0, first // step + j))
    at = pl.BlockSpec((step, feat, tok), lambda j, _: (first // step + j, 0, 0))
    keys = ["mixed", "own"]
    outs = [(tokens.shape, BF16, lane), ((local, feat, tok), BF16, at)]
    term_key, (term_first, term_last) = term
    for place, slots in enumerate(cut):
        keys.append((term_key, place))
        outs.append(
            (
                (len(slots), term_last - term_first, rows, blk),
                F32 if place == 0 else BF16,
                pl.BlockSpec((len(slots), step, rows, blk), lambda j, _: (0, (first - term_first) // step + j, 0, 0)),
            )
        )
    for shift in range(1, group):
        for key, (b_first, b_last), (j_first, j_last) in backs:
            keys.append((key, shift))
            outs.append(
                (
                    (j_last - j_first, (b_last - b_first) * per, tok),
                    BF16,
                    pl.BlockSpec(
                        (step, (b_last - b_first) * per, tok),
                        functools.partial(lambda start, j, _: (start + j, 0, 0), (first - j_first) // step),
                    ),
                )
            )
    kept = {place: held[key] for place, key in enumerate(keys) if key in held}
    cuts = [(b_first * per, b_last * per) for _, (b_first, b_last), _ in backs]
    got = call(
        functools.partial(mix_kernel, weights, cut, relative, group, local * group, cuts),
        "mix",
        ids,
        ((last - first) // step,),
        [(own, at)]
        + [(array, pl.BlockSpec((step, feat, tok), lambda j, _: (j, 0, 0))) for array in arrived]
        + weights.specs(step, lambda j: first // step + j)
        + [(tokens, lane), (upstream, lane)],
        kept,
        outs,
        [
            pltpu.VMEM((step, blk, tok), BF16),
            pltpu.VMEM((step, blk, tok), BF16),
            pltpu.VMEM((step, blk, blk), BF16),
            pltpu.VMEM((step, blk, blk), F32),
        ],
    )
    held.update(zip(keys, got))


def fold_kernel(columns, cut, relative, group, inner, pieces, ids, own_ref, *rest):
    arrived, rest = rest[: pieces * (group - 1)], rest[pieces * (group - 1) :]
    x_ref, up_ref = rest[:2]
    rest = rest[2:]
    w_refs = []
    for weights in columns:
        w_refs.append(rest[: len(weights.arrays)])
        rest = rest[len(weights.arrays) :]
    out_ref, term_refs = rest[0], rest[1:-4]
    inner_grad, held, sorted_term, term = rest[-4:]
    me = ids[0]
    blk = held.shape[2]
    width = blk // group
    for shift in range(group):
        if shift == 0:
            piece = own_ref[...]
        else:
            refs = arrived[(shift - 1) * pieces : shift * pieces]
            piece = jnp.concatenate([ref[...] for ref in refs], axis=0)
        piece = piece.astype(F32)
        for half in range(2):
            part = piece[:, half * inner : (half + 1) * inner].reshape(width, -1)
            inner_grad[half, shift * width : (shift + 1) * width, :] = part.astype(BF16)
    for half in range(2):
        cols = slice(half * blk, (half + 1) * blk)
        if len(columns) == 1:
            weight = columns[0].load(w_refs[0], half, held.at[half], ids[1])
        else:
            start = 0
            for weights, refs in zip(columns, w_refs):
                size = weights.cols
                part = held.at[half, :, start : start + size]
                part[...] = weights.load(refs, half, part, ids[1])
                start += size
            weight = held[half]
        du = inner_grad[half]
        if cut:
            unsorted = dot(du, x_ref[:, cols], 1, 0)
            for shift in range(group):
                source = lax.rem(me - shift + group, group)
                sorted_term[half, aligned(source, width), :] = unsorted[shift * width : (shift + 1) * width]
            store_term(sorted_term[half].T, cut, relative, term_refs, term.at[half], ids[1], half)
        back = dot(du.T, weight, 1, 1)
        out_ref[:, cols] = (up_ref[:, cols].astype(F32) + back).astype(BF16)


def fold(ids, own, arrived, tokens, upstream, columns, begun, span, unit, room, group, local, cut, relative, after):
    tok = tokens.shape[0]
    blk = tokens.shape[1] // local
    inner = blk // (local * group)
    first, last = span
    rows = blk // sum(len(slots) for slots in cut) if cut else blk
    start = first // 2
    lane = pl.BlockSpec((tok, 2 * blk), lambda pair, _: (0, start + pair))
    inputs = []
    for array, begin in [(own, 0)] + arrived:
        at = functools.partial(lambda skip, pair, _: (0, skip + pair, 0), start - begin // 2)
        inputs.append((array, pl.BlockSpec((array.shape[0], 2 * inner, tok), at)))
    inputs += [(tokens, lane), (upstream, lane)]
    for weights in columns:
        inputs += weights.specs(2, lambda pair: start + pair)
    outs = [(tokens.shape, BF16, lane)] + [
        (
            (len(slots), room, rows, blk),
            F32 if place == 0 else BF16,
            pl.BlockSpec(
                (len(slots), 2, rows, blk), lambda pair, _: (0, (first - unit[0]) // 2 + pair, 0, 0)
            ),
        )
        for place, slots in enumerate(cut)
    ]
    pieces = len(arrived) // (group - 1)
    held = begun
    return call(
        functools.partial(fold_kernel, columns, cut, relative, group, inner, pieces),
        "fold",
        ids,
        ((last - first) // 2,),
        inputs,
        held,
        outs,
        [
            pltpu.VMEM((2, blk, tok), BF16),
            pltpu.VMEM((2, blk, blk), BF16),
            pltpu.VMEM((2, blk, blk), F32),
            pltpu.VMEM((2, blk, blk), F32),
        ],
        after,
    )


def side_kernel(cut, inner, ids, own_ref, back_ref, x_ref, far_x_ref, *rest):
    outs, term = rest[:-1], rest[-1]
    blk = term.shape[1]
    for half in range(2):
        found = []
        for ref, acts in ((own_ref, x_ref), (back_ref, far_x_ref)):
            grad = ref[...].astype(F32)[:, half * inner : (half + 1) * inner]
            grad = grad.reshape(-1, grad.shape[2]).astype(BF16)
            found.append(dot(grad, acts[:, half * blk : (half + 1) * blk], 1, 0))
        store_term(jnp.concatenate(found, axis=0).T, cut, True, outs, term.at[half], ids[1], half)


def side(ids, own, back, tokens, far_tokens, span, room, first_room, rows, local, group, cut, after):
    tok = tokens.shape[0]
    blk = tokens.shape[1] // local
    inner = blk // (local * group)
    first, last = span
    start = first // 2
    return call(
        functools.partial(side_kernel, cut, inner),
        "side",
        ids,
        ((last - first) // 2,),
        [
            (own, pl.BlockSpec((local, 2 * inner, tok), lambda pair, _: (0, start + pair, 0))),
            (back, pl.BlockSpec((local, 2 * inner, tok), lambda pair, _: (0, pair, 0))),
            (tokens, pl.BlockSpec((tok, 2 * blk), lambda pair, _: (0, start + pair))),
            (far_tokens, pl.BlockSpec((tok, 2 * blk), lambda pair, _: (0, pair))),
        ],
        {},
        [
            (
                (len(slots), room, rows, blk),
                F32 if place == 0 else BF16,
                pl.BlockSpec((len(slots), 2, rows, blk), lambda pair, _: (0, first_room // 2 + pair, 0, 0)),
            )
            for place, slots in enumerate(cut)
        ],
        [pltpu.VMEM((2, blk, blk), F32)],
        after=after,
    )


def send(array, shift, group):
    return lax.ppermute(array, "mp", [(at, (at + shift) % group) for at in range(group)])


def gather_plain(shard):
    local, rows, blk = shard.shape
    whole = lax.all_gather(shard, "dp", axis=0, tiled=False)
    if rows % 16:
        whole = jnp.transpose(whole, (1, 0, 2, 3)).reshape(1, local, whole.shape[0] * rows, blk)
    return Whole([whole], [list(range(whole.shape[0]))], False)


def scatter_plain(term, rows, scale):
    if term.shape[2] != rows:
        _, count, whole, blk = term.shape
        term = jnp.transpose(term.reshape(count, whole // rows, rows, blk), (1, 0, 2, 3))
    return lax.psum_scatter(term, "dp", scatter_dimension=0, tiled=False) * scale


def on_device(tokens, upstream, first_factor, second_factor):
    local, rows, blk = first_factor.shape
    group, size = lax.axis_size("mp"), lax.axis_size("dp")
    width = blk // group
    scale = 1.0 / math.sqrt(tokens.shape[0] * size)
    me, device = lax.axis_index("mp"), lax.axis_index("dp")
    ids = jnp.stack([me, device]).astype(jnp.int32)
    cube = group == 2 and size >= 8 and size & (size - 1) == 0 and rows % 16 == 0 and width % 128 == 0
    cube = cube and local % 16 == 0
    net = Network(size) if cube else None
    cut = net.first_cut() if cube else [[0]]
    plain_cut = [list(range(size))] if cube else [[0]]
    j_spans = split_by(local, (3, 3, 2)) if cube else split_even(local, 4)
    b_spans = split_by(local, (3, 1, 2, 2)) if cube else [(0, local)]
    units = [(0, b_spans[1][1]), b_spans[2]] if cube else []
    aside = b_spans[-1] if cube else (0, 0)
    extra = aside[1] - aside[0]
    shifts = list(range(1, group))

    if cube:
        cols = [
            lax.dynamic_slice_in_dim(first_factor, lax.rem(me + shift, group) * width, width, 2)
            for shift in range(2)
        ]
        far = net.gather(cols[1])
        both = gather_plain(jnp.concatenate([second_factor, cols[0]], axis=2))
        second_whole = Whole(both.arrays, both.slots, False, (blk, 0))
        near = Whole(both.arrays, both.slots, False, (width, group))
        columns = [near, far]
    else:
        second_whole = gather_plain(second_factor)
        whole = gather_plain(first_factor).arrays[0]
        if whole.shape[0] > 1:
            whole = jnp.transpose(whole, (1, 0, 2, 3)).reshape(1, local, blk, blk)
        turned = jnp.roll(whole, -me * width, axis=3)
        near, far, turned = [
            Whole([array], [[0]], False) for array in (turned[..., :width], turned[..., width:], turned)
        ]
        columns = [turned]
    early = []
    if cube:
        early = [send(tokens[:, aside[0] * blk : aside[1] * blk], 1, group)]
    sends = expand(ids, tokens, far, shifts, j_spans, group, local, early)
    arrived = [
        [send(sends[(shift - 1) * len(j_spans) + at], shift, group) for shift in shifts]
        for at in range(len(j_spans))
    ]
    own = expand(ids, tokens, near, [0], [(0, local)], group, local)[0]

    held = {}
    backs = [(("back", place), b_span, (0, local)) for place, b_span in enumerate(b_spans)]
    for at, span in enumerate(j_spans):
        mix(
            ids, own, arrived[at], second_whole, tokens, upstream, held, span, group, local, cut, cube,
            ("term", (0, local)), backs,
        )
    returned = [[send(held[(key, shift)], shift, group) for shift in shifts] for key, _, _ in backs[: len(backs) - cube]]
    parts = [held[("term", place)] for place in range(len(cut))]
    begun = {}
    if cube:
        grad_second, marks = net.scatter(parts, scale)
        last = len(b_spans) - 1
        count = units[0][1] - units[0][0]
        terms = side(
            ids, held["own"], held[(("back", last), 1)], tokens, early[0], aside, count + extra, count, rows,
            local, group, cut, marks[1],
        )
        begun = {place + 1: array for place, array in enumerate(terms)}
    else:
        grad_second, marks = scatter_plain(parts[0], rows, scale), []

    sums, chains = [], [marks]
    for place, b_span in enumerate(b_spans):
        unit = [known for known in units + [b_span] if known[0] <= b_span[0] and b_span[1] <= known[1]][0]
        room = unit[1] - unit[0] + (extra if unit[0] == 0 else 0)
        plain = cube and b_span == aside
        if plain:
            piece, _ = lax.optimization_barrier((held[(("back", place), 1)], chains[1][1]))
            returned.append([send(piece, 1, group)])
        after = [array for chain, step in TIES.get(place, ()) if cube for array in chains[chain][step]]
        got = fold(
            ids, held["own"], [(array, b_span[0]) for array in returned[place]], tokens, upstream, columns,
            begun, b_span, unit, room, group, local, [] if plain else cut, cube, after,
        )
        begun = dict(enumerate(got))
        if not plain and b_span[1] == unit[1]:
            if cube:
                total, marks = net.scatter(got[1:], scale)
                chains.append(marks)
            else:
                total = scatter_plain(got[1], rows, scale)
            sums.append(total)
            begun = {0: got[0]}
    if cube:
        sums[0], shared = sums[0][:count], sums[0][count:]
        mine, theirs = shared[..., :width], shared[..., width:]
        theirs = send(theirs, 1, group)
        sums.append(
            jnp.where(
                me == 0, jnp.concatenate([mine, theirs], axis=2), jnp.concatenate([theirs, mine], axis=2)
            )
        )
    return held["mixed"], got[0], jnp.concatenate(sums), grad_second


def solution(mesh):
    placed = (P("dp", "mp"), P("dp", "mp"), P("mp", "dp", None), P("mp", "dp", None))
    return jax.shard_map(
        on_device, mesh=mesh, in_specs=placed, out_specs=placed, check_vma=False
    )
```

```python
import functools
import math

import jax
import jax.numpy as jnp
from jax import lax
from jax.experimental import pallas as pl
from jax.experimental.pallas import tpu as pltpu
from jax.sharding import PartitionSpec as P

BF16 = jnp.bfloat16
F32 = jnp.float32
ROOT_HALF = math.sqrt(0.5)
DENSITY = 1.0 / math.sqrt(2.0 * math.pi)
TIES = {0: ((0, 1),), 1: ((1, 1),), 2: ((0, 3), (1, 2), (2, 1))}
VMEM = 20 * 1024 * 1024
LARGE = 1 << 20


def split_even(count, parts):
    parts = min(count, parts)
    edges = [count * step // parts for step in range(parts + 1)]
    return list(zip(edges[:-1], edges[1:]))


def split_by(count, weights):
    total, edges, run = sum(weights), [0], 0
    for weight in weights:
        run += weight
        edges.append(count * run // total)
    return [(lo, hi) for lo, hi in zip(edges[:-1], edges[1:]) if hi > lo]


def dot(left, right, left_dim, right_dim):
    return lax.dot_general(
        left, right, (((left_dim,), (right_dim,)), ((), ())), preferred_element_type=F32
    )


def aligned(index, size):
    return pl.ds(pl.multiple_of(index * size, size), size)


def placed_for(name, array):
    if array.ndim == 2:
        space = pltpu.VMEM if name == "expand" else pltpu.HBM
        return pltpu.with_memory_space_constraint(array, space)
    if array.ndim == 4 and array.size > LARGE:
        return pltpu.with_memory_space_constraint(array, pltpu.HBM)
    return array


def call(kernel, name, ids, grid, inputs, held, outputs, scratch=(), after=()):
    places = sorted(held)
    extra = [held[place] for place in places] + list(after)
    taken = len(inputs)

    def body(ids_ref, *refs):
        kernel(ids_ref, *refs[:taken], *refs[taken + len(extra) :])

    return pl.pallas_call(
        body,
        grid_spec=pltpu.PrefetchScalarGridSpec(
            num_scalar_prefetch=1,
            grid=grid,
            in_specs=[spec for _, spec in inputs] + [pl.BlockSpec(memory_space=pl.ANY)] * len(extra),
            out_specs=[spec for _, _, spec in outputs],
            scratch_shapes=list(scratch),
        ),
        out_shape=[jax.ShapeDtypeStruct(shape, dtype) for shape, dtype, _ in outputs],
        input_output_aliases={1 + taken + at: place for at, place in enumerate(places)},
        compiler_params=pltpu.CompilerParams(
            dimension_semantics=("arbitrary",) * len(grid), vmem_limit_bytes=VMEM
        ),
        cost_estimate=pl.CostEstimate(flops=1, bytes_accessed=1, transcendentals=0),
        name=name,
    )(ids, *[placed_for(name, array) for array, _ in inputs], *extra)


class Whole:
    def __init__(self, arrays, slots, relative, lanes=None):
        self.arrays, self.slots, self.relative = arrays, slots, relative
        self.cols, self.lane = lanes or (arrays[0].shape[3], 0)

    def specs(self, count, at):
        return [
            (
                array,
                pl.BlockSpec(
                    (array.shape[0], count, array.shape[2], self.cols),
                    lambda step, _: (0, at(step), 0, self.lane),
                ),
            )
            for array in self.arrays
        ]

    def load(self, refs, block, target, device):
        if not self.relative:
            return refs[0][:, block].reshape(target.shape)
        for ref, slots in zip(refs, self.slots):
            rows = ref.shape[2]
            for place, slot in enumerate(slots):
                target[aligned(lax.bitwise_xor(device, slot), rows), :] = ref[place, block]
        return target[...]


def combos(bits):
    found = [0]
    for bit in bits:
        found += [value | bit for value in found]
    return found


class Network:
    def __init__(self, size):
        bits = [1 << k for k in range(size.bit_length() - 1)]
        self.size = size
        self.near, self.far = bits[:2], bits[2:]
        self.rounds = [(bit,) for bit in bits]
        self.order = [0]
        for bits in reversed(self.rounds):
            self.order = [slot | mask for mask in combos(bits) for slot in self.order]

    def swap(self, array, mask):
        return lax.ppermute(array, "dp", [(at, at ^ mask) for at in range(self.size)])

    def gather(self, shard):
        combo = combos(self.far)
        first = [shard[None]] + [self.swap(shard[None], mask) for mask in combo[1:]]
        have = [(jnp.concatenate(first, axis=0), combo)]
        for mask in reversed(self.near):
            have = have + [(self.swap(array, mask), [slot | mask for slot in slots]) for array, slots in have]
        return Whole([array for array, _ in have], [slots for _, slots in have], True)

    def cut(self, slots, step):
        bits = self.rounds[step]
        mask = sum(bits)
        return [[slot for slot in slots if slot & mask == value] for value in combos(bits)]

    def first_cut(self):
        return self.cut(self.order, 0)

    def scatter(self, parts, scale):
        slots = self.first_cut()[0]
        terms, sends, marks = [parts[0]], parts[1:], []
        for step, bits in enumerate(self.rounds):
            marks.append(sends)
            terms += [self.swap(piece, mask) for piece, mask in zip(sends, combos(bits)[1:])]
            if step + 1 < len(self.rounds):
                lists = self.cut(slots, step + 1)
                spans = [(slots.index(members[0]), slots.index(members[-1]) + 1) for members in lists]
                sends = [sum(term[lo:hi].astype(F32) for term in terms).astype(BF16) for lo, hi in spans[1:]]
                terms = [term[spans[0][0] : spans[0][1]] for term in terms]
                slots = lists[0]
        result = sum(term[0].astype(F32) for term in terms) * scale
        return result, marks + [[result]]


def expand_kernel(weights, shifts, spans, group, inner, ids, x_ref, *rest):
    w_refs, rest = rest[: len(weights.arrays)], rest[len(weights.arrays) :]
    outs, held = rest[:-1], rest[-1]
    blk = held.shape[1]
    halves = []
    for half in range(2):
        weight = weights.load(w_refs, half, held.at[half], ids[1])
        acts = x_ref[:, half * blk : (half + 1) * blk]
        halves.append(dot(acts, weight, 1, 0).astype(BF16).T.astype(F32))
    width = blk // group
    for at, _ in enumerate(shifts):
        parts = [
            full[at * width : (at + 1) * width].reshape(width // inner, inner, -1) for full in halves
        ]
        piece = jnp.concatenate(parts, axis=1).astype(BF16)
        for place, (start, stop) in enumerate(spans):
            outs[at * len(spans) + place][...] = piece[start:stop]


def expand(ids, tokens, weights, shifts, spans, group, local, after=()):
    tok = tokens.shape[0]
    blk = tokens.shape[1] // local
    inner = blk // (local * group)
    cols = len(shifts) * (blk // group)
    shapes = [stop - start for _ in shifts for start, stop in spans]
    return call(
        functools.partial(expand_kernel, weights, shifts, spans, group, inner),
        "expand",
        ids,
        (local // 2,),
        [(tokens, pl.BlockSpec((tok, 2 * blk), lambda pair, _: (0, pair)))]
        + weights.specs(2, lambda pair: pair),
        {},
        [
            (
                (count, local * inner, tok),
                BF16,
                pl.BlockSpec((count, 2 * inner, tok), lambda pair, _: (0, pair, 0)),
            )
            for count in shapes
        ],
        [pltpu.VMEM((2, blk, cols), BF16)],
        after,
    )


def order_matrix(blk, blocks, flip):
    inner = blk // blocks
    out = lax.broadcasted_iota(jnp.int32, (blk, blk), 1 if flip else 0)
    held = lax.broadcasted_iota(jnp.int32, (blk, blk), 0 if flip else 1)
    return (held == lax.rem(out, blocks) * inner + lax.div(out, blocks)).astype(F32).astype(BF16)


def store_term(term, slots_lists, relative, outs, scratch, device, block):
    if not relative:
        out = outs[0]
        out[:, block] = term.reshape(out.shape[0], out.shape[2], out.shape[3])
        return
    scratch[...] = term
    for out, slots in zip(outs, slots_lists):
        rows = out.shape[2]
        for place, slot in enumerate(slots):
            out[place, block] = scratch[aligned(lax.bitwise_xor(device, slot), rows), :].astype(out.dtype)


def mix_kernel(weights, cut, relative, group, blocks, backs, ids, own_ref, *rest):
    arrived, rest = rest[: group - 1], rest[group - 1 :]
    w_refs, rest = rest[: len(weights.arrays)], rest[len(weights.arrays) :]
    x_ref, up_ref = rest[:2]
    rest = rest[2:]
    mixed_ref, back_own_ref = rest[:2]
    term_refs, rest = rest[2 : 2 + len(cut)], rest[2 + len(cut) :]
    back_refs, (moved, back, held, term) = rest[:-4], rest[-4:]
    me = ids[0]
    blk = held.shape[1]
    rows = blk // group
    there = order_matrix(blk, blocks, False)
    again = order_matrix(blk, blocks, True)
    for j in range(held.shape[0]):
        cols = slice(j * blk, (j + 1) * blk)
        moved[j, aligned(me, rows), :] = own_ref[j]
        for shift in range(1, group):
            moved[j, aligned(lax.rem(me - shift + group, group), rows), :] = arrived[shift - 1][j]
        weight = weights.load(w_refs, j, held.at[j], ids[1])
        ordered = dot(there, moved[j], 1, 0).astype(BF16)
        inner_out = dot(ordered.T, weight, 1, 0)
        cdf = 0.5 + 0.5 * lax.erf(inner_out * ROOT_HALF)
        mixed_ref[:, cols] = (x_ref[:, cols].astype(F32) + inner_out * cdf).astype(BF16)
        slope = cdf + inner_out * (DENSITY * jnp.exp(-0.5 * inner_out * inner_out))
        grad_out = (up_ref[:, cols].astype(F32) * slope).astype(BF16)
        store_term(dot(ordered, grad_out, 1, 0), cut, relative, term_refs, term.at[j], ids[1], j)
        returned = dot(weight, grad_out, 1, 1).astype(BF16)
        back[j] = dot(again, returned, 1, 0).astype(BF16)
        back_own_ref[j] = back[j, aligned(me, rows), :]
        for shift in range(1, group):
            piece = back[j, aligned(lax.rem(me + shift, group), rows), :]
            for at, (start, stop) in enumerate(backs):
                back_refs[(shift - 1) * len(backs) + at][j] = piece[start:stop]


def mix(ids, own, arrived, weights, tokens, upstream, held, span, group, local, cut, relative, term, backs):
    tok = tokens.shape[0]
    blk = tokens.shape[1] // local
    feat = blk // group
    per = feat // local
    first, last = span
    rows = blk // sum(len(slots) for slots in cut)
    step = math.gcd(2, math.gcd(first, last))
    lane = pl.BlockSpec((tok, step * blk), lambda j, _: (0, first // step + j))
    at = pl.BlockSpec((step, feat, tok), lambda j, _: (first // step + j, 0, 0))
    keys = ["mixed", "own"]
    outs = [(tokens.shape, BF16, lane), ((local, feat, tok), BF16, at)]
    term_key, (term_first, term_last) = term
    for place, slots in enumerate(cut):
        keys.append((term_key, place))
        outs.append(
            (
                (len(slots), term_last - term_first, rows, blk),
                F32 if place == 0 else BF16,
                pl.BlockSpec((len(slots), step, rows, blk), lambda j, _: (0, (first - term_first) // step + j, 0, 0)),
            )
        )
    for shift in range(1, group):
        for key, (b_first, b_last), (j_first, j_last) in backs:
            keys.append((key, shift))
            outs.append(
                (
                    (j_last - j_first, (b_last - b_first) * per, tok),
                    BF16,
                    pl.BlockSpec(
                        (step, (b_last - b_first) * per, tok),
                        functools.partial(lambda start, j, _: (start + j, 0, 0), (first - j_first) // step),
                    ),
                )
            )
    kept = {place: held[key] for place, key in enumerate(keys) if key in held}
    cuts = [(b_first * per, b_last * per) for _, (b_first, b_last), _ in backs]
    got = call(
        functools.partial(mix_kernel, weights, cut, relative, group, local * group, cuts),
        "mix",
        ids,
        ((last - first) // step,),
        [(own, at)]
        + [(array, pl.BlockSpec((step, feat, tok), lambda j, _: (j, 0, 0))) for array in arrived]
        + weights.specs(step, lambda j: first // step + j)
        + [(tokens, lane), (upstream, lane)],
        kept,
        outs,
        [
            pltpu.VMEM((step, blk, tok), BF16),
            pltpu.VMEM((step, blk, tok), BF16),
            pltpu.VMEM((step, blk, blk), BF16),
            pltpu.VMEM((step, blk, blk), F32),
        ],
    )
    held.update(zip(keys, got))


def fold_kernel(columns, cut, relative, group, inner, pieces, ids, own_ref, *rest):
    arrived, rest = rest[: pieces * (group - 1)], rest[pieces * (group - 1) :]
    x_ref, up_ref = rest[:2]
    rest = rest[2:]
    w_refs = []
    for weights in columns:
        w_refs.append(rest[: len(weights.arrays)])
        rest = rest[len(weights.arrays) :]
    out_ref, term_refs = rest[0], rest[1:-4]
    inner_grad, held, sorted_term, term = rest[-4:]
    me = ids[0]
    blk = held.shape[2]
    width = blk // group
    for shift in range(group):
        if shift == 0:
            piece = own_ref[...]
        else:
            refs = arrived[(shift - 1) * pieces : shift * pieces]
            piece = jnp.concatenate([ref[...] for ref in refs], axis=0)
        piece = piece.astype(F32)
        for half in range(2):
            part = piece[:, half * inner : (half + 1) * inner].reshape(width, -1)
            inner_grad[half, shift * width : (shift + 1) * width, :] = part.astype(BF16)
    for half in range(2):
        cols = slice(half * blk, (half + 1) * blk)
        if len(columns) == 1:
            weight = columns[0].load(w_refs[0], half, held.at[half], ids[1])
        else:
            start = 0
            for weights, refs in zip(columns, w_refs):
                size = weights.cols
                part = held.at[half, :, start : start + size]
                part[...] = weights.load(refs, half, part, ids[1])
                start += size
            weight = held[half]
        du = inner_grad[half]
        unsorted = dot(du, x_ref[:, cols], 1, 0)
        for shift in range(group):
            source = lax.rem(me - shift + group, group)
            sorted_term[half, aligned(source, width), :] = unsorted[shift * width : (shift + 1) * width]
        store_term(sorted_term[half].T, cut, relative, term_refs, term.at[half], ids[1], half)
        back = dot(du.T, weight, 1, 1)
        out_ref[:, cols] = (up_ref[:, cols].astype(F32) + back).astype(BF16)


def fold(ids, own, arrived, tokens, upstream, columns, grad_tokens, span, group, local, cut, relative, after):
    tok = tokens.shape[0]
    blk = tokens.shape[1] // local
    inner = blk // (local * group)
    first, last = span
    rows = blk // sum(len(slots) for slots in cut)
    start = first // 2
    lane = pl.BlockSpec((tok, 2 * blk), lambda pair, _: (0, start + pair))
    inputs = []
    for array, begin in [(own, 0)] + arrived:
        at = functools.partial(lambda skip, pair, _: (0, skip + pair, 0), start - begin // 2)
        inputs.append((array, pl.BlockSpec((array.shape[0], 2 * inner, tok), at)))
    inputs += [(tokens, lane), (upstream, lane)]
    for weights in columns:
        inputs += weights.specs(2, lambda pair: start + pair)
    outs = [(tokens.shape, BF16, lane)] + [
        (
            (len(slots), last - first, rows, blk),
            F32 if place == 0 else BF16,
            pl.BlockSpec((len(slots), 2, rows, blk), lambda pair, _: (0, pair, 0, 0)),
        )
        for place, slots in enumerate(cut)
    ]
    pieces = len(arrived) // (group - 1)
    held = {} if grad_tokens is None else {0: grad_tokens}
    return call(
        functools.partial(fold_kernel, columns, cut, relative, group, inner, pieces),
        "fold",
        ids,
        ((last - first) // 2,),
        inputs,
        held,
        outs,
        [
            pltpu.VMEM((2, blk, tok), BF16),
            pltpu.VMEM((2, blk, blk), BF16),
            pltpu.VMEM((2, blk, blk), F32),
            pltpu.VMEM((2, blk, blk), F32),
        ],
        after,
    )


def send(array, shift, group):
    return lax.ppermute(array, "mp", [(at, (at + shift) % group) for at in range(group)])


def gather_plain(shard):
    local, rows, blk = shard.shape
    whole = lax.all_gather(shard, "dp", axis=0, tiled=False)
    if rows % 16:
        whole = jnp.transpose(whole, (1, 0, 2, 3)).reshape(1, local, whole.shape[0] * rows, blk)
    return Whole([whole], [list(range(whole.shape[0]))], False)


def scatter_plain(term, rows, scale):
    if term.shape[2] != rows:
        _, count, whole, blk = term.shape
        term = jnp.transpose(term.reshape(count, whole // rows, rows, blk), (1, 0, 2, 3))
    return lax.psum_scatter(term, "dp", scatter_dimension=0, tiled=False) * scale


def on_device(tokens, upstream, first_factor, second_factor):
    local, rows, blk = first_factor.shape
    group, size = lax.axis_size("mp"), lax.axis_size("dp")
    width = blk // group
    scale = 1.0 / math.sqrt(tokens.shape[0] * size)
    me, device = lax.axis_index("mp"), lax.axis_index("dp")
    ids = jnp.stack([me, device]).astype(jnp.int32)
    cube = group == 2 and size >= 8 and size & (size - 1) == 0 and rows % 16 == 0 and width % 128 == 0
    net = Network(size) if cube else None
    cut = net.first_cut() if cube else [[0]]
    plain_cut = [list(range(size))] if cube else [[0]]
    j_spans = split_by(local, (3, 3, 2)) if cube else split_even(local, 4)
    b_spans = [(2 * lo, 2 * hi) for lo, hi in split_by(local // 2, (3, 3, 2))]
    shifts = list(range(1, group))

    if cube:
        cols = [
            lax.dynamic_slice_in_dim(first_factor, lax.rem(me + shift, group) * width, width, 2)
            for shift in range(2)
        ]
        far = net.gather(cols[1])
        both = gather_plain(jnp.concatenate([second_factor, cols[0]], axis=2))
        second_whole = Whole(both.arrays, both.slots, False, (blk, 0))
        near = Whole(both.arrays, both.slots, False, (width, group))
        columns = [near, far]
    else:
        second_whole = gather_plain(second_factor)
        whole = gather_plain(first_factor).arrays[0]
        if whole.shape[0] > 1:
            whole = jnp.transpose(whole, (1, 0, 2, 3)).reshape(1, local, blk, blk)
        turned = jnp.roll(whole, -me * width, axis=3)
        near, far, turned = [
            Whole([array], [[0]], False) for array in (turned[..., :width], turned[..., width:], turned)
        ]
        columns = [turned]
    sends = expand(ids, tokens, far, shifts, j_spans, group, local)
    arrived = [
        [send(sends[(shift - 1) * len(j_spans) + at], shift, group) for shift in shifts]
        for at in range(len(j_spans))
    ]
    own = expand(ids, tokens, near, [0], [(0, local)], group, local)[0]

    held = {}
    backs = [(("back", place), b_span, (0, local)) for place, b_span in enumerate(b_spans)]
    for at, span in enumerate(j_spans):
        mix(
            ids, own, arrived[at], second_whole, tokens, upstream, held, span, group, local, cut, cube,
            ("term", (0, local)), backs,
        )
    returned = [[send(held[(key, shift)], shift, group) for shift in shifts] for key, _, _ in backs]
    parts = [held[("term", place)] for place in range(len(cut))]
    if cube:
        grad_second, marks = net.scatter(parts, scale)
    else:
        grad_second, marks = scatter_plain(parts[0], rows, scale), []

    grad_tokens, sums, terms, chains = None, [], [], [marks]
    tie = lambda place: [array for chain, step in TIES.get(place, ()) if cube for array in chains[chain][step]]
    for place, b_span in enumerate(b_spans):
        grad_tokens, *parts = fold(
            ids, held["own"], [(array, b_span[0]) for array in returned[place]], tokens, upstream, columns,
            grad_tokens, b_span, group, local, cut, cube, tie(place),
        )
        if cube:
            total, marks = net.scatter(parts, scale)
            chains.append(marks)
            sums.append(total)
        else:
            terms.append(parts[0])
    if not cube:
        sums = [scatter_plain(jnp.concatenate(terms, axis=1), rows, scale)]
    return held["mixed"], grad_tokens, jnp.concatenate(sums), grad_second


def solution(mesh):
    placed = (P("dp", "mp"), P("dp", "mp"), P("mp", "dp", None), P("mp", "dp", None))
    return jax.shard_map(
        on_device, mesh=mesh, in_specs=placed, out_specs=placed, check_vma=False
    )
```

```python
import functools
import math

import jax
import jax.numpy as jnp
from jax import lax
from jax.experimental import pallas as pl
from jax.experimental.pallas import tpu as pltpu
from jax.sharding import PartitionSpec as P

BF16 = jnp.bfloat16
F32 = jnp.float32
ROOT_HALF = math.sqrt(0.5)
DENSITY = 1.0 / math.sqrt(2.0 * math.pi)
JOINED = (True, True, False, False)
TIES = {0: ((0, 1),), 1: ((1, 1),), 2: ((0, 2), (1, 2), (2, 1))}
VMEM = 20 * 1024 * 1024
LARGE = 1 << 20


def split_even(count, parts):
    parts = min(count, parts)
    edges = [count * step // parts for step in range(parts + 1)]
    return list(zip(edges[:-1], edges[1:]))


def split_by(count, weights):
    total, edges, run = sum(weights), [0], 0
    for weight in weights:
        run += weight
        edges.append(count * run // total)
    return [(lo, hi) for lo, hi in zip(edges[:-1], edges[1:]) if hi > lo]


def dot(left, right, left_dim, right_dim):
    return lax.dot_general(
        left, right, (((left_dim,), (right_dim,)), ((), ())), preferred_element_type=F32
    )


def aligned(index, size):
    return pl.ds(pl.multiple_of(index * size, size), size)


def placed_for(array):
    if array.ndim == 2 or array.ndim == 4 and array.size > LARGE:
        return pltpu.with_memory_space_constraint(array, pltpu.HBM)
    return array


def call(kernel, name, ids, grid, inputs, held, outputs, scratch=(), after=()):
    places = sorted(held)
    extra = [held[place] for place in places] + list(after)
    taken = len(inputs)

    def body(ids_ref, *refs):
        kernel(ids_ref, *refs[:taken], *refs[taken + len(extra) :])

    return pl.pallas_call(
        body,
        grid_spec=pltpu.PrefetchScalarGridSpec(
            num_scalar_prefetch=1,
            grid=grid,
            in_specs=[spec for _, spec in inputs] + [pl.BlockSpec(memory_space=pl.ANY)] * len(extra),
            out_specs=[spec for _, _, spec in outputs],
            scratch_shapes=list(scratch),
        ),
        out_shape=[jax.ShapeDtypeStruct(shape, dtype) for shape, dtype, _ in outputs],
        input_output_aliases={1 + taken + at: place for at, place in enumerate(places)},
        compiler_params=pltpu.CompilerParams(
            dimension_semantics=("arbitrary",) * len(grid), vmem_limit_bytes=VMEM
        ),
        cost_estimate=pl.CostEstimate(flops=1, bytes_accessed=1, transcendentals=0),
        name=name,
    )(ids, *[placed_for(array) for array, _ in inputs], *extra)


class Whole:
    def __init__(self, arrays, slots, relative, lanes=None):
        self.arrays, self.slots, self.relative = arrays, slots, relative
        self.cols, self.lane = lanes or (arrays[0].shape[3], 0)

    def specs(self, count, at):
        return [
            (
                array,
                pl.BlockSpec(
                    (array.shape[0], count, array.shape[2], self.cols),
                    lambda step, _: (0, at(step), 0, self.lane),
                ),
            )
            for array in self.arrays
        ]

    def load(self, refs, block, target, device):
        if not self.relative:
            return refs[0][:, block].reshape(target.shape)
        for ref, slots in zip(refs, self.slots):
            rows = ref.shape[2]
            for place, slot in enumerate(slots):
                target[aligned(lax.bitwise_xor(device, slot), rows), :] = ref[place, block]
        return target[...]


def combos(bits):
    found = [0]
    for bit in bits:
        found += [value | bit for value in found]
    return found


class Network:
    def __init__(self, size):
        bits = [1 << k for k in range(size.bit_length() - 1)]
        self.size = size
        self.near, self.far = bits[:2], bits[2:]
        self.rounds = [(bit,) for bit in bits]
        self.order = [0]
        for bits in reversed(self.rounds):
            self.order = [slot | mask for mask in combos(bits) for slot in self.order]

    def swap(self, array, mask):
        return lax.ppermute(array, "dp", [(at, at ^ mask) for at in range(self.size)])

    def gather(self, shard):
        combo = combos(self.far)
        first = [shard[None]] + [self.swap(shard[None], mask) for mask in combo[1:]]
        have = [(jnp.concatenate(first, axis=0), combo)]
        for mask in reversed(self.near):
            have = have + [(self.swap(array, mask), [slot | mask for slot in slots]) for array, slots in have]
        return Whole([array for array, _ in have], [slots for _, slots in have], True)

    def cut(self, slots, bits):
        mask = sum(bits)
        return [[slot for slot in slots if slot & mask == value] for value in combos(bits)]

    def first_cut(self):
        return self.cut(self.order, self.rounds[0])

    def scatter(self, parts, scale, joined=False):
        rounds = self.rounds[: len(self.near)] + [tuple(self.far)] if joined else self.rounds
        slots = self.first_cut()[0]
        terms, sends, marks = [parts[0]], parts[1:], []
        for step, bits in enumerate(rounds):
            marks.append(sends)
            terms += [self.swap(piece, mask) for piece, mask in zip(sends, combos(bits)[1:])]
            if step + 1 < len(rounds):
                lists = self.cut(slots, rounds[step + 1])
                spans = [(slots.index(members[0]), slots.index(members[-1]) + 1) for members in lists]
                sends = [sum(term[lo:hi].astype(F32) for term in terms).astype(BF16) for lo, hi in spans[1:]]
                terms = [term[spans[0][0] : spans[0][1]] for term in terms]
                slots = lists[0]
        result = sum(term[0].astype(F32) for term in terms) * scale
        return result, marks + [[result]]


def tiles(array, rows, cols, down, along, at):
    return [
        (
            array,
            pl.BlockSpec(
                (rows, cols),
                functools.partial(lambda row, col, step, _: (row, along * at(step) + col), row, col),
            ),
        )
        for row in range(down)
        for col in range(along)
    ]


def expand_kernel(weights, shifts, spans, group, inner, ids, *rest):
    x_refs, rest = rest[:4], rest[4:]
    w_refs, rest = rest[: len(weights.arrays)], rest[len(weights.arrays) :]
    outs, held = rest[:-1], rest[-1]
    blk = held.shape[1]
    halves = []
    for half in range(2):
        weight = weights.load(w_refs, half, held.at[half], ids[1])
        acts = jnp.concatenate([x_refs[half][...], x_refs[2 + half][...]], axis=0)
        halves.append(dot(acts, weight, 1, 0).astype(BF16).T.astype(F32))
    width = blk // group
    for at, _ in enumerate(shifts):
        parts = [
            full[at * width : (at + 1) * width].reshape(width // inner, inner, -1) for full in halves
        ]
        piece = jnp.concatenate(parts, axis=1).astype(BF16)
        for place, (start, stop) in enumerate(spans):
            outs[at * len(spans) + place][...] = piece[start:stop]


def expand(ids, tokens, weights, shifts, spans, group, local, after=()):
    tok = tokens.shape[0]
    blk = tokens.shape[1] // local
    inner = blk // (local * group)
    cols = len(shifts) * (blk // group)
    shapes = [stop - start for _ in shifts for start, stop in spans]
    return call(
        functools.partial(expand_kernel, weights, shifts, spans, group, inner),
        "expand",
        ids,
        (local // 2,),
        tiles(tokens, tok // 2, blk, 2, 2, lambda pair: pair)
        + weights.specs(2, lambda pair: pair),
        {},
        [
            (
                (count, local * inner, tok),
                BF16,
                pl.BlockSpec((count, 2 * inner, tok), lambda pair, _: (0, pair, 0)),
            )
            for count in shapes
        ],
        [pltpu.VMEM((2, blk, cols), BF16)],
        after,
    )


def order_matrix(blk, blocks, flip):
    inner = blk // blocks
    out = lax.broadcasted_iota(jnp.int32, (blk, blk), 1 if flip else 0)
    held = lax.broadcasted_iota(jnp.int32, (blk, blk), 0 if flip else 1)
    return (held == lax.rem(out, blocks) * inner + lax.div(out, blocks)).astype(F32).astype(BF16)


def store_term(term, slots_lists, relative, outs, scratch, device, block):
    if not relative:
        out = outs[0]
        out[:, block] = term.reshape(out.shape[0], out.shape[2], out.shape[3])
        return
    scratch[...] = term
    for out, slots in zip(outs, slots_lists):
        rows = out.shape[2]
        for place, slot in enumerate(slots):
            out[place, block] = scratch[aligned(lax.bitwise_xor(device, slot), rows), :].astype(out.dtype)


def mix_kernel(weights, cut, relative, group, blocks, backs, ids, own_ref, *rest):
    arrived, rest = rest[: group - 1], rest[group - 1 :]
    w_refs, rest = rest[: len(weights.arrays)], rest[len(weights.arrays) :]
    step = (len(rest) - 6 - len(cut) - len(backs) * (group - 1)) // 2
    x_refs, up_refs, rest = rest[:step], rest[step : 2 * step], rest[2 * step :]
    mixed_ref, back_own_ref = rest[:2]
    term_refs, rest = rest[2 : 2 + len(cut)], rest[2 + len(cut) :]
    back_refs, (moved, back, held, term) = rest[:-4], rest[-4:]
    me = ids[0]
    blk = held.shape[1]
    rows = blk // group
    there = order_matrix(blk, blocks, False)
    again = order_matrix(blk, blocks, True)
    for j in range(held.shape[0]):
        cols = slice(j * blk, (j + 1) * blk)
        moved[j, aligned(me, rows), :] = own_ref[j]
        for shift in range(1, group):
            moved[j, aligned(lax.rem(me - shift + group, group), rows), :] = arrived[shift - 1][j]
        weight = weights.load(w_refs, j, held.at[j], ids[1])
        ordered = dot(there, moved[j], 1, 0).astype(BF16)
        inner_out = dot(ordered.T, weight, 1, 0)
        cdf = 0.5 + 0.5 * lax.erf(inner_out * ROOT_HALF)
        mixed_ref[:, cols] = (x_refs[j][...].astype(F32) + inner_out * cdf).astype(BF16)
        slope = cdf + inner_out * (DENSITY * jnp.exp(-0.5 * inner_out * inner_out))
        grad_out = (up_refs[j][...].astype(F32) * slope).astype(BF16)
        store_term(dot(ordered, grad_out, 1, 0), cut, relative, term_refs, term.at[j], ids[1], j)
        returned = dot(weight, grad_out, 1, 1).astype(BF16)
        back[j] = dot(again, returned, 1, 0).astype(BF16)
        back_own_ref[j] = back[j, aligned(me, rows), :]
        for shift in range(1, group):
            piece = back[j, aligned(lax.rem(me + shift, group), rows), :]
            for at, (start, stop) in enumerate(backs):
                back_refs[(shift - 1) * len(backs) + at][j] = piece[start:stop]


def mix(ids, own, arrived, weights, tokens, upstream, held, span, group, local, cut, relative, term, backs):
    tok = tokens.shape[0]
    blk = tokens.shape[1] // local
    feat = blk // group
    per = feat // local
    first, last = span
    rows = blk // sum(len(slots) for slots in cut)
    step = math.gcd(2, math.gcd(first, last))
    lane = pl.BlockSpec((tok, step * blk), lambda j, _: (0, first // step + j))
    at = pl.BlockSpec((step, feat, tok), lambda j, _: (first // step + j, 0, 0))
    keys = ["mixed", "own"]
    outs = [(tokens.shape, BF16, lane), ((local, feat, tok), BF16, at)]
    term_key, (term_first, term_last) = term
    for place, slots in enumerate(cut):
        keys.append((term_key, place))
        outs.append(
            (
                (len(slots), term_last - term_first, rows, blk),
                F32 if place == 0 else BF16,
                pl.BlockSpec((len(slots), step, rows, blk), lambda j, _: (0, (first - term_first) // step + j, 0, 0)),
            )
        )
    for shift in range(1, group):
        for key, (b_first, b_last), (j_first, j_last) in backs:
            keys.append((key, shift))
            outs.append(
                (
                    (j_last - j_first, (b_last - b_first) * per, tok),
                    BF16,
                    pl.BlockSpec(
                        (step, (b_last - b_first) * per, tok),
                        functools.partial(lambda start, j, _: (start + j, 0, 0), (first - j_first) // step),
                    ),
                )
            )
    kept = {place: held[key] for place, key in enumerate(keys) if key in held}
    cuts = [(b_first * per, b_last * per) for _, (b_first, b_last), _ in backs]
    got = call(
        functools.partial(mix_kernel, weights, cut, relative, group, local * group, cuts),
        "mix",
        ids,
        ((last - first) // step,),
        [(own, at)]
        + [(array, pl.BlockSpec((step, feat, tok), lambda j, _: (j, 0, 0))) for array in arrived]
        + weights.specs(step, lambda j: first // step + j)
        + tiles(tokens, tok, blk, 1, step, lambda j: first // step + j)
        + tiles(upstream, tok, blk, 1, step, lambda j: first // step + j),
        kept,
        outs,
        [
            pltpu.VMEM((step, blk, tok), BF16),
            pltpu.VMEM((step, blk, tok), BF16),
            pltpu.VMEM((step, blk, blk), BF16),
            pltpu.VMEM((step, blk, blk), F32),
        ],
    )
    held.update(zip(keys, got))


def fold_kernel(columns, cut, relative, group, inner, pieces, ids, own_ref, *rest):
    arrived, rest = rest[: pieces * (group - 1)], rest[pieces * (group - 1) :]
    x_refs, up_refs, rest = rest[:2], rest[2:4], rest[4:]
    w_refs = []
    for weights in columns:
        w_refs.append(rest[: len(weights.arrays)])
        rest = rest[len(weights.arrays) :]
    out_ref, term_refs = rest[0], rest[1:-4]
    inner_grad, held, sorted_term, term = rest[-4:]
    me = ids[0]
    blk = held.shape[2]
    width = blk // group
    for shift in range(group):
        if shift == 0:
            piece = own_ref[...]
        else:
            refs = arrived[(shift - 1) * pieces : shift * pieces]
            piece = jnp.concatenate([ref[...] for ref in refs], axis=0)
        piece = piece.astype(F32)
        for half in range(2):
            part = piece[:, half * inner : (half + 1) * inner].reshape(width, -1)
            inner_grad[half, shift * width : (shift + 1) * width, :] = part.astype(BF16)
    for half in range(2):
        cols = slice(half * blk, (half + 1) * blk)
        if len(columns) == 1:
            weight = columns[0].load(w_refs[0], half, held.at[half], ids[1])
        else:
            start = 0
            for weights, refs in zip(columns, w_refs):
                size = weights.cols
                part = held.at[half, :, start : start + size]
                part[...] = weights.load(refs, half, part, ids[1])
                start += size
            weight = held[half]
        du = inner_grad[half]
        unsorted = dot(du, x_refs[half][...], 1, 0)
        for shift in range(group):
            source = lax.rem(me - shift + group, group)
            sorted_term[half, aligned(source, width), :] = unsorted[shift * width : (shift + 1) * width]
        store_term(sorted_term[half].T, cut, relative, term_refs, term.at[half], ids[1], half)
        back = dot(du.T, weight, 1, 1)
        out_ref[:, cols] = (up_refs[half][...].astype(F32) + back).astype(BF16)


def fold(ids, own, arrived, tokens, upstream, columns, grad_tokens, span, group, local, cut, relative, after):
    tok = tokens.shape[0]
    blk = tokens.shape[1] // local
    inner = blk // (local * group)
    first, last = span
    rows = blk // sum(len(slots) for slots in cut)
    start = first // 2
    lane = pl.BlockSpec((tok, 2 * blk), lambda pair, _: (0, start + pair))
    inputs = []
    for array, begin in [(own, 0)] + arrived:
        at = functools.partial(lambda skip, pair, _: (0, skip + pair, 0), start - begin // 2)
        inputs.append((array, pl.BlockSpec((array.shape[0], 2 * inner, tok), at)))
    for array in (tokens, upstream):
        inputs += tiles(array, tok, blk, 1, 2, lambda pair: start + pair)
    for weights in columns:
        inputs += weights.specs(2, lambda pair: start + pair)
    outs = [(tokens.shape, BF16, lane)] + [
        (
            (len(slots), last - first, rows, blk),
            F32 if place == 0 else BF16,
            pl.BlockSpec((len(slots), 2, rows, blk), lambda pair, _: (0, pair, 0, 0)),
        )
        for place, slots in enumerate(cut)
    ]
    pieces = len(arrived) // (group - 1)
    held = {} if grad_tokens is None else {0: grad_tokens}
    return call(
        functools.partial(fold_kernel, columns, cut, relative, group, inner, pieces),
        "fold",
        ids,
        ((last - first) // 2,),
        inputs,
        held,
        outs,
        [
            pltpu.VMEM((2, blk, tok), BF16),
            pltpu.VMEM((2, blk, blk), BF16),
            pltpu.VMEM((2, blk, blk), F32),
            pltpu.VMEM((2, blk, blk), F32),
        ],
        after,
    )


def send(array, shift, group):
    return lax.ppermute(array, "mp", [(at, (at + shift) % group) for at in range(group)])


def gather_plain(shard):
    local, rows, blk = shard.shape
    whole = lax.all_gather(shard, "dp", axis=0, tiled=False)
    if rows % 16:
        whole = jnp.transpose(whole, (1, 0, 2, 3)).reshape(1, local, whole.shape[0] * rows, blk)
    return Whole([whole], [list(range(whole.shape[0]))], False)


def scatter_plain(term, rows, scale):
    if term.shape[2] != rows:
        _, count, whole, blk = term.shape
        term = jnp.transpose(term.reshape(count, whole // rows, rows, blk), (1, 0, 2, 3))
    return lax.psum_scatter(term, "dp", scatter_dimension=0, tiled=False) * scale


def on_device(tokens, upstream, first_factor, second_factor):
    local, rows, blk = first_factor.shape
    group, size = lax.axis_size("mp"), lax.axis_size("dp")
    width = blk // group
    scale = 1.0 / math.sqrt(tokens.shape[0] * size)
    me, device = lax.axis_index("mp"), lax.axis_index("dp")
    ids = jnp.stack([me, device]).astype(jnp.int32)
    cube = group == 2 and size >= 8 and size & (size - 1) == 0 and rows % 16 == 0 and width % 128 == 0
    net = Network(size) if cube else None
    cut = net.first_cut() if cube else [[0]]
    plain_cut = [list(range(size))] if cube else [[0]]
    j_spans = split_by(local, (3, 3, 2)) if cube else split_even(local, 4)
    b_spans = [(2 * lo, 2 * hi) for lo, hi in split_by(local // 2, (3, 3, 2))]
    shifts = list(range(1, group))

    if cube:
        cols = [
            lax.dynamic_slice_in_dim(first_factor, lax.rem(me + shift, group) * width, width, 2)
            for shift in range(2)
        ]
        far = net.gather(cols[1])
        both = gather_plain(jnp.concatenate([second_factor, cols[0]], axis=2))
        second_whole = Whole(both.arrays, both.slots, False, (blk, 0))
        near = Whole(both.arrays, both.slots, False, (width, group))
        columns = [near, far]
    else:
        second_whole = gather_plain(second_factor)
        whole = gather_plain(first_factor).arrays[0]
        if whole.shape[0] > 1:
            whole = jnp.transpose(whole, (1, 0, 2, 3)).reshape(1, local, blk, blk)
        turned = jnp.roll(whole, -me * width, axis=3)
        near, far, turned = [
            Whole([array], [[0]], False) for array in (turned[..., :width], turned[..., width:], turned)
        ]
        columns = [turned]
    sends = expand(ids, tokens, far, shifts, j_spans, group, local)
    arrived = [
        [send(sends[(shift - 1) * len(j_spans) + at], shift, group) for shift in shifts]
        for at in range(len(j_spans))
    ]
    own = expand(ids, tokens, near, [0], [(0, local)], group, local)[0]

    held = {}
    backs = [(("back", place), b_span, (0, local)) for place, b_span in enumerate(b_spans)]
    for at, span in enumerate(j_spans):
        mix(
            ids, own, arrived[at], second_whole, tokens, upstream, held, span, group, local, cut, cube,
            ("term", (0, local)), backs,
        )
    returned = [[send(held[(key, shift)], shift, group) for shift in shifts] for key, _, _ in backs]
    parts = [held[("term", place)] for place in range(len(cut))]
    if cube:
        grad_second, marks = net.scatter(parts, scale, JOINED[0])
    else:
        grad_second, marks = scatter_plain(parts[0], rows, scale), []

    grad_tokens, sums, terms, chains = None, [], [], [marks]
    tie = lambda place: [array for chain, step in TIES.get(place, ()) if cube for array in chains[chain][step]]
    for place, b_span in enumerate(b_spans):
        grad_tokens, *parts = fold(
            ids, held["own"], [(array, b_span[0]) for array in returned[place]], tokens, upstream, columns,
            grad_tokens, b_span, group, local, cut, cube, tie(place),
        )
        if cube:
            total, marks = net.scatter(parts, scale, JOINED[1 + place])
            chains.append(marks)
            sums.append(total)
        else:
            terms.append(parts[0])
    if not cube:
        sums = [scatter_plain(jnp.concatenate(terms, axis=1), rows, scale)]
    return held["mixed"], grad_tokens, jnp.concatenate(sums), grad_second


def solution(mesh):
    placed = (P("dp", "mp"), P("dp", "mp"), P("mp", "dp", None), P("mp", "dp", None))
    return jax.shard_map(
        on_device, mesh=mesh, in_specs=placed, out_specs=placed, check_vma=False
    )
```

```python
import functools
import math

import jax
import jax.numpy as jnp
from jax import lax
from jax.experimental import pallas as pl
from jax.experimental.pallas import tpu as pltpu
from jax.sharding import PartitionSpec as P

BF16 = jnp.bfloat16
F32 = jnp.float32
ROOT_HALF = math.sqrt(0.5)
DENSITY = 1.0 / math.sqrt(2.0 * math.pi)
JOINED = (True, True, False, False)
TIES = {0: ((0, 2),), 1: ((1, 1),), 2: ((0, 3), (1, 3), (2, 2))}
VMEM = 20 * 1024 * 1024
LARGE = 1 << 20


def split_even(count, parts):
    parts = min(count, parts)
    edges = [count * step // parts for step in range(parts + 1)]
    return list(zip(edges[:-1], edges[1:]))


def split_by(count, weights):
    total, edges, run = sum(weights), [0], 0
    for weight in weights:
        run += weight
        edges.append(count * run // total)
    return [(lo, hi) for lo, hi in zip(edges[:-1], edges[1:]) if hi > lo]


def dot(left, right, left_dim, right_dim):
    return lax.dot_general(
        left, right, (((left_dim,), (right_dim,)), ((), ())), preferred_element_type=F32
    )


def aligned(index, size):
    return pl.ds(pl.multiple_of(index * size, size), size)


def placed_for(array):
    if array.ndim == 2 or array.ndim == 4 and array.size > LARGE:
        return pltpu.with_memory_space_constraint(array, pltpu.HBM)
    return array


def call(kernel, name, ids, grid, inputs, held, outputs, scratch=(), after=()):
    places = sorted(held)
    extra = [held[place] for place in places] + list(after)
    taken = len(inputs)

    def body(ids_ref, *refs):
        kernel(ids_ref, *refs[:taken], *refs[taken + len(extra) :])

    return pl.pallas_call(
        body,
        grid_spec=pltpu.PrefetchScalarGridSpec(
            num_scalar_prefetch=1,
            grid=grid,
            in_specs=[spec for _, spec in inputs] + [pl.BlockSpec(memory_space=pl.ANY)] * len(extra),
            out_specs=[spec for _, _, spec in outputs],
            scratch_shapes=list(scratch),
        ),
        out_shape=[jax.ShapeDtypeStruct(shape, dtype) for shape, dtype, _ in outputs],
        input_output_aliases={1 + taken + at: place for at, place in enumerate(places)},
        compiler_params=pltpu.CompilerParams(
            dimension_semantics=("arbitrary",) * len(grid), vmem_limit_bytes=VMEM
        ),
        cost_estimate=pl.CostEstimate(flops=1, bytes_accessed=1, transcendentals=0),
        name=name,
    )(ids, *[placed_for(array) for array, _ in inputs], *extra)


class Whole:
    def __init__(self, arrays, slots, relative, lanes=None):
        self.arrays, self.slots, self.relative = arrays, slots, relative
        self.cols, self.lane = lanes or (arrays[0].shape[3], 0)

    def specs(self, count, at):
        return [
            (
                array,
                pl.BlockSpec(
                    (array.shape[0], count, array.shape[2], self.cols),
                    lambda step, _: (0, at(step), 0, self.lane),
                ),
            )
            for array in self.arrays
        ]

    def load(self, refs, block, target, device):
        if not self.relative:
            return refs[0][:, block].reshape(target.shape)
        for ref, slots in zip(refs, self.slots):
            rows = ref.shape[2]
            for place, slot in enumerate(slots):
                target[aligned(lax.bitwise_xor(device, slot), rows), :] = ref[place, block]
        return target[...]


def combos(bits):
    found = [0]
    for bit in bits:
        found += [value | bit for value in found]
    return found


class Network:
    def __init__(self, size):
        bits = [1 << k for k in range(size.bit_length() - 1)]
        self.size = size
        self.near, self.far = bits[:2], bits[2:]
        self.rounds = [(bit,) for bit in bits]
        self.order = [0]
        for bits in reversed(self.rounds):
            self.order = [slot | mask for mask in combos(bits) for slot in self.order]

    def swap(self, array, mask):
        return lax.ppermute(array, "dp", [(at, at ^ mask) for at in range(self.size)])

    def gather(self, shard):
        combo = combos(self.far)
        first = [shard[None]] + [self.swap(shard[None], mask) for mask in combo[1:]]
        have = [(jnp.concatenate(first, axis=0), combo)]
        for mask in reversed(self.near):
            have = have + [(self.swap(array, mask), [slot | mask for slot in slots]) for array, slots in have]
        return Whole([array for array, _ in have], [slots for _, slots in have], True)

    def cut(self, slots, bits):
        mask = sum(bits)
        return [[slot for slot in slots if slot & mask == value] for value in combos(bits)]

    def first_cut(self):
        return self.cut(self.order, self.rounds[0])

    def scatter(self, parts, scale, joined=False):
        rounds = self.rounds[: len(self.near)] + [tuple(self.far)] if joined else self.rounds
        slots = self.first_cut()[0]
        terms, sends, marks = [parts[0]], parts[1:], []
        for step, bits in enumerate(rounds):
            marks.append(sends)
            terms += [self.swap(piece, mask) for piece, mask in zip(sends, combos(bits)[1:])]
            if step + 1 < len(rounds):
                lists = self.cut(slots, rounds[step + 1])
                spans = [(slots.index(members[0]), slots.index(members[-1]) + 1) for members in lists]
                sends = [sum(term[lo:hi].astype(F32) for term in terms).astype(BF16) for lo, hi in spans[1:]]
                terms = [term[spans[0][0] : spans[0][1]] for term in terms]
                slots = lists[0]
        result = sum(term[0].astype(F32) for term in terms) * scale
        return result, marks + [[result]]


def tiles(array, rows, cols, down, along, at):
    return [
        (
            array,
            pl.BlockSpec(
                (rows, cols),
                functools.partial(lambda row, col, step, _: (row, along * at(step) + col), row, col),
            ),
        )
        for row in range(down)
        for col in range(along)
    ]


def expand_kernel(weights, shifts, spans, group, inner, ids, *rest):
    x_refs, rest = rest[:4], rest[4:]
    w_refs, rest = rest[: len(weights.arrays)], rest[len(weights.arrays) :]
    outs, held = rest[:-1], rest[-1]
    blk = held.shape[1]
    halves = []
    for half in range(2):
        weight = weights.load(w_refs, half, held.at[half], ids[1])
        acts = jnp.concatenate([x_refs[half][...], x_refs[2 + half][...]], axis=0)
        halves.append(dot(acts, weight, 1, 0).astype(BF16).T.astype(F32))
    width = blk // group
    for at, _ in enumerate(shifts):
        parts = [
            full[at * width : (at + 1) * width].reshape(width // inner, inner, -1) for full in halves
        ]
        piece = jnp.concatenate(parts, axis=1).astype(BF16)
        for place, (start, stop) in enumerate(spans):
            outs[at * len(spans) + place][...] = piece[start:stop]


def expand(ids, tokens, weights, shifts, spans, group, local, after=()):
    tok = tokens.shape[0]
    blk = tokens.shape[1] // local
    inner = blk // (local * group)
    cols = len(shifts) * (blk // group)
    shapes = [stop - start for _ in shifts for start, stop in spans]
    return call(
        functools.partial(expand_kernel, weights, shifts, spans, group, inner),
        "expand",
        ids,
        (local // 2,),
        tiles(tokens, tok // 2, blk, 2, 2, lambda pair: pair)
        + weights.specs(2, lambda pair: pair),
        {},
        [
            (
                (count, local * inner, tok),
                BF16,
                pl.BlockSpec((count, 2 * inner, tok), lambda pair, _: (0, pair, 0)),
            )
            for count in shapes
        ],
        [pltpu.VMEM((2, blk, cols), BF16)],
        after,
    )


def order_matrix(blk, blocks, flip):
    inner = blk // blocks
    out = lax.broadcasted_iota(jnp.int32, (blk, blk), 1 if flip else 0)
    held = lax.broadcasted_iota(jnp.int32, (blk, blk), 0 if flip else 1)
    return (held == lax.rem(out, blocks) * inner + lax.div(out, blocks)).astype(F32).astype(BF16)


def store_term(term, slots_lists, relative, outs, scratch, device, block):
    if not relative:
        out = outs[0]
        out[:, block] = term.reshape(out.shape[0], out.shape[2], out.shape[3])
        return
    scratch[...] = term
    for out, slots in zip(outs, slots_lists):
        rows = out.shape[2]
        for place, slot in enumerate(slots):
            out[place, block] = scratch[aligned(lax.bitwise_xor(device, slot), rows), :].astype(out.dtype)


def mix_kernel(weights, cut, relative, group, blocks, backs, ids, own_ref, *rest):
    arrived, rest = rest[: group - 1], rest[group - 1 :]
    w_refs, rest = rest[: len(weights.arrays)], rest[len(weights.arrays) :]
    step = (len(rest) - 6 - len(cut) - len(backs) * (group - 1)) // 2
    x_refs, up_refs, rest = rest[:step], rest[step : 2 * step], rest[2 * step :]
    mixed_ref, back_own_ref = rest[:2]
    term_refs, rest = rest[2 : 2 + len(cut)], rest[2 + len(cut) :]
    back_refs, (moved, back, held, term) = rest[:-4], rest[-4:]
    me = ids[0]
    blk = held.shape[1]
    rows = blk // group
    there = order_matrix(blk, blocks, False)
    again = order_matrix(blk, blocks, True)
    for j in range(held.shape[0]):
        cols = slice(j * blk, (j + 1) * blk)
        moved[j, aligned(me, rows), :] = own_ref[j]
        for shift in range(1, group):
            moved[j, aligned(lax.rem(me - shift + group, group), rows), :] = arrived[shift - 1][j]
        weight = weights.load(w_refs, j, held.at[j], ids[1])
        ordered = dot(there, moved[j], 1, 0).astype(BF16)
        inner_out = dot(ordered.T, weight, 1, 0)
        cdf = 0.5 + 0.5 * lax.erf(inner_out * ROOT_HALF)
        mixed_ref[:, cols] = (x_refs[j][...].astype(F32) + inner_out * cdf).astype(BF16)
        slope = cdf + inner_out * (DENSITY * jnp.exp(-0.5 * inner_out * inner_out))
        grad_out = (up_refs[j][...].astype(F32) * slope).astype(BF16)
        store_term(dot(ordered, grad_out, 1, 0), cut, relative, term_refs, term.at[j], ids[1], j)
        returned = dot(weight, grad_out, 1, 1).astype(BF16)
        back[j] = dot(again, returned, 1, 0).astype(BF16)
        back_own_ref[j] = back[j, aligned(me, rows), :]
        for shift in range(1, group):
            piece = back[j, aligned(lax.rem(me + shift, group), rows), :]
            for at, (start, stop) in enumerate(backs):
                back_refs[(shift - 1) * len(backs) + at][j] = piece[start:stop]


def mix(ids, own, arrived, weights, tokens, upstream, held, span, group, local, cut, relative, term, backs):
    tok = tokens.shape[0]
    blk = tokens.shape[1] // local
    feat = blk // group
    per = feat // local
    first, last = span
    rows = blk // sum(len(slots) for slots in cut)
    step = math.gcd(2, math.gcd(first, last))
    lane = pl.BlockSpec((tok, step * blk), lambda j, _: (0, first // step + j))
    at = pl.BlockSpec((step, feat, tok), lambda j, _: (first // step + j, 0, 0))
    keys = ["mixed", "own"]
    outs = [(tokens.shape, BF16, lane), ((local, feat, tok), BF16, at)]
    term_key, (term_first, term_last) = term
    for place, slots in enumerate(cut):
        keys.append((term_key, place))
        outs.append(
            (
                (len(slots), term_last - term_first, rows, blk),
                F32 if place == 0 else BF16,
                pl.BlockSpec((len(slots), step, rows, blk), lambda j, _: (0, (first - term_first) // step + j, 0, 0)),
            )
        )
    for shift in range(1, group):
        for key, (b_first, b_last), (j_first, j_last) in backs:
            keys.append((key, shift))
            outs.append(
                (
                    (j_last - j_first, (b_last - b_first) * per, tok),
                    BF16,
                    pl.BlockSpec(
                        (step, (b_last - b_first) * per, tok),
                        functools.partial(lambda start, j, _: (start + j, 0, 0), (first - j_first) // step),
                    ),
                )
            )
    kept = {place: held[key] for place, key in enumerate(keys) if key in held}
    cuts = [(b_first * per, b_last * per) for _, (b_first, b_last), _ in backs]
    got = call(
        functools.partial(mix_kernel, weights, cut, relative, group, local * group, cuts),
        "mix",
        ids,
        ((last - first) // step,),
        [(own, at)]
        + [(array, pl.BlockSpec((step, feat, tok), lambda j, _: (j, 0, 0))) for array in arrived]
        + weights.specs(step, lambda j: first // step + j)
        + tiles(tokens, tok, blk, 1, step, lambda j: first // step + j)
        + tiles(upstream, tok, blk, 1, step, lambda j: first // step + j),
        kept,
        outs,
        [
            pltpu.VMEM((step, blk, tok), BF16),
            pltpu.VMEM((step, blk, tok), BF16),
            pltpu.VMEM((step, blk, blk), BF16),
            pltpu.VMEM((step, blk, blk), F32),
        ],
    )
    held.update(zip(keys, got))


def fold_kernel(columns, cut, relative, group, inner, pieces, ids, own_ref, *rest):
    arrived, rest = rest[: pieces * (group - 1)], rest[pieces * (group - 1) :]
    x_refs, up_refs, rest = rest[:2], rest[2:4], rest[4:]
    w_refs = []
    for weights in columns:
        w_refs.append(rest[: len(weights.arrays)])
        rest = rest[len(weights.arrays) :]
    out_ref, term_refs = rest[0], rest[1:-4]
    inner_grad, held, sorted_term, term = rest[-4:]
    me = ids[0]
    blk = held.shape[2]
    width = blk // group
    for shift in range(group):
        if shift == 0:
            piece = own_ref[...]
        else:
            refs = arrived[(shift - 1) * pieces : shift * pieces]
            piece = jnp.concatenate([ref[...] for ref in refs], axis=0)
        piece = piece.astype(F32)
        for half in range(2):
            part = piece[:, half * inner : (half + 1) * inner].reshape(width, -1)
            inner_grad[half, shift * width : (shift + 1) * width, :] = part.astype(BF16)
    for half in range(2):
        cols = slice(half * blk, (half + 1) * blk)
        if len(columns) == 1:
            weight = columns[0].load(w_refs[0], half, held.at[half], ids[1])
        else:
            start = 0
            for weights, refs in zip(columns, w_refs):
                size = weights.cols
                part = held.at[half, :, start : start + size]
                part[...] = weights.load(refs, half, part, ids[1])
                start += size
            weight = held[half]
        du = inner_grad[half]
        unsorted = dot(du, x_refs[half][...], 1, 0)
        for shift in range(group):
            source = lax.rem(me - shift + group, group)
            sorted_term[half, aligned(source, width), :] = unsorted[shift * width : (shift + 1) * width]
        store_term(sorted_term[half].T, cut, relative, term_refs, term.at[half], ids[1], half)
        back = dot(du.T, weight, 1, 1)
        out_ref[:, cols] = (up_refs[half][...].astype(F32) + back).astype(BF16)


def fold(ids, own, arrived, tokens, upstream, columns, grad_tokens, span, group, local, cut, relative, after):
    tok = tokens.shape[0]
    blk = tokens.shape[1] // local
    inner = blk // (local * group)
    first, last = span
    rows = blk // sum(len(slots) for slots in cut)
    start = first // 2
    lane = pl.BlockSpec((tok, 2 * blk), lambda pair, _: (0, start + pair))
    inputs = []
    for array, begin in [(own, 0)] + arrived:
        at = functools.partial(lambda skip, pair, _: (0, skip + pair, 0), start - begin // 2)
        inputs.append((array, pl.BlockSpec((array.shape[0], 2 * inner, tok), at)))
    for array in (tokens, upstream):
        inputs += tiles(array, tok, blk, 1, 2, lambda pair: start + pair)
    for weights in columns:
        inputs += weights.specs(2, lambda pair: start + pair)
    outs = [(tokens.shape, BF16, lane)] + [
        (
            (len(slots), last - first, rows, blk),
            F32 if place == 0 else BF16,
            pl.BlockSpec((len(slots), 2, rows, blk), lambda pair, _: (0, pair, 0, 0)),
        )
        for place, slots in enumerate(cut)
    ]
    pieces = len(arrived) // (group - 1)
    held = {} if grad_tokens is None else {0: grad_tokens}
    return call(
        functools.partial(fold_kernel, columns, cut, relative, group, inner, pieces),
        "fold",
        ids,
        ((last - first) // 2,),
        inputs,
        held,
        outs,
        [
            pltpu.VMEM((2, blk, tok), BF16),
            pltpu.VMEM((2, blk, blk), BF16),
            pltpu.VMEM((2, blk, blk), F32),
            pltpu.VMEM((2, blk, blk), F32),
        ],
        after,
    )


def send(array, shift, group):
    return lax.ppermute(array, "mp", [(at, (at + shift) % group) for at in range(group)])


def gather_plain(shard):
    local, rows, blk = shard.shape
    whole = lax.all_gather(shard, "dp", axis=0, tiled=False)
    if rows % 16:
        whole = jnp.transpose(whole, (1, 0, 2, 3)).reshape(1, local, whole.shape[0] * rows, blk)
    return Whole([whole], [list(range(whole.shape[0]))], False)


def scatter_plain(term, rows, scale):
    if term.shape[2] != rows:
        _, count, whole, blk = term.shape
        term = jnp.transpose(term.reshape(count, whole // rows, rows, blk), (1, 0, 2, 3))
    return lax.psum_scatter(term, "dp", scatter_dimension=0, tiled=False) * scale


def on_device(tokens, upstream, first_factor, second_factor):
    local, rows, blk = first_factor.shape
    group, size = lax.axis_size("mp"), lax.axis_size("dp")
    width = blk // group
    scale = 1.0 / math.sqrt(tokens.shape[0] * size)
    me, device = lax.axis_index("mp"), lax.axis_index("dp")
    ids = jnp.stack([me, device]).astype(jnp.int32)
    cube = group == 2 and size >= 8 and size & (size - 1) == 0 and rows % 16 == 0 and width % 128 == 0
    net = Network(size) if cube else None
    cut = net.first_cut() if cube else [[0]]
    plain_cut = [list(range(size))] if cube else [[0]]
    j_spans = split_by(local, (3, 3, 2)) if cube else split_even(local, 4)
    b_spans = [(2 * lo, 2 * hi) for lo, hi in split_by(local // 2, (3, 3, 2))]
    shifts = list(range(1, group))

    if cube:
        cols = [
            lax.dynamic_slice_in_dim(first_factor, lax.rem(me + shift, group) * width, width, 2)
            for shift in range(2)
        ]
        far = net.gather(cols[1])
        both = gather_plain(jnp.concatenate([second_factor, cols[0]], axis=2))
        second_whole = Whole(both.arrays, both.slots, False, (blk, 0))
        near = Whole(both.arrays, both.slots, False, (width, group))
        columns = [near, far]
    else:
        second_whole = gather_plain(second_factor)
        whole = gather_plain(first_factor).arrays[0]
        if whole.shape[0] > 1:
            whole = jnp.transpose(whole, (1, 0, 2, 3)).reshape(1, local, blk, blk)
        turned = jnp.roll(whole, -me * width, axis=3)
        near, far, turned = [
            Whole([array], [[0]], False) for array in (turned[..., :width], turned[..., width:], turned)
        ]
        columns = [turned]
    sends = expand(ids, tokens, far, shifts, j_spans, group, local)
    arrived = [
        [send(sends[(shift - 1) * len(j_spans) + at], shift, group) for shift in shifts]
        for at in range(len(j_spans))
    ]
    own = expand(ids, tokens, near, [0], [(0, local)], group, local)[0]

    held = {}
    backs = [(("back", place), b_span, (0, local)) for place, b_span in enumerate(b_spans)]
    for at, span in enumerate(j_spans):
        mix(
            ids, own, arrived[at], second_whole, tokens, upstream, held, span, group, local, cut, cube,
            ("term", (0, local)), backs,
        )
    returned = [[send(held[(key, shift)], shift, group) for shift in shifts] for key, _, _ in backs]
    parts = [held[("term", place)] for place in range(len(cut))]
    if cube:
        grad_second, marks = net.scatter(parts, scale, JOINED[0])
    else:
        grad_second, marks = scatter_plain(parts[0], rows, scale), []

    grad_tokens, sums, terms, chains = None, [], [], [marks]
    tie = lambda place: [array for chain, step in TIES.get(place, ()) if cube for array in chains[chain][step]]
    for place, b_span in enumerate(b_spans):
        grad_tokens, *parts = fold(
            ids, held["own"], [(array, b_span[0]) for array in returned[place]], tokens, upstream, columns,
            grad_tokens, b_span, group, local, cut, cube, tie(place),
        )
        if cube:
            total, marks = net.scatter(parts, scale, JOINED[1 + place])
            chains.append(marks)
            sums.append(total)
        else:
            terms.append(parts[0])
    if not cube:
        sums = [scatter_plain(jnp.concatenate(terms, axis=1), rows, scale)]
    return held["mixed"], grad_tokens, jnp.concatenate(sums), grad_second


def solution(mesh):
    placed = (P("dp", "mp"), P("dp", "mp"), P("mp", "dp", None), P("mp", "dp", None))
    return jax.shard_map(
        on_device, mesh=mesh, in_specs=placed, out_specs=placed, check_vma=False
    )
```

```python
import functools
import math

import jax
import jax.numpy as jnp
from jax import lax
from jax.experimental import pallas as pl
from jax.experimental.pallas import tpu as pltpu
from jax.sharding import PartitionSpec as P

BF16 = jnp.bfloat16
F32 = jnp.float32
ROOT_HALF = math.sqrt(0.5)
DENSITY = 1.0 / math.sqrt(2.0 * math.pi)
JOINED = (True, True, False, False)
TIES = {0: ((0, 2),), 1: ((1, 1),), 2: ((0, 3), (1, 3), (2, 2))}
VMEM = 20 * 1024 * 1024
LARGE = 1 << 20


def split_even(count, parts):
    parts = min(count, parts)
    edges = [count * step // parts for step in range(parts + 1)]
    return list(zip(edges[:-1], edges[1:]))


def split_by(count, weights):
    total, edges, run = sum(weights), [0], 0
    for weight in weights:
        run += weight
        edges.append(count * run // total)
    return [(lo, hi) for lo, hi in zip(edges[:-1], edges[1:]) if hi > lo]


def dot(left, right, left_dim, right_dim):
    return lax.dot_general(
        left, right, (((left_dim,), (right_dim,)), ((), ())), preferred_element_type=F32
    )


def aligned(index, size):
    return pl.ds(pl.multiple_of(index * size, size), size)


def placed_for(array):
    if array.ndim == 2 or array.ndim == 4 and array.size > LARGE:
        return pltpu.with_memory_space_constraint(array, pltpu.HBM)
    return array


def call(kernel, name, ids, grid, inputs, held, outputs, scratch=(), after=()):
    places = sorted(held)
    extra = [held[place] for place in places] + list(after)
    taken = len(inputs)

    def body(ids_ref, *refs):
        kernel(ids_ref, *refs[:taken], *refs[taken + len(extra) :])

    return pl.pallas_call(
        body,
        grid_spec=pltpu.PrefetchScalarGridSpec(
            num_scalar_prefetch=1,
            grid=grid,
            in_specs=[spec for _, spec in inputs] + [pl.BlockSpec(memory_space=pl.ANY)] * len(extra),
            out_specs=[spec for _, _, spec in outputs],
            scratch_shapes=list(scratch),
        ),
        out_shape=[jax.ShapeDtypeStruct(shape, dtype) for shape, dtype, _ in outputs],
        input_output_aliases={1 + taken + at: place for at, place in enumerate(places)},
        compiler_params=pltpu.CompilerParams(
            dimension_semantics=("arbitrary",) * len(grid), vmem_limit_bytes=VMEM
        ),
        cost_estimate=pl.CostEstimate(flops=1, bytes_accessed=1, transcendentals=0),
        name=name,
    )(ids, *[placed_for(array) for array, _ in inputs], *extra)


class Whole:
    def __init__(self, arrays, slots, relative, lanes=None):
        self.arrays, self.slots, self.relative = arrays, slots, relative
        self.cols, self.lane = lanes or (arrays[0].shape[3], 0)

    def specs(self, count, at):
        return [
            (
                array,
                pl.BlockSpec(
                    (array.shape[0], count, array.shape[2], self.cols),
                    lambda step, _: (0, at(step), 0, self.lane),
                ),
            )
            for array in self.arrays
        ]

    def load(self, refs, block, target, device):
        if not self.relative:
            return refs[0][:, block].reshape(target.shape)
        for ref, slots in zip(refs, self.slots):
            rows = ref.shape[2]
            for place, slot in enumerate(slots):
                target[aligned(lax.bitwise_xor(device, slot), rows), :] = ref[place, block]
        return target[...]


def combos(bits):
    found = [0]
    for bit in bits:
        found += [value | bit for value in found]
    return found


class Network:
    def __init__(self, size):
        bits = [1 << k for k in range(size.bit_length() - 1)]
        self.size = size
        self.near, self.far = bits[:2], bits[2:]
        self.rounds = [(bit,) for bit in bits]
        self.order = [0]
        for bits in reversed(self.rounds):
            self.order = [slot | mask for mask in combos(bits) for slot in self.order]

    def swap(self, array, mask):
        return lax.ppermute(array, "dp", [(at, at ^ mask) for at in range(self.size)])

    def gather(self, shard):
        combo = combos(self.far)
        first = [shard[None]] + [self.swap(shard[None], mask) for mask in combo[1:]]
        have = [(jnp.concatenate(first, axis=0), combo)]
        for mask in reversed(self.near):
            have = have + [(self.swap(array, mask), [slot | mask for slot in slots]) for array, slots in have]
        return Whole([array for array, _ in have], [slots for _, slots in have], True)

    def cut(self, slots, bits):
        mask = sum(bits)
        return [[slot for slot in slots if slot & mask == value] for value in combos(bits)]

    def first_cut(self):
        return self.cut(self.order, self.rounds[0])

    def scatter(self, parts, scale, joined=False):
        rounds = self.rounds[: len(self.near)] + [tuple(self.far)] if joined else self.rounds
        slots = self.first_cut()[0]
        terms, sends, marks = [parts[0]], parts[1:], []
        for step, bits in enumerate(rounds):
            marks.append(sends)
            terms += [self.swap(piece, mask) for piece, mask in zip(sends, combos(bits)[1:])]
            if step + 1 < len(rounds):
                lists = self.cut(slots, rounds[step + 1])
                spans = [(slots.index(members[0]), slots.index(members[-1]) + 1) for members in lists]
                sends = [sum(term[lo:hi].astype(F32) for term in terms).astype(BF16) for lo, hi in spans[1:]]
                terms = [term[spans[0][0] : spans[0][1]] for term in terms]
                slots = lists[0]
        result = sum(term[0].astype(F32) for term in terms) * scale
        return result, marks + [[result]]


def tiles(array, rows, cols, down, along, at):
    return [
        (
            array,
            pl.BlockSpec(
                (rows, cols),
                functools.partial(lambda row, col, step, _: (row, along * at(step) + col), row, col),
            ),
        )
        for row in range(down)
        for col in range(along)
    ]


def expand_kernel(weights, shifts, spans, group, inner, ids, *rest):
    x_refs, rest = rest[:4], rest[4:]
    w_refs, rest = rest[: len(weights.arrays)], rest[len(weights.arrays) :]
    outs, held = rest[:-1], rest[-1]
    blk = held.shape[1]
    halves = []
    for half in range(2):
        weight = weights.load(w_refs, half, held.at[half], ids[1])
        acts = jnp.concatenate([x_refs[half][...], x_refs[2 + half][...]], axis=0)
        halves.append(dot(acts, weight, 1, 0).astype(BF16).T.astype(F32))
    width = blk // group
    for at, _ in enumerate(shifts):
        parts = [
            full[at * width : (at + 1) * width].reshape(width // inner, inner, -1) for full in halves
        ]
        piece = jnp.concatenate(parts, axis=1).astype(BF16)
        for place, (start, stop) in enumerate(spans):
            outs[at * len(spans) + place][...] = piece[start:stop]


def expand(ids, tokens, weights, shifts, spans, group, local, after=()):
    tok = tokens.shape[0]
    blk = tokens.shape[1] // local
    inner = blk // (local * group)
    cols = len(shifts) * (blk // group)
    shapes = [stop - start for _ in shifts for start, stop in spans]
    return call(
        functools.partial(expand_kernel, weights, shifts, spans, group, inner),
        "expand",
        ids,
        (local // 2,),
        tiles(tokens, tok // 2, blk, 2, 2, lambda pair: pair)
        + weights.specs(2, lambda pair: pair),
        {},
        [
            (
                (count, local * inner, tok),
                BF16,
                pl.BlockSpec((count, 2 * inner, tok), lambda pair, _: (0, pair, 0)),
            )
            for count in shapes
        ],
        [pltpu.VMEM((2, blk, cols), BF16)],
        after,
    )


def order_matrix(blk, blocks, flip):
    inner = blk // blocks
    out = lax.broadcasted_iota(jnp.int32, (blk, blk), 1 if flip else 0)
    held = lax.broadcasted_iota(jnp.int32, (blk, blk), 0 if flip else 1)
    return (held == lax.rem(out, blocks) * inner + lax.div(out, blocks)).astype(F32).astype(BF16)


def store_term(term, slots_lists, relative, outs, scratch, device, block):
    if not relative:
        out = outs[0]
        out[:, block] = term.reshape(out.shape[0], out.shape[2], out.shape[3])
        return
    scratch[...] = term
    for out, slots in zip(outs, slots_lists):
        rows = out.shape[2]
        for place, slot in enumerate(slots):
            out[place, block] = scratch[aligned(lax.bitwise_xor(device, slot), rows), :].astype(out.dtype)


def mix_kernel(weights, cut, relative, group, blocks, backs, ids, own_ref, *rest):
    arrived, rest = rest[: group - 1], rest[group - 1 :]
    w_refs, rest = rest[: len(weights.arrays)], rest[len(weights.arrays) :]
    step = (len(rest) - 6 - len(cut) - len(backs) * (group - 1)) // 2
    x_refs, up_refs, rest = rest[:step], rest[step : 2 * step], rest[2 * step :]
    mixed_ref, back_own_ref = rest[:2]
    term_refs, rest = rest[2 : 2 + len(cut)], rest[2 + len(cut) :]
    back_refs, (moved, back, held, term) = rest[:-4], rest[-4:]
    me = ids[0]
    blk = held.shape[1]
    rows = blk // group
    there = order_matrix(blk, blocks, False)
    again = order_matrix(blk, blocks, True)
    for j in range(held.shape[0]):
        cols = slice(j * blk, (j + 1) * blk)
        moved[j, aligned(me, rows), :] = own_ref[j]
        for shift in range(1, group):
            moved[j, aligned(lax.rem(me - shift + group, group), rows), :] = arrived[shift - 1][j]
        weight = weights.load(w_refs, j, held.at[j], ids[1])
        ordered = dot(there, moved[j], 1, 0).astype(BF16)
        inner_out = dot(ordered.T, weight, 1, 0)
        cdf = 0.5 + 0.5 * lax.erf(inner_out * ROOT_HALF)
        mixed_ref[:, cols] = (x_refs[j][...].astype(F32) + inner_out * cdf).astype(BF16)
        slope = cdf + inner_out * (DENSITY * jnp.exp(-0.5 * inner_out * inner_out))
        grad_out = (up_refs[j][...].astype(F32) * slope).astype(BF16)
        store_term(dot(ordered, grad_out, 1, 0), cut, relative, term_refs, term.at[j], ids[1], j)
        returned = dot(weight, grad_out, 1, 1).astype(BF16)
        back[j] = dot(again, returned, 1, 0).astype(BF16)
        back_own_ref[j] = back[j, aligned(me, rows), :]
        for shift in range(1, group):
            piece = back[j, aligned(lax.rem(me + shift, group), rows), :]
            for at, (start, stop) in enumerate(backs):
                back_refs[(shift - 1) * len(backs) + at][j] = piece[start:stop]


def mix(ids, own, arrived, weights, tokens, upstream, held, span, group, local, cut, relative, term, backs):
    tok = tokens.shape[0]
    blk = tokens.shape[1] // local
    feat = blk // group
    per = feat // local
    first, last = span
    rows = blk // sum(len(slots) for slots in cut)
    step = math.gcd(2, math.gcd(first, last))
    lane = pl.BlockSpec((tok, step * blk), lambda j, _: (0, first // step + j))
    at = pl.BlockSpec((step, feat, tok), lambda j, _: (first // step + j, 0, 0))
    keys = ["mixed", "own"]
    outs = [(tokens.shape, BF16, lane), ((local, feat, tok), BF16, at)]
    term_key, (term_first, term_last) = term
    for place, slots in enumerate(cut):
        keys.append((term_key, place))
        outs.append(
            (
                (len(slots), term_last - term_first, rows, blk),
                F32 if place == 0 else BF16,
                pl.BlockSpec((len(slots), step, rows, blk), lambda j, _: (0, (first - term_first) // step + j, 0, 0)),
            )
        )
    for shift in range(1, group):
        for key, (b_first, b_last), (j_first, j_last) in backs:
            keys.append((key, shift))
            outs.append(
                (
                    (j_last - j_first, (b_last - b_first) * per, tok),
                    BF16,
                    pl.BlockSpec(
                        (step, (b_last - b_first) * per, tok),
                        functools.partial(lambda start, j, _: (start + j, 0, 0), (first - j_first) // step),
                    ),
                )
            )
    kept = {place: held[key] for place, key in enumerate(keys) if key in held}
    cuts = [(b_first * per, b_last * per) for _, (b_first, b_last), _ in backs]
    got = call(
        functools.partial(mix_kernel, weights, cut, relative, group, local * group, cuts),
        "mix",
        ids,
        ((last - first) // step,),
        [(own, at)]
        + [(array, pl.BlockSpec((step, feat, tok), lambda j, _: (j, 0, 0))) for array in arrived]
        + weights.specs(step, lambda j: first // step + j)
        + tiles(tokens, tok, blk, 1, step, lambda j: first // step + j)
        + tiles(upstream, tok, blk, 1, step, lambda j: first // step + j),
        kept,
        outs,
        [
            pltpu.VMEM((step, blk, tok), BF16),
            pltpu.VMEM((step, blk, tok), BF16),
            pltpu.VMEM((step, blk, blk), BF16),
            pltpu.VMEM((step, blk, blk), F32),
        ],
    )
    held.update(zip(keys, got))


def fold_kernel(columns, cut, relative, group, inner, pieces, ids, own_ref, *rest):
    arrived, rest = rest[: pieces * (group - 1)], rest[pieces * (group - 1) :]
    x_refs, up_refs, rest = rest[:2], rest[2:4], rest[4:]
    w_refs = []
    for weights in columns:
        w_refs.append(rest[: len(weights.arrays)])
        rest = rest[len(weights.arrays) :]
    out_ref, term_refs = rest[0], rest[1:-4]
    inner_grad, held, sorted_term, term = rest[-4:]
    me = ids[0]
    blk = held.shape[2]
    width = blk // group
    for shift in range(group):
        if shift == 0:
            piece = own_ref[...]
        else:
            refs = arrived[(shift - 1) * pieces : shift * pieces]
            piece = jnp.concatenate([ref[...] for ref in refs], axis=0)
        piece = piece.astype(F32)
        for half in range(2):
            part = piece[:, half * inner : (half + 1) * inner].reshape(width, -1)
            inner_grad[half, shift * width : (shift + 1) * width, :] = part.astype(BF16)
    for half in range(2):
        cols = slice(half * blk, (half + 1) * blk)
        if len(columns) == 1:
            weight = columns[0].load(w_refs[0], half, held.at[half], ids[1])
        else:
            start = 0
            for weights, refs in zip(columns, w_refs):
                size = weights.cols
                part = held.at[half, :, start : start + size]
                part[...] = weights.load(refs, half, part, ids[1])
                start += size
            weight = held[half]
        du = inner_grad[half]
        unsorted = dot(du, x_refs[half][...], 1, 0)
        for shift in range(group):
            source = lax.rem(me - shift + group, group)
            sorted_term[half, aligned(source, width), :] = unsorted[shift * width : (shift + 1) * width]
        store_term(sorted_term[half].T, cut, relative, term_refs, term.at[half], ids[1], half)
        back = dot(du.T, weight, 1, 1)
        out_ref[:, cols] = (up_refs[half][...].astype(F32) + back).astype(BF16)


def fold(ids, own, arrived, tokens, upstream, columns, grad_tokens, span, group, local, cut, relative, after):
    tok = tokens.shape[0]
    blk = tokens.shape[1] // local
    inner = blk // (local * group)
    first, last = span
    rows = blk // sum(len(slots) for slots in cut)
    start = first // 2
    lane = pl.BlockSpec((tok, 2 * blk), lambda pair, _: (0, start + pair))
    inputs = []
    for array, begin in [(own, 0)] + arrived:
        at = functools.partial(lambda skip, pair, _: (0, skip + pair, 0), start - begin // 2)
        inputs.append((array, pl.BlockSpec((array.shape[0], 2 * inner, tok), at)))
    for array in (tokens, upstream):
        inputs += tiles(array, tok, blk, 1, 2, lambda pair: start + pair)
    for weights in columns:
        inputs += weights.specs(2, lambda pair: start + pair)
    outs = [(tokens.shape, BF16, lane)] + [
        (
            (len(slots), last - first, rows, blk),
            F32 if place == 0 else BF16,
            pl.BlockSpec((len(slots), 2, rows, blk), lambda pair, _: (0, pair, 0, 0)),
        )
        for place, slots in enumerate(cut)
    ]
    pieces = len(arrived) // (group - 1)
    held = {} if grad_tokens is None else {0: grad_tokens}
    return call(
        functools.partial(fold_kernel, columns, cut, relative, group, inner, pieces),
        "fold",
        ids,
        ((last - first) // 2,),
        inputs,
        held,
        outs,
        [
            pltpu.VMEM((2, blk, tok), BF16),
            pltpu.VMEM((2, blk, blk), BF16),
            pltpu.VMEM((2, blk, blk), F32),
            pltpu.VMEM((2, blk, blk), F32),
        ],
        after,
    )


def send(array, shift, group):
    return lax.ppermute(array, "mp", [(at, (at + shift) % group) for at in range(group)])


def gather_plain(shard):
    local, rows, blk = shard.shape
    whole = lax.all_gather(shard, "dp", axis=0, tiled=False)
    if rows % 16:
        whole = jnp.transpose(whole, (1, 0, 2, 3)).reshape(1, local, whole.shape[0] * rows, blk)
    return Whole([whole], [list(range(whole.shape[0]))], False)


def scatter_plain(term, rows, scale):
    if term.shape[2] != rows:
        _, count, whole, blk = term.shape
        term = jnp.transpose(term.reshape(count, whole // rows, rows, blk), (1, 0, 2, 3))
    return lax.psum_scatter(term, "dp", scatter_dimension=0, tiled=False) * scale


def on_device(tokens, upstream, first_factor, second_factor):
    local, rows, blk = first_factor.shape
    group, size = lax.axis_size("mp"), lax.axis_size("dp")
    width = blk // group
    scale = 1.0 / math.sqrt(tokens.shape[0] * size)
    me, device = lax.axis_index("mp"), lax.axis_index("dp")
    ids = jnp.stack([me, device]).astype(jnp.int32)
    cube = group == 2 and size >= 8 and size & (size - 1) == 0 and rows % 16 == 0 and width % 128 == 0
    net = Network(size) if cube else None
    cut = net.first_cut() if cube else [[0]]
    plain_cut = [list(range(size))] if cube else [[0]]
    j_spans = split_by(local, (3, 3, 2)) if cube else split_even(local, 4)
    b_spans = [(2 * lo, 2 * hi) for lo, hi in split_by(local // 2, (4, 3, 1))]
    shifts = list(range(1, group))

    if cube:
        cols = [
            lax.dynamic_slice_in_dim(first_factor, lax.rem(me + shift, group) * width, width, 2)
            for shift in range(2)
        ]
        far = net.gather(cols[1])
        both = gather_plain(jnp.concatenate([second_factor, cols[0]], axis=2))
        second_whole = Whole(both.arrays, both.slots, False, (blk, 0))
        near = Whole(both.arrays, both.slots, False, (width, group))
        columns = [near, far]
    else:
        second_whole = gather_plain(second_factor)
        whole = gather_plain(first_factor).arrays[0]
        if whole.shape[0] > 1:
            whole = jnp.transpose(whole, (1, 0, 2, 3)).reshape(1, local, blk, blk)
        turned = jnp.roll(whole, -me * width, axis=3)
        near, far, turned = [
            Whole([array], [[0]], False) for array in (turned[..., :width], turned[..., width:], turned)
        ]
        columns = [turned]
    sends = expand(ids, tokens, far, shifts, j_spans, group, local)
    arrived = [
        [send(sends[(shift - 1) * len(j_spans) + at], shift, group) for shift in shifts]
        for at in range(len(j_spans))
    ]
    own = expand(ids, tokens, near, [0], [(0, local)], group, local)[0]

    held = {}
    backs = [(("back", place), b_span, (0, local)) for place, b_span in enumerate(b_spans)]
    for at, span in enumerate(j_spans):
        mix(
            ids, own, arrived[at], second_whole, tokens, upstream, held, span, group, local, cut, cube,
            ("term", (0, local)), backs,
        )
    returned = [[send(held[(key, shift)], shift, group) for shift in shifts] for key, _, _ in backs]
    parts = [held[("term", place)] for place in range(len(cut))]
    if cube:
        grad_second, marks = net.scatter(parts, scale, JOINED[0])
    else:
        grad_second, marks = scatter_plain(parts[0], rows, scale), []

    grad_tokens, sums, terms, chains = None, [], [], [marks]
    tie = lambda place: [array for chain, step in TIES.get(place, ()) if cube for array in chains[chain][step]]
    for place, b_span in enumerate(b_spans):
        grad_tokens, *parts = fold(
            ids, held["own"], [(array, b_span[0]) for array in returned[place]], tokens, upstream, columns,
            grad_tokens, b_span, group, local, cut, cube, tie(place),
        )
        if cube:
            total, marks = net.scatter(parts, scale, JOINED[1 + place])
            chains.append(marks)
            sums.append(total)
        else:
            terms.append(parts[0])
    if not cube:
        sums = [scatter_plain(jnp.concatenate(terms, axis=1), rows, scale)]
    return held["mixed"], grad_tokens, jnp.concatenate(sums), grad_second


def solution(mesh):
    placed = (P("dp", "mp"), P("dp", "mp"), P("mp", "dp", None), P("mp", "dp", None))
    return jax.shard_map(
        on_device, mesh=mesh, in_specs=placed, out_specs=placed, check_vma=False
    )
```

```python
import functools
import math

import jax
import jax.numpy as jnp
from jax import lax
from jax.experimental import pallas as pl
from jax.experimental.pallas import tpu as pltpu
from jax.sharding import PartitionSpec as P

BF16 = jnp.bfloat16
F32 = jnp.float32
ROOT_HALF = math.sqrt(0.5)
DENSITY = 1.0 / math.sqrt(2.0 * math.pi)
JOINED = (True, True, False, False)
TIES = {0: ((0, 2),), 1: ((1, 1),), 2: ((0, 3), (1, 3), (2, 2))}
VMEM = 20 * 1024 * 1024


def split_even(count, parts):
    parts = min(count, parts)
    edges = [count * step // parts for step in range(parts + 1)]
    return list(zip(edges[:-1], edges[1:]))


def split_by(count, weights):
    total, edges, run = sum(weights), [0], 0
    for weight in weights:
        run += weight
        edges.append(count * run // total)
    return [(lo, hi) for lo, hi in zip(edges[:-1], edges[1:]) if hi > lo]


def dot(left, right, left_dim, right_dim):
    return lax.dot_general(
        left, right, (((left_dim,), (right_dim,)), ((), ())), preferred_element_type=F32
    )


def aligned(index, size):
    return pl.ds(pl.multiple_of(index * size, size), size)


def outside(array):
    return pltpu.with_memory_space_constraint(array, pltpu.HBM)


def call(kernel, name, ids, grid, inputs, held, outputs, scratch=(), after=()):
    places = sorted(held)
    extra = [held[place] for place in places] + list(after)
    taken = len(inputs)

    def body(ids_ref, *refs):
        kernel(ids_ref, *refs[:taken], *refs[taken + len(extra) :])

    return pl.pallas_call(
        body,
        grid_spec=pltpu.PrefetchScalarGridSpec(
            num_scalar_prefetch=1,
            grid=grid,
            in_specs=[spec for _, spec in inputs] + [pl.BlockSpec(memory_space=pl.ANY)] * len(extra),
            out_specs=[spec for _, _, spec in outputs],
            scratch_shapes=list(scratch),
        ),
        out_shape=[jax.ShapeDtypeStruct(shape, dtype) for shape, dtype, _ in outputs],
        input_output_aliases={1 + taken + at: place for at, place in enumerate(places)},
        compiler_params=pltpu.CompilerParams(
            dimension_semantics=("arbitrary",) * len(grid), vmem_limit_bytes=VMEM
        ),
        cost_estimate=pl.CostEstimate(flops=1, bytes_accessed=1, transcendentals=0),
        name=name,
    )(ids, *[array for array, _ in inputs], *extra)


class Whole:
    def __init__(self, arrays, slots, relative, lanes=None):
        self.arrays, self.slots, self.relative = arrays, slots, relative
        self.cols, self.lane = lanes or (arrays[0].shape[3], 0)

    def specs(self, count, at):
        return [
            (
                array,
                pl.BlockSpec(
                    (array.shape[0], count, array.shape[2], self.cols),
                    lambda step, _: (0, at(step), 0, self.lane),
                ),
            )
            for array in self.arrays
        ]

    def load(self, refs, block, target, device):
        if not self.relative:
            return refs[0][:, block].reshape(target.shape)
        for ref, slots in zip(refs, self.slots):
            rows = ref.shape[2]
            for place, slot in enumerate(slots):
                target[aligned(lax.bitwise_xor(device, slot), rows), :] = ref[place, block]
        return target[...]


def combos(bits):
    found = [0]
    for bit in bits:
        found += [value | bit for value in found]
    return found


class Network:
    def __init__(self, size):
        bits = [1 << k for k in range(size.bit_length() - 1)]
        self.size = size
        self.near, self.far = bits[:2], bits[2:]
        self.rounds = [(bit,) for bit in bits]
        self.order = [0]
        for bits in reversed(self.rounds):
            self.order = [slot | mask for mask in combos(bits) for slot in self.order]

    def swap(self, array, mask):
        return lax.ppermute(array, "dp", [(at, at ^ mask) for at in range(self.size)])

    def gather(self, shard):
        combo = combos(self.far)
        first = [shard[None]] + [self.swap(shard[None], mask) for mask in combo[1:]]
        have = [(jnp.concatenate(first, axis=0), combo)]
        for mask in reversed(self.near):
            have = have + [(self.swap(array, mask), [slot | mask for slot in slots]) for array, slots in have]
        return Whole([array for array, _ in have], [slots for _, slots in have], True)

    def cut(self, slots, bits):
        mask = sum(bits)
        return [[slot for slot in slots if slot & mask == value] for value in combos(bits)]

    def first_cut(self):
        return self.cut(self.order, self.rounds[0])

    def scatter(self, parts, scale, joined=False):
        rounds = self.rounds[: len(self.near)] + [tuple(self.far)] if joined else self.rounds
        slots = self.first_cut()[0]
        terms, sends, marks = [parts[0]], parts[1:], []
        for step, bits in enumerate(rounds):
            marks.append(sends)
            terms += [self.swap(piece, mask) for piece, mask in zip(sends, combos(bits)[1:])]
            if step + 1 < len(rounds):
                lists = self.cut(slots, rounds[step + 1])
                spans = [(slots.index(members[0]), slots.index(members[-1]) + 1) for members in lists]
                sends = [sum(term[lo:hi].astype(F32) for term in terms).astype(BF16) for lo, hi in spans[1:]]
                terms = [term[spans[0][0] : spans[0][1]] for term in terms]
                slots = lists[0]
        result = sum(term[0].astype(F32) for term in terms) * scale
        return result, marks + [[result]]


def tiles(array, rows, cols, down, along, at):
    return [
        (
            array,
            pl.BlockSpec(
                (rows, cols),
                functools.partial(lambda row, col, step, _: (row, along * at(step) + col), row, col),
            ),
        )
        for row in range(down)
        for col in range(along)
    ]


def expand_kernel(weights, shifts, spans, group, inner, keep, ids, *rest):
    x_refs, rest = rest[:4], rest[4:]
    w_refs, rest = rest[: len(weights.arrays)], rest[len(weights.arrays) :]
    outs, held = rest[:-1], rest[-1]
    blk = held.shape[1]
    halves = []
    for half in range(2):
        weight = weights.load(w_refs, half, held.at[half], ids[1])
        acts = jnp.concatenate([x_refs[half][...], x_refs[2 + half][...]], axis=0)
        if keep:
            outs[-1][:, half * blk : (half + 1) * blk] = acts
        halves.append(dot(acts, weight, 1, 0).astype(BF16).T.astype(F32))
    width = blk // group
    for at, _ in enumerate(shifts):
        parts = [
            full[at * width : (at + 1) * width].reshape(width // inner, inner, -1) for full in halves
        ]
        piece = jnp.concatenate(parts, axis=1).astype(BF16)
        for place, (start, stop) in enumerate(spans):
            outs[at * len(spans) + place][...] = piece[start:stop]


def expand(ids, tokens, weights, shifts, spans, group, local, keep):
    tok = tokens.shape[0]
    blk = tokens.shape[1] // local
    inner = blk // (local * group)
    cols = len(shifts) * (blk // group)
    shapes = [stop - start for _ in shifts for start, stop in spans]
    return call(
        functools.partial(expand_kernel, weights, shifts, spans, group, inner, keep),
        "expand",
        ids,
        (local // 2,),
        tiles(tokens, tok // 2, blk, 2, 2, lambda pair: pair)
        + weights.specs(2, lambda pair: pair),
        {},
        [
            (
                (count, local * inner, tok),
                BF16,
                pl.BlockSpec((count, 2 * inner, tok), lambda pair, _: (0, pair, 0)),
            )
            for count in shapes
        ]
        + [(tokens.shape, BF16, pl.BlockSpec((tok, 2 * blk), lambda pair, _: (0, pair)))] * keep,
        [pltpu.VMEM((2, blk, cols), BF16)],
    )


def order_matrix(blk, blocks, flip):
    inner = blk // blocks
    out = lax.broadcasted_iota(jnp.int32, (blk, blk), 1 if flip else 0)
    held = lax.broadcasted_iota(jnp.int32, (blk, blk), 0 if flip else 1)
    return (held == lax.rem(out, blocks) * inner + lax.div(out, blocks)).astype(F32).astype(BF16)


def store_term(term, slots_lists, relative, outs, scratch, device, block):
    if not relative:
        out = outs[0]
        out[:, block] = term.reshape(out.shape[0], out.shape[2], out.shape[3])
        return
    scratch[...] = term
    for out, slots in zip(outs, slots_lists):
        rows = out.shape[2]
        for place, slot in enumerate(slots):
            out[place, block] = scratch[aligned(lax.bitwise_xor(device, slot), rows), :].astype(out.dtype)


def mix_kernel(weights, cut, relative, group, blocks, backs, ids, own_ref, *rest):
    arrived, rest = rest[: group - 1], rest[group - 1 :]
    w_refs, rest = rest[: len(weights.arrays)], rest[len(weights.arrays) :]
    step = (len(rest) - 6 - len(cut) - len(backs) * (group - 1)) // 2
    x_refs, up_refs, rest = rest[:step], rest[step : 2 * step], rest[2 * step :]
    mixed_ref, back_own_ref = rest[:2]
    term_refs, rest = rest[2 : 2 + len(cut)], rest[2 + len(cut) :]
    back_refs, (moved, back, held, term) = rest[:-4], rest[-4:]
    me = ids[0]
    blk = held.shape[1]
    rows = blk // group
    there = order_matrix(blk, blocks, False)
    again = order_matrix(blk, blocks, True)
    for j in range(held.shape[0]):
        cols = slice(j * blk, (j + 1) * blk)
        moved[j, aligned(me, rows), :] = own_ref[j]
        for shift in range(1, group):
            moved[j, aligned(lax.rem(me - shift + group, group), rows), :] = arrived[shift - 1][j]
        weight = weights.load(w_refs, j, held.at[j], ids[1])
        ordered = dot(there, moved[j], 1, 0).astype(BF16)
        inner_out = dot(ordered.T, weight, 1, 0)
        cdf = 0.5 + 0.5 * lax.erf(inner_out * ROOT_HALF)
        mixed_ref[:, cols] = (x_refs[j][...].astype(F32) + inner_out * cdf).astype(BF16)
        slope = cdf + inner_out * (DENSITY * jnp.exp(-0.5 * inner_out * inner_out))
        grad_out = (up_refs[j][...].astype(F32) * slope).astype(BF16)
        store_term(dot(ordered, grad_out, 1, 0), cut, relative, term_refs, term.at[j], ids[1], j)
        returned = dot(weight, grad_out, 1, 1).astype(BF16)
        back[j] = dot(again, returned, 1, 0).astype(BF16)
        back_own_ref[j] = back[j, aligned(me, rows), :]
        for shift in range(1, group):
            piece = back[j, aligned(lax.rem(me + shift, group), rows), :]
            for at, (start, stop) in enumerate(backs):
                back_refs[(shift - 1) * len(backs) + at][j] = piece[start:stop]


def mix(ids, own, arrived, weights, tokens, upstream, held, span, group, local, cut, relative, term, backs):
    tok = tokens.shape[0]
    blk = tokens.shape[1] // local
    feat = blk // group
    per = feat // local
    first, last = span
    rows = blk // sum(len(slots) for slots in cut)
    step = math.gcd(2, math.gcd(first, last))
    lane = pl.BlockSpec((tok, step * blk), lambda j, _: (0, first // step + j))
    at = pl.BlockSpec((step, feat, tok), lambda j, _: (first // step + j, 0, 0))
    keys = ["mixed", "own"]
    outs = [(tokens.shape, BF16, lane), ((local, feat, tok), BF16, at)]
    term_key, (term_first, term_last) = term
    for place, slots in enumerate(cut):
        keys.append((term_key, place))
        outs.append(
            (
                (len(slots), term_last - term_first, rows, blk),
                F32 if place == 0 else BF16,
                pl.BlockSpec((len(slots), step, rows, blk), lambda j, _: (0, (first - term_first) // step + j, 0, 0)),
            )
        )
    for shift in range(1, group):
        for key, (b_first, b_last), (j_first, j_last) in backs:
            keys.append((key, shift))
            outs.append(
                (
                    (j_last - j_first, (b_last - b_first) * per, tok),
                    BF16,
                    pl.BlockSpec(
                        (step, (b_last - b_first) * per, tok),
                        functools.partial(lambda start, j, _: (start + j, 0, 0), (first - j_first) // step),
                    ),
                )
            )
    kept = {place: held[key] for place, key in enumerate(keys) if key in held}
    cuts = [(b_first * per, b_last * per) for _, (b_first, b_last), _ in backs]
    got = call(
        functools.partial(mix_kernel, weights, cut, relative, group, local * group, cuts),
        "mix",
        ids,
        ((last - first) // step,),
        [(own, at)]
        + [(array, pl.BlockSpec((step, feat, tok), lambda j, _: (j, 0, 0))) for array in arrived]
        + weights.specs(step, lambda j: first // step + j)
        + tiles(tokens, tok, blk, 1, step, lambda j: first // step + j)
        + tiles(upstream, tok, blk, 1, step, lambda j: first // step + j),
        kept,
        outs,
        [
            pltpu.VMEM((step, blk, tok), BF16),
            pltpu.VMEM((step, blk, tok), BF16),
            pltpu.VMEM((step, blk, blk), BF16),
            pltpu.VMEM((step, blk, blk), F32),
        ],
    )
    held.update(zip(keys, got))


def fold_kernel(columns, cut, relative, group, inner, pieces, ids, own_ref, *rest):
    arrived, rest = rest[: pieces * (group - 1)], rest[pieces * (group - 1) :]
    x_refs, up_refs, rest = rest[:2], rest[2:4], rest[4:]
    w_refs = []
    for weights in columns:
        w_refs.append(rest[: len(weights.arrays)])
        rest = rest[len(weights.arrays) :]
    out_ref, term_refs = rest[0], rest[1:-4]
    inner_grad, held, sorted_term, term = rest[-4:]
    me = ids[0]
    blk = held.shape[2]
    width = blk // group
    for shift in range(group):
        if shift == 0:
            piece = own_ref[...]
        else:
            refs = arrived[(shift - 1) * pieces : shift * pieces]
            piece = jnp.concatenate([ref[...] for ref in refs], axis=0)
        piece = piece.astype(F32)
        for half in range(2):
            part = piece[:, half * inner : (half + 1) * inner].reshape(width, -1)
            inner_grad[half, shift * width : (shift + 1) * width, :] = part.astype(BF16)
    for half in range(2):
        cols = slice(half * blk, (half + 1) * blk)
        if len(columns) == 1:
            weight = columns[0].load(w_refs[0], half, held.at[half], ids[1])
        else:
            start = 0
            for weights, refs in zip(columns, w_refs):
                size = weights.cols
                part = held.at[half, :, start : start + size]
                part[...] = weights.load(refs, half, part, ids[1])
                start += size
            weight = held[half]
        du = inner_grad[half]
        unsorted = dot(du, x_refs[half][...], 1, 0)
        for shift in range(group):
            source = lax.rem(me - shift + group, group)
            sorted_term[half, aligned(source, width), :] = unsorted[shift * width : (shift + 1) * width]
        store_term(sorted_term[half].T, cut, relative, term_refs, term.at[half], ids[1], half)
        back = dot(du.T, weight, 1, 1)
        out_ref[:, cols] = (up_refs[half][...].astype(F32) + back).astype(BF16)


def fold(ids, own, arrived, tokens, upstream, columns, grad_tokens, span, group, local, cut, relative, after):
    tok = tokens.shape[0]
    blk = tokens.shape[1] // local
    inner = blk // (local * group)
    first, last = span
    rows = blk // sum(len(slots) for slots in cut)
    start = first // 2
    lane = pl.BlockSpec((tok, 2 * blk), lambda pair, _: (0, start + pair))
    inputs = []
    for array, begin in [(own, 0)] + arrived:
        at = functools.partial(lambda skip, pair, _: (0, skip + pair, 0), start - begin // 2)
        inputs.append((array, pl.BlockSpec((array.shape[0], 2 * inner, tok), at)))
    for array in (tokens, upstream):
        inputs += tiles(array, tok, blk, 1, 2, lambda pair: start + pair)
    for weights in columns:
        inputs += weights.specs(2, lambda pair: start + pair)
    outs = [(tokens.shape, BF16, lane)] + [
        (
            (len(slots), last - first, rows, blk),
            F32 if place == 0 else BF16,
            pl.BlockSpec((len(slots), 2, rows, blk), lambda pair, _: (0, pair, 0, 0)),
        )
        for place, slots in enumerate(cut)
    ]
    pieces = len(arrived) // (group - 1)
    held = {} if grad_tokens is None else {0: grad_tokens}
    return call(
        functools.partial(fold_kernel, columns, cut, relative, group, inner, pieces),
        "fold",
        ids,
        ((last - first) // 2,),
        inputs,
        held,
        outs,
        [
            pltpu.VMEM((2, blk, tok), BF16),
            pltpu.VMEM((2, blk, blk), BF16),
            pltpu.VMEM((2, blk, blk), F32),
            pltpu.VMEM((2, blk, blk), F32),
        ],
        after,
    )


def send(array, shift, group):
    return lax.ppermute(array, "mp", [(at, (at + shift) % group) for at in range(group)])


def gather_plain(shard):
    local, rows, blk = shard.shape
    whole = lax.all_gather(shard, "dp", axis=0, tiled=False)
    if rows % 16:
        whole = jnp.transpose(whole, (1, 0, 2, 3)).reshape(1, local, whole.shape[0] * rows, blk)
    return Whole([whole], [list(range(whole.shape[0]))], False)


def scatter_plain(term, rows, scale):
    if term.shape[2] != rows:
        _, count, whole, blk = term.shape
        term = jnp.transpose(term.reshape(count, whole // rows, rows, blk), (1, 0, 2, 3))
    return lax.psum_scatter(term, "dp", scatter_dimension=0, tiled=False) * scale


def on_device(tokens, upstream, first_factor, second_factor):
    local, rows, blk = first_factor.shape
    group, size = lax.axis_size("mp"), lax.axis_size("dp")
    width = blk // group
    scale = 1.0 / math.sqrt(tokens.shape[0] * size)
    me, device = lax.axis_index("mp"), lax.axis_index("dp")
    ids = jnp.stack([me, device]).astype(jnp.int32)
    cube = group == 2 and size >= 8 and size & (size - 1) == 0 and rows % 16 == 0 and width % 128 == 0
    net = Network(size) if cube else None
    cut = net.first_cut() if cube else [[0]]
    plain_cut = [list(range(size))] if cube else [[0]]
    j_spans = split_by(local, (3, 3, 2)) if cube else split_even(local, 4)
    b_spans = [(2 * lo, 2 * hi) for lo, hi in split_by(local // 2, (3, 3, 2))]
    shifts = list(range(1, group))

    if cube:
        cols = [
            lax.dynamic_slice_in_dim(first_factor, lax.rem(me + shift, group) * width, width, 2)
            for shift in range(2)
        ]
        far = net.gather(cols[1])
        both = gather_plain(jnp.concatenate([second_factor, cols[0]], axis=2))
        both.arrays = [outside(array) for array in both.arrays]
        second_whole = Whole(both.arrays, both.slots, False, (blk, 0))
        near = Whole(both.arrays, both.slots, False, (width, group))
        columns = [near, far]
    else:
        second_whole = gather_plain(second_factor)
        whole = gather_plain(first_factor).arrays[0]
        if whole.shape[0] > 1:
            whole = jnp.transpose(whole, (1, 0, 2, 3)).reshape(1, local, blk, blk)
        turned = jnp.roll(whole, -me * width, axis=3)
        near, far, turned = [
            Whole([array], [[0]], False) for array in (turned[..., :width], turned[..., width:], turned)
        ]
        columns = [turned]
    tokens, upstream = outside(tokens), outside(upstream)
    *sends, tokens = expand(ids, tokens, far, shifts, j_spans, group, local, True)
    arrived = [
        [send(sends[(shift - 1) * len(j_spans) + at], shift, group) for shift in shifts]
        for at in range(len(j_spans))
    ]
    own = expand(ids, tokens, near, [0], [(0, local)], group, local, False)[0]

    held = {}
    backs = [(("back", place), b_span, (0, local)) for place, b_span in enumerate(b_spans)]
    for at, span in enumerate(j_spans):
        mix(
            ids, own, arrived[at], second_whole, tokens, upstream, held, span, group, local, cut, cube,
            ("term", (0, local)), backs,
        )
    returned = [[send(held[(key, shift)], shift, group) for shift in shifts] for key, _, _ in backs]
    parts = [held[("term", place)] for place in range(len(cut))]
    if cube:
        grad_second, marks = net.scatter(parts, scale, JOINED[0])
    else:
        grad_second, marks = scatter_plain(parts[0], rows, scale), []

    grad_tokens, sums, terms, chains = None, [], [], [marks]
    tie = lambda place: [array for chain, step in TIES.get(place, ()) if cube for array in chains[chain][step]]
    for place, b_span in enumerate(b_spans):
        grad_tokens, *parts = fold(
            ids, held["own"], [(array, b_span[0]) for array in returned[place]], tokens, upstream, columns,
            grad_tokens, b_span, group, local, cut, cube, tie(place),
        )
        if cube:
            total, marks = net.scatter(parts, scale, JOINED[1 + place])
            chains.append(marks)
            sums.append(total)
        else:
            terms.append(parts[0])
    if not cube:
        sums = [scatter_plain(jnp.concatenate(terms, axis=1), rows, scale)]
    return held["mixed"], grad_tokens, jnp.concatenate(sums), grad_second


def solution(mesh):
    placed = (P("dp", "mp"), P("dp", "mp"), P("mp", "dp", None), P("mp", "dp", None))
    return jax.shard_map(
        on_device, mesh=mesh, in_specs=placed, out_specs=placed, check_vma=False
    )
```

```python
import functools
import math

import jax
import jax.numpy as jnp
from jax import lax
from jax.experimental import pallas as pl
from jax.experimental.pallas import tpu as pltpu
from jax.sharding import PartitionSpec as P

BF16 = jnp.bfloat16
F32 = jnp.float32
ROOT_HALF = math.sqrt(0.5)
DENSITY = 1.0 / math.sqrt(2.0 * math.pi)
JOINED = (True, False, False, False)
TIES = {0: ((0, 2),), 1: ((1, 1),), 2: ((0, 3), (1, 3), (2, 2))}
VMEM = 20 * 1024 * 1024
LARGE = 1 << 20


def split_even(count, parts):
    parts = min(count, parts)
    edges = [count * step // parts for step in range(parts + 1)]
    return list(zip(edges[:-1], edges[1:]))


def split_by(count, weights):
    total, edges, run = sum(weights), [0], 0
    for weight in weights:
        run += weight
        edges.append(count * run // total)
    return [(lo, hi) for lo, hi in zip(edges[:-1], edges[1:]) if hi > lo]


def dot(left, right, left_dim, right_dim):
    return lax.dot_general(
        left, right, (((left_dim,), (right_dim,)), ((), ())), preferred_element_type=F32
    )


def aligned(index, size):
    return pl.ds(pl.multiple_of(index * size, size), size)


def placed_for(array):
    if array.ndim == 2 or array.ndim == 4 and array.size > LARGE:
        return pltpu.with_memory_space_constraint(array, pltpu.HBM)
    return array


def call(kernel, name, ids, grid, inputs, held, outputs, scratch=(), after=()):
    places = sorted(held)
    extra = [held[place] for place in places] + list(after)
    taken = len(inputs)

    def body(ids_ref, *refs):
        kernel(ids_ref, *refs[:taken], *refs[taken + len(extra) :])

    return pl.pallas_call(
        body,
        grid_spec=pltpu.PrefetchScalarGridSpec(
            num_scalar_prefetch=1,
            grid=grid,
            in_specs=[spec for _, spec in inputs] + [pl.BlockSpec(memory_space=pl.ANY)] * len(extra),
            out_specs=[spec for _, _, spec in outputs],
            scratch_shapes=list(scratch),
        ),
        out_shape=[jax.ShapeDtypeStruct(shape, dtype) for shape, dtype, _ in outputs],
        input_output_aliases={1 + taken + at: place for at, place in enumerate(places)},
        compiler_params=pltpu.CompilerParams(
            dimension_semantics=("arbitrary",) * len(grid), vmem_limit_bytes=VMEM
        ),
        cost_estimate=pl.CostEstimate(flops=1, bytes_accessed=1, transcendentals=0),
        name=name,
    )(ids, *[placed_for(array) for array, _ in inputs], *extra)


class Whole:
    def __init__(self, arrays, slots, relative, lanes=None):
        self.arrays, self.slots, self.relative = arrays, slots, relative
        self.cols, self.lane = lanes or (arrays[0].shape[3], 0)

    def specs(self, count, at):
        return [
            (
                array,
                pl.BlockSpec(
                    (array.shape[0], count, array.shape[2], self.cols),
                    lambda step, _: (0, at(step), 0, self.lane),
                ),
            )
            for array in self.arrays
        ]

    def load(self, refs, block, target, device):
        if not self.relative:
            return refs[0][:, block].reshape(target.shape)
        for ref, slots in zip(refs, self.slots):
            rows = ref.shape[2]
            for place, slot in enumerate(slots):
                target[aligned(lax.bitwise_xor(device, slot), rows), :] = ref[place, block]
        return target[...]


def combos(bits):
    found = [0]
    for bit in bits:
        found += [value | bit for value in found]
    return found


class Network:
    def __init__(self, size):
        bits = [1 << k for k in range(size.bit_length() - 1)]
        self.size = size
        self.near, self.far = bits[:2], bits[2:]
        self.rounds = [(bit,) for bit in bits]
        self.order = [0]
        for bits in reversed(self.rounds):
            self.order = [slot | mask for mask in combos(bits) for slot in self.order]

    def swap(self, array, mask):
        return lax.ppermute(array, "dp", [(at, at ^ mask) for at in range(self.size)])

    def gather(self, shard):
        combo = combos(self.far)
        first = [shard[None]] + [self.swap(shard[None], mask) for mask in combo[1:]]
        have = [(jnp.concatenate(first, axis=0), combo)]
        for mask in reversed(self.near):
            have = have + [(self.swap(array, mask), [slot | mask for slot in slots]) for array, slots in have]
        return Whole([array for array, _ in have], [slots for _, slots in have], True)

    def cut(self, slots, bits):
        mask = sum(bits)
        return [[slot for slot in slots if slot & mask == value] for value in combos(bits)]

    def first_cut(self):
        return self.cut(self.order, self.rounds[0])

    def scatter(self, parts, scale, joined=False):
        rounds = self.rounds[: len(self.near)] + [tuple(self.far)] if joined else self.rounds
        slots = self.first_cut()[0]
        terms, sends, marks = [parts[0]], parts[1:], []
        for step, bits in enumerate(rounds):
            marks.append(sends)
            terms += [self.swap(piece, mask) for piece, mask in zip(sends, combos(bits)[1:])]
            if step + 1 < len(rounds):
                lists = self.cut(slots, rounds[step + 1])
                spans = [(slots.index(members[0]), slots.index(members[-1]) + 1) for members in lists]
                sends = [sum(term[lo:hi].astype(F32) for term in terms).astype(BF16) for lo, hi in spans[1:]]
                terms = [term[spans[0][0] : spans[0][1]] for term in terms]
                slots = lists[0]
        result = sum(term[0].astype(F32) for term in terms) * scale
        return result, marks + [[result]]


def tiles(array, rows, cols, down, along, at):
    return [
        (
            array,
            pl.BlockSpec(
                (rows, cols),
                functools.partial(lambda row, col, step, _: (row, along * at(step) + col), row, col),
            ),
        )
        for row in range(down)
        for col in range(along)
    ]


def expand_kernel(weights, shifts, spans, group, inner, ids, *rest):
    x_refs, rest = rest[:2], rest[2:]
    w_refs, rest = rest[: len(weights.arrays)], rest[len(weights.arrays) :]
    outs, held = rest[:-1], rest[-1]
    blk = held.shape[1]
    halves = []
    for half in range(2):
        weight = weights.load(w_refs, half, held.at[half], ids[1])
        halves.append(dot(x_refs[half][...], weight, 1, 0).astype(BF16).T.astype(F32))
    width = blk // group
    for at, _ in enumerate(shifts):
        parts = [
            full[at * width : (at + 1) * width].reshape(width // inner, inner, -1) for full in halves
        ]
        piece = jnp.concatenate(parts, axis=1).astype(BF16)
        for place, (start, stop) in enumerate(spans):
            outs[at * len(spans) + place][...] = piece[start:stop]


def expand(ids, tokens, weights, shifts, spans, group, local, after=()):
    tok = tokens.shape[0]
    blk = tokens.shape[1] // local
    inner = blk // (local * group)
    cols = len(shifts) * (blk // group)
    shapes = [stop - start for _ in shifts for start, stop in spans]
    return call(
        functools.partial(expand_kernel, weights, shifts, spans, group, inner),
        "expand",
        ids,
        (local // 2,),
        tiles(tokens, tok, blk, 1, 2, lambda pair: pair)
        + weights.specs(2, lambda pair: pair),
        {},
        [
            (
                (count, local * inner, tok),
                BF16,
                pl.BlockSpec((count, 2 * inner, tok), lambda pair, _: (0, pair, 0)),
            )
            for count in shapes
        ],
        [pltpu.VMEM((2, blk, cols), BF16)],
        after,
    )


def order_matrix(blk, blocks, flip):
    inner = blk // blocks
    out = lax.broadcasted_iota(jnp.int32, (blk, blk), 1 if flip else 0)
    held = lax.broadcasted_iota(jnp.int32, (blk, blk), 0 if flip else 1)
    return (held == lax.rem(out, blocks) * inner + lax.div(out, blocks)).astype(F32).astype(BF16)


def store_term(term, slots_lists, relative, outs, scratch, device, block):
    if not relative:
        out = outs[0]
        out[:, block] = term.reshape(out.shape[0], out.shape[2], out.shape[3])
        return
    scratch[...] = term
    for out, slots in zip(outs, slots_lists):
        rows = out.shape[2]
        for place, slot in enumerate(slots):
            out[place, block] = scratch[aligned(lax.bitwise_xor(device, slot), rows), :].astype(out.dtype)


def mix_kernel(weights, cut, relative, group, blocks, backs, ids, own_ref, *rest):
    arrived, rest = rest[: group - 1], rest[group - 1 :]
    w_refs, rest = rest[: len(weights.arrays)], rest[len(weights.arrays) :]
    step = (len(rest) - 6 - len(cut) - len(backs) * (group - 1)) // 2
    x_refs, up_refs, rest = rest[:step], rest[step : 2 * step], rest[2 * step :]
    mixed_ref, back_own_ref = rest[:2]
    term_refs, rest = rest[2 : 2 + len(cut)], rest[2 + len(cut) :]
    back_refs, (moved, back, held, term) = rest[:-4], rest[-4:]
    me = ids[0]
    blk = held.shape[1]
    rows = blk // group
    there = order_matrix(blk, blocks, False)
    again = order_matrix(blk, blocks, True)
    for j in range(held.shape[0]):
        cols = slice(j * blk, (j + 1) * blk)
        moved[j, aligned(me, rows), :] = own_ref[j]
        for shift in range(1, group):
            moved[j, aligned(lax.rem(me - shift + group, group), rows), :] = arrived[shift - 1][j]
        weight = weights.load(w_refs, j, held.at[j], ids[1])
        ordered = dot(there, moved[j], 1, 0).astype(BF16)
        inner_out = dot(ordered.T, weight, 1, 0)
        cdf = 0.5 + 0.5 * lax.erf(inner_out * ROOT_HALF)
        mixed_ref[:, cols] = (x_refs[j][...].astype(F32) + inner_out * cdf).astype(BF16)
        slope = cdf + inner_out * (DENSITY * jnp.exp(-0.5 * inner_out * inner_out))
        grad_out = (up_refs[j][...].astype(F32) * slope).astype(BF16)
        store_term(dot(ordered, grad_out, 1, 0), cut, relative, term_refs, term.at[j], ids[1], j)
        returned = dot(weight, grad_out, 1, 1).astype(BF16)
        back[j] = dot(again, returned, 1, 0).astype(BF16)
        back_own_ref[j] = back[j, aligned(me, rows), :]
        for shift in range(1, group):
            piece = back[j, aligned(lax.rem(me + shift, group), rows), :]
            for at, (start, stop) in enumerate(backs):
                back_refs[(shift - 1) * len(backs) + at][j] = piece[start:stop]


def mix(ids, own, arrived, weights, tokens, upstream, held, span, group, local, cut, relative, term, backs):
    tok = tokens.shape[0]
    blk = tokens.shape[1] // local
    feat = blk // group
    per = feat // local
    first, last = span
    rows = blk // sum(len(slots) for slots in cut)
    step = math.gcd(2, math.gcd(first, last))
    lane = pl.BlockSpec((tok, step * blk), lambda j, _: (0, first // step + j))
    at = pl.BlockSpec((step, feat, tok), lambda j, _: (first // step + j, 0, 0))
    keys = ["mixed", "own"]
    outs = [(tokens.shape, BF16, lane), ((local, feat, tok), BF16, at)]
    term_key, (term_first, term_last) = term
    for place, slots in enumerate(cut):
        keys.append((term_key, place))
        outs.append(
            (
                (len(slots), term_last - term_first, rows, blk),
                F32 if place == 0 else BF16,
                pl.BlockSpec((len(slots), step, rows, blk), lambda j, _: (0, (first - term_first) // step + j, 0, 0)),
            )
        )
    for shift in range(1, group):
        for key, (b_first, b_last), (j_first, j_last) in backs:
            keys.append((key, shift))
            outs.append(
                (
                    (j_last - j_first, (b_last - b_first) * per, tok),
                    BF16,
                    pl.BlockSpec(
                        (step, (b_last - b_first) * per, tok),
                        functools.partial(lambda start, j, _: (start + j, 0, 0), (first - j_first) // step),
                    ),
                )
            )
    kept = {place: held[key] for place, key in enumerate(keys) if key in held}
    cuts = [(b_first * per, b_last * per) for _, (b_first, b_last), _ in backs]
    got = call(
        functools.partial(mix_kernel, weights, cut, relative, group, local * group, cuts),
        "mix",
        ids,
        ((last - first) // step,),
        [(own, at)]
        + [(array, pl.BlockSpec((step, feat, tok), lambda j, _: (j, 0, 0))) for array in arrived]
        + weights.specs(step, lambda j: first // step + j)
        + tiles(tokens, tok, blk, 1, step, lambda j: first // step + j)
        + tiles(upstream, tok, blk, 1, step, lambda j: first // step + j),
        kept,
        outs,
        [
            pltpu.VMEM((step, blk, tok), BF16),
            pltpu.VMEM((step, blk, tok), BF16),
            pltpu.VMEM((step, blk, blk), BF16),
            pltpu.VMEM((step, blk, blk), F32),
        ],
    )
    held.update(zip(keys, got))


def fold_kernel(columns, cut, relative, group, inner, pieces, ids, own_ref, *rest):
    arrived, rest = rest[: pieces * (group - 1)], rest[pieces * (group - 1) :]
    x_refs, up_refs, rest = rest[:2], rest[2:4], rest[4:]
    w_refs = []
    for weights in columns:
        w_refs.append(rest[: len(weights.arrays)])
        rest = rest[len(weights.arrays) :]
    out_ref, term_refs = rest[0], rest[1:-4]
    inner_grad, held, sorted_term, term = rest[-4:]
    me = ids[0]
    blk = held.shape[2]
    width = blk // group
    for shift in range(group):
        if shift == 0:
            piece = own_ref[...]
        else:
            refs = arrived[(shift - 1) * pieces : shift * pieces]
            piece = jnp.concatenate([ref[...] for ref in refs], axis=0)
        piece = piece.astype(F32)
        for half in range(2):
            part = piece[:, half * inner : (half + 1) * inner].reshape(width, -1)
            inner_grad[half, shift * width : (shift + 1) * width, :] = part.astype(BF16)
    for half in range(2):
        cols = slice(half * blk, (half + 1) * blk)
        if len(columns) == 1:
            weight = columns[0].load(w_refs[0], half, held.at[half], ids[1])
        else:
            start = 0
            for weights, refs in zip(columns, w_refs):
                size = weights.cols
                part = held.at[half, :, start : start + size]
                part[...] = weights.load(refs, half, part, ids[1])
                start += size
            weight = held[half]
        du = inner_grad[half]
        unsorted = dot(du, x_refs[half][...], 1, 0)
        for shift in range(group):
            source = lax.rem(me - shift + group, group)
            sorted_term[half, aligned(source, width), :] = unsorted[shift * width : (shift + 1) * width]
        store_term(sorted_term[half].T, cut, relative, term_refs, term.at[half], ids[1], half)
        back = dot(du.T, weight, 1, 1)
        out_ref[:, cols] = (up_refs[half][...].astype(F32) + back).astype(BF16)


def fold(ids, own, arrived, tokens, upstream, columns, grad_tokens, span, group, local, cut, relative, after):
    tok = tokens.shape[0]
    blk = tokens.shape[1] // local
    inner = blk // (local * group)
    first, last = span
    rows = blk // sum(len(slots) for slots in cut)
    start = first // 2
    lane = pl.BlockSpec((tok, 2 * blk), lambda pair, _: (0, start + pair))
    inputs = []
    for array, begin in [(own, 0)] + arrived:
        at = functools.partial(lambda skip, pair, _: (0, skip + pair, 0), start - begin // 2)
        inputs.append((array, pl.BlockSpec((array.shape[0], 2 * inner, tok), at)))
    for array in (tokens, upstream):
        inputs += tiles(array, tok, blk, 1, 2, lambda pair: start + pair)
    for weights in columns:
        inputs += weights.specs(2, lambda pair: start + pair)
    outs = [(tokens.shape, BF16, lane)] + [
        (
            (len(slots), last - first, rows, blk),
            F32 if place == 0 else BF16,
            pl.BlockSpec((len(slots), 2, rows, blk), lambda pair, _: (0, pair, 0, 0)),
        )
        for place, slots in enumerate(cut)
    ]
    pieces = len(arrived) // (group - 1)
    held = {} if grad_tokens is None else {0: grad_tokens}
    return call(
        functools.partial(fold_kernel, columns, cut, relative, group, inner, pieces),
        "fold",
        ids,
        ((last - first) // 2,),
        inputs,
        held,
        outs,
        [
            pltpu.VMEM((2, blk, tok), BF16),
            pltpu.VMEM((2, blk, blk), BF16),
            pltpu.VMEM((2, blk, blk), F32),
            pltpu.VMEM((2, blk, blk), F32),
        ],
        after,
    )


def send(array, shift, group):
    return lax.ppermute(array, "mp", [(at, (at + shift) % group) for at in range(group)])


def gather_plain(shard):
    local, rows, blk = shard.shape
    whole = lax.all_gather(shard, "dp", axis=0, tiled=False)
    if rows % 16:
        whole = jnp.transpose(whole, (1, 0, 2, 3)).reshape(1, local, whole.shape[0] * rows, blk)
    return Whole([whole], [list(range(whole.shape[0]))], False)


def scatter_plain(term, rows, scale):
    if term.shape[2] != rows:
        _, count, whole, blk = term.shape
        term = jnp.transpose(term.reshape(count, whole // rows, rows, blk), (1, 0, 2, 3))
    return lax.psum_scatter(term, "dp", scatter_dimension=0, tiled=False) * scale


def on_device(tokens, upstream, first_factor, second_factor):
    local, rows, blk = first_factor.shape
    group, size = lax.axis_size("mp"), lax.axis_size("dp")
    width = blk // group
    scale = 1.0 / math.sqrt(tokens.shape[0] * size)
    me, device = lax.axis_index("mp"), lax.axis_index("dp")
    ids = jnp.stack([me, device]).astype(jnp.int32)
    cube = group == 2 and size >= 8 and size & (size - 1) == 0 and rows % 16 == 0 and width % 128 == 0
    net = Network(size) if cube else None
    cut = net.first_cut() if cube else [[0]]
    plain_cut = [list(range(size))] if cube else [[0]]
    j_spans = split_by(local, (4, 3, 1)) if cube else split_even(local, 4)
    b_spans = [(2 * lo, 2 * hi) for lo, hi in split_by(local // 2, (3, 3, 2))]
    shifts = list(range(1, group))

    if cube:
        cols = [
            lax.dynamic_slice_in_dim(first_factor, lax.rem(me + shift, group) * width, width, 2)
            for shift in range(2)
        ]
        far = net.gather(cols[1])
        both = gather_plain(jnp.concatenate([second_factor, cols[0]], axis=2))
        second_whole = Whole(both.arrays, both.slots, False, (blk, 0))
        near = Whole(both.arrays, both.slots, False, (width, group))
        columns = [near, far]
    else:
        second_whole = gather_plain(second_factor)
        whole = gather_plain(first_factor).arrays[0]
        if whole.shape[0] > 1:
            whole = jnp.transpose(whole, (1, 0, 2, 3)).reshape(1, local, blk, blk)
        turned = jnp.roll(whole, -me * width, axis=3)
        near, far, turned = [
            Whole([array], [[0]], False) for array in (turned[..., :width], turned[..., width:], turned)
        ]
        columns = [turned]
    sends = expand(ids, tokens, far, shifts, j_spans, group, local)
    arrived = [
        [send(sends[(shift - 1) * len(j_spans) + at], shift, group) for shift in shifts]
        for at in range(len(j_spans))
    ]
    own = expand(ids, tokens, near, [0], [(0, local)], group, local)[0]

    held = {}
    backs = [(("back", place), b_span, (0, local)) for place, b_span in enumerate(b_spans)]
    for at, span in enumerate(j_spans):
        mix(
            ids, own, arrived[at], second_whole, tokens, upstream, held, span, group, local, cut, cube,
            ("term", (0, local)), backs,
        )
    returned = [[send(held[(key, shift)], shift, group) for shift in shifts] for key, _, _ in backs]
    parts = [held[("term", place)] for place in range(len(cut))]
    if cube:
        grad_second, marks = net.scatter(parts, scale, JOINED[0])
    else:
        grad_second, marks = scatter_plain(parts[0], rows, scale), []

    grad_tokens, sums, terms, chains = None, [], [], [marks]
    tie = lambda place: [array for chain, step in TIES.get(place, ()) if cube for array in chains[chain][step]]
    for place, b_span in enumerate(b_spans):
        grad_tokens, *parts = fold(
            ids, held["own"], [(array, b_span[0]) for array in returned[place]], tokens, upstream, columns,
            grad_tokens, b_span, group, local, cut, cube, tie(place),
        )
        if cube:
            total, marks = net.scatter(parts, scale, JOINED[1 + place])
            chains.append(marks)
            sums.append(total)
        else:
            terms.append(parts[0])
    if not cube:
        sums = [scatter_plain(jnp.concatenate(terms, axis=1), rows, scale)]
    return held["mixed"], grad_tokens, jnp.concatenate(sums), grad_second


def solution(mesh):
    placed = (P("dp", "mp"), P("dp", "mp"), P("mp", "dp", None), P("mp", "dp", None))
    return jax.shard_map(
        on_device, mesh=mesh, in_specs=placed, out_specs=placed, check_vma=False
    )
```

```python
import functools
import math

import jax
import jax.numpy as jnp
from jax import lax
from jax.experimental import pallas as pl
from jax.experimental.pallas import tpu as pltpu
from jax.sharding import PartitionSpec as P

BF16 = jnp.bfloat16
F32 = jnp.float32
ROOT_HALF = math.sqrt(0.5)
DENSITY = 1.0 / math.sqrt(2.0 * math.pi)
JOINED = (True, False, False, False)
TIES = {0: ((0, 2),), 1: ((1, 1),), 2: ((0, 3), (1, 3), (2, 2))}
VMEM = 20 * 1024 * 1024
LARGE = 1 << 20


def split_even(count, parts):
    parts = min(count, parts)
    edges = [count * step // parts for step in range(parts + 1)]
    return list(zip(edges[:-1], edges[1:]))


def split_by(count, weights):
    total, edges, run = sum(weights), [0], 0
    for weight in weights:
        run += weight
        edges.append(count * run // total)
    return [(lo, hi) for lo, hi in zip(edges[:-1], edges[1:]) if hi > lo]


def dot(left, right, left_dim, right_dim):
    return lax.dot_general(
        left, right, (((left_dim,), (right_dim,)), ((), ())), preferred_element_type=F32
    )


def aligned(index, size):
    return pl.ds(pl.multiple_of(index * size, size), size)


def placed_for(array):
    if array.ndim == 2 or array.ndim == 4 and array.size > LARGE:
        return pltpu.with_memory_space_constraint(array, pltpu.HBM)
    return array


def call(kernel, name, ids, grid, inputs, held, outputs, scratch=(), after=()):
    places = sorted(held)
    extra = [held[place] for place in places] + list(after)
    taken = len(inputs)

    def body(ids_ref, *refs):
        kernel(ids_ref, *refs[:taken], *refs[taken + len(extra) :])

    return pl.pallas_call(
        body,
        grid_spec=pltpu.PrefetchScalarGridSpec(
            num_scalar_prefetch=1,
            grid=grid,
            in_specs=[spec for _, spec in inputs] + [pl.BlockSpec(memory_space=pl.ANY)] * len(extra),
            out_specs=[spec for _, _, spec in outputs],
            scratch_shapes=list(scratch),
        ),
        out_shape=[jax.ShapeDtypeStruct(shape, dtype) for shape, dtype, _ in outputs],
        input_output_aliases={1 + taken + at: place for at, place in enumerate(places)},
        compiler_params=pltpu.CompilerParams(
            dimension_semantics=("arbitrary",) * len(grid), vmem_limit_bytes=VMEM
        ),
        cost_estimate=pl.CostEstimate(flops=1, bytes_accessed=1, transcendentals=0),
        name=name,
    )(ids, *[placed_for(array) for array, _ in inputs], *extra)


class Whole:
    def __init__(self, arrays, slots, relative, lanes=None):
        self.arrays, self.slots, self.relative = arrays, slots, relative
        self.cols, self.lane = lanes or (arrays[0].shape[3], 0)

    def specs(self, count, at):
        return [
            (
                array,
                pl.BlockSpec(
                    (array.shape[0], count, array.shape[2], self.cols),
                    lambda step, _: (0, at(step), 0, self.lane),
                ),
            )
            for array in self.arrays
        ]

    def load(self, refs, block, target, device):
        if not self.relative:
            return refs[0][:, block].reshape(target.shape)
        for ref, slots in zip(refs, self.slots):
            rows = ref.shape[2]
            for place, slot in enumerate(slots):
                target[aligned(lax.bitwise_xor(device, slot), rows), :] = ref[place, block]
        return target[...]


def combos(bits):
    found = [0]
    for bit in bits:
        found += [value | bit for value in found]
    return found


class Network:
    def __init__(self, size):
        bits = [1 << k for k in range(size.bit_length() - 1)]
        self.size = size
        self.near, self.far = bits[:2], bits[2:]
        self.rounds = [(bit,) for bit in bits]
        self.order = [0]
        for bits in reversed(self.rounds):
            self.order = [slot | mask for mask in combos(bits) for slot in self.order]

    def swap(self, array, mask):
        return lax.ppermute(array, "dp", [(at, at ^ mask) for at in range(self.size)])

    def gather(self, shard):
        combo = combos(self.far)
        first = [shard[None]] + [self.swap(shard[None], mask) for mask in combo[1:]]
        have = [(jnp.concatenate(first, axis=0), combo)]
        for mask in reversed(self.near):
            have = have + [(self.swap(array, mask), [slot | mask for slot in slots]) for array, slots in have]
        return Whole([array for array, _ in have], [slots for _, slots in have], True)

    def cut(self, slots, bits):
        mask = sum(bits)
        return [[slot for slot in slots if slot & mask == value] for value in combos(bits)]

    def first_cut(self):
        return self.cut(self.order, self.rounds[0])

    def scatter(self, parts, scale, joined=False):
        rounds = self.rounds[: len(self.near)] + [tuple(self.far)] if joined else self.rounds
        slots = self.first_cut()[0]
        terms, sends, marks = [parts[0]], parts[1:], []
        for step, bits in enumerate(rounds):
            marks.append(sends)
            terms += [self.swap(piece, mask) for piece, mask in zip(sends, combos(bits)[1:])]
            if step + 1 < len(rounds):
                lists = self.cut(slots, rounds[step + 1])
                spans = [(slots.index(members[0]), slots.index(members[-1]) + 1) for members in lists]
                sends = [sum(term[lo:hi].astype(F32) for term in terms).astype(BF16) for lo, hi in spans[1:]]
                terms = [term[spans[0][0] : spans[0][1]] for term in terms]
                slots = lists[0]
        result = sum(term[0].astype(F32) for term in terms) * scale
        return result, marks + [[result]]


def tiles(array, rows, cols, down, along, at):
    return [
        (
            array,
            pl.BlockSpec(
                (rows, cols),
                functools.partial(lambda row, col, step, _: (row, along * at(step) + col), row, col),
            ),
        )
        for row in range(down)
        for col in range(along)
    ]


def expand_kernel(weights, shifts, spans, group, inner, ids, *rest):
    x_refs, rest = rest[:2], rest[2:]
    w_refs, rest = rest[: len(weights.arrays)], rest[len(weights.arrays) :]
    outs, held = rest[:-1], rest[-1]
    blk = held.shape[1]
    halves = []
    for half in range(2):
        weight = weights.load(w_refs, half, held.at[half], ids[1])
        halves.append(dot(x_refs[half][...], weight, 1, 0).astype(BF16).T.astype(F32))
    width = blk // group
    for at, _ in enumerate(shifts):
        parts = [
            full[at * width : (at + 1) * width].reshape(width // inner, inner, -1) for full in halves
        ]
        piece = jnp.concatenate(parts, axis=1).astype(BF16)
        for place, (start, stop) in enumerate(spans):
            outs[at * len(spans) + place][...] = piece[start:stop]


def expand(ids, tokens, weights, shifts, spans, group, local, after=()):
    tok = tokens.shape[0]
    blk = tokens.shape[1] // local
    inner = blk // (local * group)
    cols = len(shifts) * (blk // group)
    shapes = [stop - start for _ in shifts for start, stop in spans]
    return call(
        functools.partial(expand_kernel, weights, shifts, spans, group, inner),
        "expand",
        ids,
        (local // 2,),
        tiles(tokens, tok, blk, 1, 2, lambda pair: pair)
        + weights.specs(2, lambda pair: pair),
        {},
        [
            (
                (count, local * inner, tok),
                BF16,
                pl.BlockSpec((count, 2 * inner, tok), lambda pair, _: (0, pair, 0)),
            )
            for count in shapes
        ],
        [pltpu.VMEM((2, blk, cols), BF16)],
        after,
    )


def order_matrix(blk, blocks, flip):
    inner = blk // blocks
    out = lax.broadcasted_iota(jnp.int32, (blk, blk), 1 if flip else 0)
    held = lax.broadcasted_iota(jnp.int32, (blk, blk), 0 if flip else 1)
    return (held == lax.rem(out, blocks) * inner + lax.div(out, blocks)).astype(F32).astype(BF16)


def store_term(term, slots_lists, relative, outs, scratch, device, block):
    if not relative:
        out = outs[0]
        out[:, block] = term.reshape(out.shape[0], out.shape[2], out.shape[3])
        return
    scratch[...] = term
    for out, slots in zip(outs, slots_lists):
        rows = out.shape[2]
        for place, slot in enumerate(slots):
            out[place, block] = scratch[aligned(lax.bitwise_xor(device, slot), rows), :].astype(out.dtype)


def mix_kernel(weights, cut, relative, group, blocks, backs, ids, own_ref, *rest):
    arrived, rest = rest[: group - 1], rest[group - 1 :]
    w_refs, rest = rest[: len(weights.arrays)], rest[len(weights.arrays) :]
    step = (len(rest) - 6 - len(cut) - len(backs) * (group - 1)) // 2
    x_refs, up_refs, rest = rest[:step], rest[step : 2 * step], rest[2 * step :]
    mixed_ref, back_own_ref = rest[:2]
    term_refs, rest = rest[2 : 2 + len(cut)], rest[2 + len(cut) :]
    back_refs, (moved, back, held, term) = rest[:-4], rest[-4:]
    me = ids[0]
    blk = held.shape[1]
    rows = blk // group
    there = order_matrix(blk, blocks, False)
    again = order_matrix(blk, blocks, True)
    for j in range(held.shape[0]):
        cols = slice(j * blk, (j + 1) * blk)
        moved[j, aligned(me, rows), :] = own_ref[j]
        for shift in range(1, group):
            moved[j, aligned(lax.rem(me - shift + group, group), rows), :] = arrived[shift - 1][j]
        weight = weights.load(w_refs, j, held.at[j], ids[1])
        ordered = dot(there, moved[j], 1, 0).astype(BF16)
        inner_out = dot(ordered.T, weight, 1, 0)
        cdf = 0.5 + 0.5 * lax.erf(inner_out * ROOT_HALF)
        mixed_ref[:, cols] = (x_refs[j][...].astype(F32) + inner_out * cdf).astype(BF16)
        slope = cdf + inner_out * (DENSITY * jnp.exp(-0.5 * inner_out * inner_out))
        grad_out = (up_refs[j][...].astype(F32) * slope).astype(BF16)
        store_term(dot(ordered, grad_out, 1, 0), cut, relative, term_refs, term.at[j], ids[1], j)
        returned = dot(weight, grad_out, 1, 1).astype(BF16)
        back[j] = dot(again, returned, 1, 0).astype(BF16)
        back_own_ref[j] = back[j, aligned(me, rows), :]
        for shift in range(1, group):
            piece = back[j, aligned(lax.rem(me + shift, group), rows), :]
            for at, (start, stop) in enumerate(backs):
                back_refs[(shift - 1) * len(backs) + at][j] = piece[start:stop]


def mix(ids, own, arrived, weights, tokens, upstream, held, span, group, local, cut, relative, term, backs):
    tok = tokens.shape[0]
    blk = tokens.shape[1] // local
    feat = blk // group
    per = feat // local
    first, last = span
    rows = blk // sum(len(slots) for slots in cut)
    step = math.gcd(2, math.gcd(first, last))
    lane = pl.BlockSpec((tok, step * blk), lambda j, _: (0, first // step + j))
    at = pl.BlockSpec((step, feat, tok), lambda j, _: (first // step + j, 0, 0))
    keys = ["mixed", "own"]
    outs = [(tokens.shape, BF16, lane), ((local, feat, tok), BF16, at)]
    term_key, (term_first, term_last) = term
    for place, slots in enumerate(cut):
        keys.append((term_key, place))
        outs.append(
            (
                (len(slots), term_last - term_first, rows, blk),
                F32 if place == 0 else BF16,
                pl.BlockSpec((len(slots), step, rows, blk), lambda j, _: (0, (first - term_first) // step + j, 0, 0)),
            )
        )
    for shift in range(1, group):
        for key, (b_first, b_last), (j_first, j_last) in backs:
            keys.append((key, shift))
            outs.append(
                (
                    (j_last - j_first, (b_last - b_first) * per, tok),
                    BF16,
                    pl.BlockSpec(
                        (step, (b_last - b_first) * per, tok),
                        functools.partial(lambda start, j, _: (start + j, 0, 0), (first - j_first) // step),
                    ),
                )
            )
    kept = {place: held[key] for place, key in enumerate(keys) if key in held}
    cuts = [(b_first * per, b_last * per) for _, (b_first, b_last), _ in backs]
    got = call(
        functools.partial(mix_kernel, weights, cut, relative, group, local * group, cuts),
        "mix",
        ids,
        ((last - first) // step,),
        [(own, at)]
        + [(array, pl.BlockSpec((step, feat, tok), lambda j, _: (j, 0, 0))) for array in arrived]
        + weights.specs(step, lambda j: first // step + j)
        + tiles(tokens, tok, blk, 1, step, lambda j: first // step + j)
        + tiles(upstream, tok, blk, 1, step, lambda j: first // step + j),
        kept,
        outs,
        [
            pltpu.VMEM((step, blk, tok), BF16),
            pltpu.VMEM((step, blk, tok), BF16),
            pltpu.VMEM((step, blk, blk), BF16),
            pltpu.VMEM((step, blk, blk), F32),
        ],
    )
    held.update(zip(keys, got))


def fold_kernel(columns, cut, relative, group, inner, pieces, ids, own_ref, *rest):
    arrived, rest = rest[: pieces * (group - 1)], rest[pieces * (group - 1) :]
    x_refs, up_refs, rest = rest[:2], rest[2:4], rest[4:]
    w_refs = []
    for weights in columns:
        w_refs.append(rest[: len(weights.arrays)])
        rest = rest[len(weights.arrays) :]
    out_ref, term_refs = rest[0], rest[1:-4]
    inner_grad, held, sorted_term, term = rest[-4:]
    me = ids[0]
    blk = held.shape[2]
    width = blk // group
    for shift in range(group):
        if shift == 0:
            piece = own_ref[...]
        else:
            refs = arrived[(shift - 1) * pieces : shift * pieces]
            piece = jnp.concatenate([ref[...] for ref in refs], axis=0)
        piece = piece.astype(F32)
        for half in range(2):
            part = piece[:, half * inner : (half + 1) * inner].reshape(width, -1)
            inner_grad[half, shift * width : (shift + 1) * width, :] = part.astype(BF16)
    for half in range(2):
        cols = slice(half * blk, (half + 1) * blk)
        if len(columns) == 1:
            weight = columns[0].load(w_refs[0], half, held.at[half], ids[1])
        else:
            start = 0
            for weights, refs in zip(columns, w_refs):
                size = weights.cols
                part = held.at[half, :, start : start + size]
                part[...] = weights.load(refs, half, part, ids[1])
                start += size
            weight = held[half]
        du = inner_grad[half]
        unsorted = dot(du, x_refs[half][...], 1, 0)
        for shift in range(group):
            source = lax.rem(me - shift + group, group)
            sorted_term[half, aligned(source, width), :] = unsorted[shift * width : (shift + 1) * width]
        store_term(sorted_term[half].T, cut, relative, term_refs, term.at[half], ids[1], half)
        back = dot(du.T, weight, 1, 1)
        out_ref[:, cols] = (up_refs[half][...].astype(F32) + back).astype(BF16)


def fold(ids, own, arrived, tokens, upstream, columns, grad_tokens, span, group, local, cut, relative, after):
    tok = tokens.shape[0]
    blk = tokens.shape[1] // local
    inner = blk // (local * group)
    first, last = span
    rows = blk // sum(len(slots) for slots in cut)
    start = first // 2
    lane = pl.BlockSpec((tok, 2 * blk), lambda pair, _: (0, start + pair))
    inputs = []
    for array, begin in [(own, 0)] + arrived:
        at = functools.partial(lambda skip, pair, _: (0, skip + pair, 0), start - begin // 2)
        inputs.append((array, pl.BlockSpec((array.shape[0], 2 * inner, tok), at)))
    for array in (tokens, upstream):
        inputs += tiles(array, tok, blk, 1, 2, lambda pair: start + pair)
    for weights in columns:
        inputs += weights.specs(2, lambda pair: start + pair)
    outs = [(tokens.shape, BF16, lane)] + [
        (
            (len(slots), last - first, rows, blk),
            F32 if place == 0 else BF16,
            pl.BlockSpec((len(slots), 2, rows, blk), lambda pair, _: (0, pair, 0, 0)),
        )
        for place, slots in enumerate(cut)
    ]
    pieces = len(arrived) // (group - 1)
    held = {} if grad_tokens is None else {0: grad_tokens}
    return call(
        functools.partial(fold_kernel, columns, cut, relative, group, inner, pieces),
        "fold",
        ids,
        ((last - first) // 2,),
        inputs,
        held,
        outs,
        [
            pltpu.VMEM((2, blk, tok), BF16),
            pltpu.VMEM((2, blk, blk), BF16),
            pltpu.VMEM((2, blk, blk), F32),
            pltpu.VMEM((2, blk, blk), F32),
        ],
        after,
    )


def send(array, shift, group):
    return lax.ppermute(array, "mp", [(at, (at + shift) % group) for at in range(group)])


def gather_plain(shard):
    local, rows, blk = shard.shape
    whole = lax.all_gather(shard, "dp", axis=0, tiled=False)
    if rows % 16:
        whole = jnp.transpose(whole, (1, 0, 2, 3)).reshape(1, local, whole.shape[0] * rows, blk)
    return Whole([whole], [list(range(whole.shape[0]))], False)


def scatter_plain(term, rows, scale):
    if term.shape[2] != rows:
        _, count, whole, blk = term.shape
        term = jnp.transpose(term.reshape(count, whole // rows, rows, blk), (1, 0, 2, 3))
    return lax.psum_scatter(term, "dp", scatter_dimension=0, tiled=False) * scale


def on_device(tokens, upstream, first_factor, second_factor):
    local, rows, blk = first_factor.shape
    group, size = lax.axis_size("mp"), lax.axis_size("dp")
    width = blk // group
    scale = 1.0 / math.sqrt(tokens.shape[0] * size)
    me, device = lax.axis_index("mp"), lax.axis_index("dp")
    ids = jnp.stack([me, device]).astype(jnp.int32)
    cube = group == 2 and size >= 8 and size & (size - 1) == 0 and rows % 16 == 0 and width % 128 == 0
    net = Network(size) if cube else None
    cut = net.first_cut() if cube else [[0]]
    plain_cut = [list(range(size))] if cube else [[0]]
    j_spans = split_by(local, (3, 3, 2)) if cube else split_even(local, 4)
    b_spans = [(2 * lo, 2 * hi) for lo, hi in split_by(local // 2, (3, 3, 2))]
    shifts = list(range(1, group))

    if cube:
        cols = [
            lax.dynamic_slice_in_dim(first_factor, lax.rem(me + shift, group) * width, width, 2)
            for shift in range(2)
        ]
        far = net.gather(cols[1])
        both = gather_plain(jnp.concatenate([second_factor, cols[0]], axis=2))
        second_whole = Whole(both.arrays, both.slots, False, (blk, 0))
        near = Whole(both.arrays, both.slots, False, (width, group))
        columns = [near, far]
    else:
        second_whole = gather_plain(second_factor)
        whole = gather_plain(first_factor).arrays[0]
        if whole.shape[0] > 1:
            whole = jnp.transpose(whole, (1, 0, 2, 3)).reshape(1, local, blk, blk)
        turned = jnp.roll(whole, -me * width, axis=3)
        near, far, turned = [
            Whole([array], [[0]], False) for array in (turned[..., :width], turned[..., width:], turned)
        ]
        columns = [turned]
    sends = expand(ids, tokens, far, shifts, j_spans, group, local)
    arrived = [
        [send(sends[(shift - 1) * len(j_spans) + at], shift, group) for shift in shifts]
        for at in range(len(j_spans))
    ]
    own = expand(ids, tokens, near, [0], [(0, local)], group, local)[0]

    held = {}
    backs = [(("back", place), b_span, (0, local)) for place, b_span in enumerate(b_spans)]
    for at, span in enumerate(j_spans):
        mix(
            ids, own, arrived[at], second_whole, tokens, upstream, held, span, group, local, cut, cube,
            ("term", (0, local)), backs,
        )
    returned = [[send(held[(key, shift)], shift, group) for shift in shifts] for key, _, _ in backs]
    parts = [held[("term", place)] for place in range(len(cut))]
    if cube:
        grad_second, marks = net.scatter(parts, scale, JOINED[0])
    else:
        grad_second, marks = scatter_plain(parts[0], rows, scale), []

    grad_tokens, sums, terms, chains = None, [], [], [marks]
    tie = lambda place: [array for chain, step in TIES.get(place, ()) if cube for array in chains[chain][step]]
    for place, b_span in enumerate(b_spans):
        grad_tokens, *parts = fold(
            ids, held["own"], [(array, b_span[0]) for array in returned[place]], tokens, upstream, columns,
            grad_tokens, b_span, group, local, cut, cube, tie(place),
        )
        if cube:
            total, marks = net.scatter(parts, scale, JOINED[1 + place])
            chains.append(marks)
            sums.append(total)
        else:
            terms.append(parts[0])
    if not cube:
        sums = [scatter_plain(jnp.concatenate(terms, axis=1), rows, scale)]
    return held["mixed"], grad_tokens, jnp.concatenate(sums), grad_second


def solution(mesh):
    placed = (P("dp", "mp"), P("dp", "mp"), P("mp", "dp", None), P("mp", "dp", None))
    return jax.shard_map(
        on_device, mesh=mesh, in_specs=placed, out_specs=placed, check_vma=False
    )
```

```python
import functools
import math

import jax
import jax.numpy as jnp
from jax import lax
from jax.experimental import pallas as pl
from jax.experimental.pallas import tpu as pltpu
from jax.sharding import PartitionSpec as P

BF16 = jnp.bfloat16
F32 = jnp.float32
ROOT_HALF = math.sqrt(0.5)
DENSITY = 1.0 / math.sqrt(2.0 * math.pi)
TOGETHER = 2
JOINED = (True, False, False, False)
TIES = {0: ((0, 2),), 1: ((1, 1),), 2: ((0, 3), (1, 3), (2, 2))}
VMEM = 20 * 1024 * 1024
LARGE = 1 << 20


def split_even(count, parts):
    parts = min(count, parts)
    edges = [count * step // parts for step in range(parts + 1)]
    return list(zip(edges[:-1], edges[1:]))


def split_by(count, weights):
    total, edges, run = sum(weights), [0], 0
    for weight in weights:
        run += weight
        edges.append(count * run // total)
    return [(lo, hi) for lo, hi in zip(edges[:-1], edges[1:]) if hi > lo]


def dot(left, right, left_dim, right_dim):
    return lax.dot_general(
        left, right, (((left_dim,), (right_dim,)), ((), ())), preferred_element_type=F32
    )


def aligned(index, size):
    return pl.ds(pl.multiple_of(index * size, size), size)


def placed_for(array):
    if array.ndim == 2 or array.ndim == 4 and array.size > LARGE:
        return pltpu.with_memory_space_constraint(array, pltpu.HBM)
    return array


def call(kernel, name, ids, grid, inputs, held, outputs, scratch=(), after=()):
    places = sorted(held)
    extra = [held[place] for place in places] + list(after)
    taken = len(inputs)

    def body(ids_ref, *refs):
        kernel(ids_ref, *refs[:taken], *refs[taken + len(extra) :])

    return pl.pallas_call(
        body,
        grid_spec=pltpu.PrefetchScalarGridSpec(
            num_scalar_prefetch=1,
            grid=grid,
            in_specs=[spec for _, spec in inputs] + [pl.BlockSpec(memory_space=pl.ANY)] * len(extra),
            out_specs=[spec for _, _, spec in outputs],
            scratch_shapes=list(scratch),
        ),
        out_shape=[jax.ShapeDtypeStruct(shape, dtype) for shape, dtype, _ in outputs],
        input_output_aliases={1 + taken + at: place for at, place in enumerate(places)},
        compiler_params=pltpu.CompilerParams(
            dimension_semantics=("arbitrary",) * len(grid), vmem_limit_bytes=VMEM
        ),
        cost_estimate=pl.CostEstimate(flops=1, bytes_accessed=1, transcendentals=0),
        name=name,
    )(ids, *[placed_for(array) for array, _ in inputs], *extra)


class Whole:
    def __init__(self, arrays, slots, relative, lanes=None):
        self.arrays, self.slots, self.relative = arrays, slots, relative
        self.cols, self.lane = lanes or (arrays[0].shape[3], 0)

    def specs(self, count, at):
        return [
            (
                array,
                pl.BlockSpec(
                    (array.shape[0], count, array.shape[2], self.cols),
                    lambda step, _: (0, at(step), 0, self.lane),
                ),
            )
            for array in self.arrays
        ]

    def load(self, refs, block, target, device):
        if not self.relative:
            return refs[0][:, block].reshape(target.shape)
        for ref, slots in zip(refs, self.slots):
            rows = ref.shape[2]
            for place, slot in enumerate(slots):
                target[aligned(lax.bitwise_xor(device, slot), rows), :] = ref[place, block]
        return target[...]


def combos(bits):
    found = [0]
    for bit in bits:
        found += [value | bit for value in found]
    return found


class Network:
    def __init__(self, size):
        bits = [1 << k for k in range(size.bit_length() - 1)]
        self.size = size
        self.near, self.far = bits[:2], bits[2:]
        self.rounds = [(bit,) for bit in bits]
        self.order = [0]
        for bits in reversed(self.rounds):
            self.order = [slot | mask for mask in combos(bits) for slot in self.order]

    def swap(self, array, mask):
        return lax.ppermute(array, "dp", [(at, at ^ mask) for at in range(self.size)])

    def gather(self, shard):
        combo = combos(self.far)
        first = [shard[None]] + [self.swap(shard[None], mask) for mask in combo[1:]]
        have = [(jnp.concatenate(first, axis=0), combo)]
        for mask in reversed(self.near):
            have = have + [(self.swap(array, mask), [slot | mask for slot in slots]) for array, slots in have]
        return Whole([array for array, _ in have], [slots for _, slots in have], True)

    def cut(self, slots, bits):
        mask = sum(bits)
        return [[slot for slot in slots if slot & mask == value] for value in combos(bits)]

    def first_cut(self):
        return self.cut(self.order, self.rounds[0])

    def scatter(self, parts, scale, joined=False, closed=True):
        rounds = self.rounds[: len(self.near)] + [tuple(self.far)] if joined else self.rounds
        slots = self.first_cut()[0]
        terms, sends, marks = [parts[0]], parts[1:], []
        for step, bits in enumerate(rounds):
            marks.append(sends)
            if step + 1 == len(rounds) and not closed:
                return (terms, sends[0]), marks
            terms += [self.swap(piece, mask) for piece, mask in zip(sends, combos(bits)[1:])]
            if step + 1 < len(rounds):
                lists = self.cut(slots, rounds[step + 1])
                spans = [(slots.index(members[0]), slots.index(members[-1]) + 1) for members in lists]
                sends = [sum(term[lo:hi].astype(F32) for term in terms).astype(BF16) for lo, hi in spans[1:]]
                terms = [term[spans[0][0] : spans[0][1]] for term in terms]
                slots = lists[0]
        result = sum(term[0].astype(F32) for term in terms) * scale
        return result, marks + [[result]]

    def close(self, opened, scale):
        got = self.swap(jnp.concatenate([sent for _, sent in opened], axis=1), self.rounds[-1][0])
        results, start = [], 0
        for terms, sent in opened:
            part = got[:, start : start + sent.shape[1]]
            results.append(sum(term[0].astype(F32) for term in terms + [part]) * scale)
            start += sent.shape[1]
        return results


def tiles(array, rows, cols, down, along, at):
    return [
        (
            array,
            pl.BlockSpec(
                (rows, cols),
                functools.partial(lambda row, col, step, _: (row, along * at(step) + col), row, col),
            ),
        )
        for row in range(down)
        for col in range(along)
    ]


def expand_kernel(weights, shifts, spans, group, inner, ids, *rest):
    x_refs, rest = rest[:2], rest[2:]
    w_refs, rest = rest[: len(weights.arrays)], rest[len(weights.arrays) :]
    outs, held = rest[:-1], rest[-1]
    blk = held.shape[1]
    halves = []
    for half in range(2):
        weight = weights.load(w_refs, half, held.at[half], ids[1])
        halves.append(dot(x_refs[half][...], weight, 1, 0).astype(BF16).T.astype(F32))
    width = blk // group
    for at, _ in enumerate(shifts):
        parts = [
            full[at * width : (at + 1) * width].reshape(width // inner, inner, -1) for full in halves
        ]
        piece = jnp.concatenate(parts, axis=1).astype(BF16)
        for place, (start, stop) in enumerate(spans):
            outs[at * len(spans) + place][...] = piece[start:stop]


def expand(ids, tokens, weights, shifts, spans, group, local, after=()):
    tok = tokens.shape[0]
    blk = tokens.shape[1] // local
    inner = blk // (local * group)
    cols = len(shifts) * (blk // group)
    shapes = [stop - start for _ in shifts for start, stop in spans]
    return call(
        functools.partial(expand_kernel, weights, shifts, spans, group, inner),
        "expand",
        ids,
        (local // 2,),
        tiles(tokens, tok, blk, 1, 2, lambda pair: pair)
        + weights.specs(2, lambda pair: pair),
        {},
        [
            (
                (count, local * inner, tok),
                BF16,
                pl.BlockSpec((count, 2 * inner, tok), lambda pair, _: (0, pair, 0)),
            )
            for count in shapes
        ],
        [pltpu.VMEM((2, blk, cols), BF16)],
        after,
    )


def order_matrix(blk, blocks, flip):
    inner = blk // blocks
    out = lax.broadcasted_iota(jnp.int32, (blk, blk), 1 if flip else 0)
    held = lax.broadcasted_iota(jnp.int32, (blk, blk), 0 if flip else 1)
    return (held == lax.rem(out, blocks) * inner + lax.div(out, blocks)).astype(F32).astype(BF16)


def store_term(term, slots_lists, relative, outs, scratch, device, block):
    if not relative:
        out = outs[0]
        out[:, block] = term.reshape(out.shape[0], out.shape[2], out.shape[3])
        return
    scratch[...] = term
    for out, slots in zip(outs, slots_lists):
        rows = out.shape[2]
        for place, slot in enumerate(slots):
            out[place, block] = scratch[aligned(lax.bitwise_xor(device, slot), rows), :].astype(out.dtype)


def mix_kernel(weights, cut, relative, group, blocks, backs, ids, own_ref, *rest):
    arrived, rest = rest[: group - 1], rest[group - 1 :]
    w_refs, rest = rest[: len(weights.arrays)], rest[len(weights.arrays) :]
    step = (len(rest) - 6 - len(cut) - len(backs) * (group - 1)) // 2
    x_refs, up_refs, rest = rest[:step], rest[step : 2 * step], rest[2 * step :]
    mixed_ref, back_own_ref = rest[:2]
    term_refs, rest = rest[2 : 2 + len(cut)], rest[2 + len(cut) :]
    back_refs, (moved, back, held, term) = rest[:-4], rest[-4:]
    me = ids[0]
    blk = held.shape[1]
    rows = blk // group
    there = order_matrix(blk, blocks, False)
    again = order_matrix(blk, blocks, True)
    for j in range(held.shape[0]):
        cols = slice(j * blk, (j + 1) * blk)
        moved[j, aligned(me, rows), :] = own_ref[j]
        for shift in range(1, group):
            moved[j, aligned(lax.rem(me - shift + group, group), rows), :] = arrived[shift - 1][j]
        weight = weights.load(w_refs, j, held.at[j], ids[1])
        ordered = dot(there, moved[j], 1, 0).astype(BF16)
        inner_out = dot(ordered.T, weight, 1, 0)
        cdf = 0.5 + 0.5 * lax.erf(inner_out * ROOT_HALF)
        mixed_ref[:, cols] = (x_refs[j][...].astype(F32) + inner_out * cdf).astype(BF16)
        slope = cdf + inner_out * (DENSITY * jnp.exp(-0.5 * inner_out * inner_out))
        grad_out = (up_refs[j][...].astype(F32) * slope).astype(BF16)
        store_term(dot(ordered, grad_out, 1, 0), cut, relative, term_refs, term.at[j], ids[1], j)
        returned = dot(weight, grad_out, 1, 1).astype(BF16)
        back[j] = dot(again, returned, 1, 0).astype(BF16)
        back_own_ref[j] = back[j, aligned(me, rows), :]
        for shift in range(1, group):
            piece = back[j, aligned(lax.rem(me + shift, group), rows), :]
            for at, (start, stop) in enumerate(backs):
                back_refs[(shift - 1) * len(backs) + at][j] = piece[start:stop]


def mix(ids, own, arrived, weights, tokens, upstream, held, span, group, local, cut, relative, term, backs):
    tok = tokens.shape[0]
    blk = tokens.shape[1] // local
    feat = blk // group
    per = feat // local
    first, last = span
    rows = blk // sum(len(slots) for slots in cut)
    step = math.gcd(2, math.gcd(first, last))
    lane = pl.BlockSpec((tok, step * blk), lambda j, _: (0, first // step + j))
    at = pl.BlockSpec((step, feat, tok), lambda j, _: (first // step + j, 0, 0))
    keys = ["mixed", "own"]
    outs = [(tokens.shape, BF16, lane), ((local, feat, tok), BF16, at)]
    term_key, (term_first, term_last) = term
    for place, slots in enumerate(cut):
        keys.append((term_key, place))
        outs.append(
            (
                (len(slots), term_last - term_first, rows, blk),
                F32 if place == 0 else BF16,
                pl.BlockSpec((len(slots), step, rows, blk), lambda j, _: (0, (first - term_first) // step + j, 0, 0)),
            )
        )
    for shift in range(1, group):
        for key, (b_first, b_last), (j_first, j_last) in backs:
            keys.append((key, shift))
            outs.append(
                (
                    (j_last - j_first, (b_last - b_first) * per, tok),
                    BF16,
                    pl.BlockSpec(
                        (step, (b_last - b_first) * per, tok),
                        functools.partial(lambda start, j, _: (start + j, 0, 0), (first - j_first) // step),
                    ),
                )
            )
    kept = {place: held[key] for place, key in enumerate(keys) if key in held}
    cuts = [(b_first * per, b_last * per) for _, (b_first, b_last), _ in backs]
    got = call(
        functools.partial(mix_kernel, weights, cut, relative, group, local * group, cuts),
        "mix",
        ids,
        ((last - first) // step,),
        [(own, at)]
        + [(array, pl.BlockSpec((step, feat, tok), lambda j, _: (j, 0, 0))) for array in arrived]
        + weights.specs(step, lambda j: first // step + j)
        + tiles(tokens, tok, blk, 1, step, lambda j: first // step + j)
        + tiles(upstream, tok, blk, 1, step, lambda j: first // step + j),
        kept,
        outs,
        [
            pltpu.VMEM((step, blk, tok), BF16),
            pltpu.VMEM((step, blk, tok), BF16),
            pltpu.VMEM((step, blk, blk), BF16),
            pltpu.VMEM((step, blk, blk), F32),
        ],
    )
    held.update(zip(keys, got))


def fold_kernel(columns, cut, relative, group, inner, pieces, ids, own_ref, *rest):
    arrived, rest = rest[: pieces * (group - 1)], rest[pieces * (group - 1) :]
    x_refs, up_refs, rest = rest[:2], rest[2:4], rest[4:]
    w_refs = []
    for weights in columns:
        w_refs.append(rest[: len(weights.arrays)])
        rest = rest[len(weights.arrays) :]
    out_ref, term_refs = rest[0], rest[1:-4]
    inner_grad, held, sorted_term, term = rest[-4:]
    me = ids[0]
    blk = held.shape[2]
    width = blk // group
    for shift in range(group):
        if shift == 0:
            piece = own_ref[...]
        else:
            refs = arrived[(shift - 1) * pieces : shift * pieces]
            piece = jnp.concatenate([ref[...] for ref in refs], axis=0)
        piece = piece.astype(F32)
        for half in range(2):
            part = piece[:, half * inner : (half + 1) * inner].reshape(width, -1)
            inner_grad[half, shift * width : (shift + 1) * width, :] = part.astype(BF16)
    for half in range(2):
        cols = slice(half * blk, (half + 1) * blk)
        if len(columns) == 1:
            weight = columns[0].load(w_refs[0], half, held.at[half], ids[1])
        else:
            start = 0
            for weights, refs in zip(columns, w_refs):
                size = weights.cols
                part = held.at[half, :, start : start + size]
                part[...] = weights.load(refs, half, part, ids[1])
                start += size
            weight = held[half]
        du = inner_grad[half]
        unsorted = dot(du, x_refs[half][...], 1, 0)
        for shift in range(group):
            source = lax.rem(me - shift + group, group)
            sorted_term[half, aligned(source, width), :] = unsorted[shift * width : (shift + 1) * width]
        store_term(sorted_term[half].T, cut, relative, term_refs, term.at[half], ids[1], half)
        back = dot(du.T, weight, 1, 1)
        out_ref[:, cols] = (up_refs[half][...].astype(F32) + back).astype(BF16)


def fold(ids, own, arrived, tokens, upstream, columns, grad_tokens, span, group, local, cut, relative, after):
    tok = tokens.shape[0]
    blk = tokens.shape[1] // local
    inner = blk // (local * group)
    first, last = span
    rows = blk // sum(len(slots) for slots in cut)
    start = first // 2
    lane = pl.BlockSpec((tok, 2 * blk), lambda pair, _: (0, start + pair))
    inputs = []
    for array, begin in [(own, 0)] + arrived:
        at = functools.partial(lambda skip, pair, _: (0, skip + pair, 0), start - begin // 2)
        inputs.append((array, pl.BlockSpec((array.shape[0], 2 * inner, tok), at)))
    for array in (tokens, upstream):
        inputs += tiles(array, tok, blk, 1, 2, lambda pair: start + pair)
    for weights in columns:
        inputs += weights.specs(2, lambda pair: start + pair)
    outs = [(tokens.shape, BF16, lane)] + [
        (
            (len(slots), last - first, rows, blk),
            F32 if place == 0 else BF16,
            pl.BlockSpec((len(slots), 2, rows, blk), lambda pair, _: (0, pair, 0, 0)),
        )
        for place, slots in enumerate(cut)
    ]
    pieces = len(arrived) // (group - 1)
    held = {} if grad_tokens is None else {0: grad_tokens}
    return call(
        functools.partial(fold_kernel, columns, cut, relative, group, inner, pieces),
        "fold",
        ids,
        ((last - first) // 2,),
        inputs,
        held,
        outs,
        [
            pltpu.VMEM((2, blk, tok), BF16),
            pltpu.VMEM((2, blk, blk), BF16),
            pltpu.VMEM((2, blk, blk), F32),
            pltpu.VMEM((2, blk, blk), F32),
        ],
        after,
    )


def send(array, shift, group):
    return lax.ppermute(array, "mp", [(at, (at + shift) % group) for at in range(group)])


def gather_plain(shard):
    local, rows, blk = shard.shape
    whole = lax.all_gather(shard, "dp", axis=0, tiled=False)
    if rows % 16:
        whole = jnp.transpose(whole, (1, 0, 2, 3)).reshape(1, local, whole.shape[0] * rows, blk)
    return Whole([whole], [list(range(whole.shape[0]))], False)


def scatter_plain(term, rows, scale):
    if term.shape[2] != rows:
        _, count, whole, blk = term.shape
        term = jnp.transpose(term.reshape(count, whole // rows, rows, blk), (1, 0, 2, 3))
    return lax.psum_scatter(term, "dp", scatter_dimension=0, tiled=False) * scale


def on_device(tokens, upstream, first_factor, second_factor):
    local, rows, blk = first_factor.shape
    group, size = lax.axis_size("mp"), lax.axis_size("dp")
    width = blk // group
    scale = 1.0 / math.sqrt(tokens.shape[0] * size)
    me, device = lax.axis_index("mp"), lax.axis_index("dp")
    ids = jnp.stack([me, device]).astype(jnp.int32)
    cube = group == 2 and size >= 8 and size & (size - 1) == 0 and rows % 16 == 0 and width % 128 == 0
    net = Network(size) if cube else None
    cut = net.first_cut() if cube else [[0]]
    plain_cut = [list(range(size))] if cube else [[0]]
    j_spans = split_by(local, (3, 3, 2)) if cube else split_even(local, 4)
    b_spans = [(2 * lo, 2 * hi) for lo, hi in split_by(local // 2, (3, 3, 2))]
    shifts = list(range(1, group))

    if cube:
        cols = [
            lax.dynamic_slice_in_dim(first_factor, lax.rem(me + shift, group) * width, width, 2)
            for shift in range(2)
        ]
        far = net.gather(cols[1])
        both = gather_plain(jnp.concatenate([second_factor, cols[0]], axis=2))
        second_whole = Whole(both.arrays, both.slots, False, (blk, 0))
        near = Whole(both.arrays, both.slots, False, (width, group))
        columns = [near, far]
    else:
        second_whole = gather_plain(second_factor)
        whole = gather_plain(first_factor).arrays[0]
        if whole.shape[0] > 1:
            whole = jnp.transpose(whole, (1, 0, 2, 3)).reshape(1, local, blk, blk)
        turned = jnp.roll(whole, -me * width, axis=3)
        near, far, turned = [
            Whole([array], [[0]], False) for array in (turned[..., :width], turned[..., width:], turned)
        ]
        columns = [turned]
    sends = expand(ids, tokens, far, shifts, j_spans, group, local)
    arrived = [
        [send(sends[(shift - 1) * len(j_spans) + at], shift, group) for shift in shifts]
        for at in range(len(j_spans))
    ]
    own = expand(ids, tokens, near, [0], [(0, local)], group, local)[0]

    held = {}
    backs = [(("back", place), b_span, (0, local)) for place, b_span in enumerate(b_spans)]
    for at, span in enumerate(j_spans):
        mix(
            ids, own, arrived[at], second_whole, tokens, upstream, held, span, group, local, cut, cube,
            ("term", (0, local)), backs,
        )
    returned = [[send(held[(key, shift)], shift, group) for shift in shifts] for key, _, _ in backs]
    parts = [held[("term", place)] for place in range(len(cut))]
    if cube:
        grad_second, marks = net.scatter(parts, scale, JOINED[0])
    else:
        grad_second, marks = scatter_plain(parts[0], rows, scale), []

    grad_tokens, sums, terms, opened, chains = None, [], [], [], [marks]
    tie = lambda place: [array for chain, step in TIES.get(place, ()) if cube for array in chains[chain][step]]
    for place, b_span in enumerate(b_spans):
        grad_tokens, *parts = fold(
            ids, held["own"], [(array, b_span[0]) for array in returned[place]], tokens, upstream, columns,
            grad_tokens, b_span, group, local, cut, cube, tie(place),
        )
        if cube:
            total, marks = net.scatter(parts, scale, JOINED[1 + place], place >= TOGETHER)
            chains.append(marks)
            if place >= TOGETHER:
                sums.append(total)
            else:
                opened.append(total)
                if len(opened) == TOGETHER:
                    sums += net.close(opened, scale)
        else:
            terms.append(parts[0])
    if not cube:
        sums = [scatter_plain(jnp.concatenate(terms, axis=1), rows, scale)]
    return held["mixed"], grad_tokens, jnp.concatenate(sums), grad_second


def solution(mesh):
    placed = (P("dp", "mp"), P("dp", "mp"), P("mp", "dp", None), P("mp", "dp", None))
    return jax.shard_map(
        on_device, mesh=mesh, in_specs=placed, out_specs=placed, check_vma=False
    )
```

```python
import functools
import math

import jax
import jax.numpy as jnp
from jax import lax
from jax.experimental import pallas as pl
from jax.experimental.pallas import tpu as pltpu
from jax.sharding import PartitionSpec as P

BF16 = jnp.bfloat16
F32 = jnp.float32
ROOT_HALF = math.sqrt(0.5)
DENSITY = 1.0 / math.sqrt(2.0 * math.pi)
JOINED = (True, False, False, True)
TIES = {0: ((0, 2),), 1: ((1, 1),), 2: ((0, 3), (1, 3), (2, 2))}
VMEM = 20 * 1024 * 1024
LARGE = 1 << 20


def split_even(count, parts):
    parts = min(count, parts)
    edges = [count * step // parts for step in range(parts + 1)]
    return list(zip(edges[:-1], edges[1:]))


def split_by(count, weights):
    total, edges, run = sum(weights), [0], 0
    for weight in weights:
        run += weight
        edges.append(count * run // total)
    return [(lo, hi) for lo, hi in zip(edges[:-1], edges[1:]) if hi > lo]


def dot(left, right, left_dim, right_dim):
    return lax.dot_general(
        left, right, (((left_dim,), (right_dim,)), ((), ())), preferred_element_type=F32
    )


def aligned(index, size):
    return pl.ds(pl.multiple_of(index * size, size), size)


def placed_for(array):
    if array.ndim == 2 or array.ndim == 4 and array.size > LARGE:
        return pltpu.with_memory_space_constraint(array, pltpu.HBM)
    return array


def call(kernel, name, ids, grid, inputs, held, outputs, scratch=(), after=()):
    places = sorted(held)
    extra = [held[place] for place in places] + list(after)
    taken = len(inputs)

    def body(ids_ref, *refs):
        kernel(ids_ref, *refs[:taken], *refs[taken + len(extra) :])

    return pl.pallas_call(
        body,
        grid_spec=pltpu.PrefetchScalarGridSpec(
            num_scalar_prefetch=1,
            grid=grid,
            in_specs=[spec for _, spec in inputs] + [pl.BlockSpec(memory_space=pl.ANY)] * len(extra),
            out_specs=[spec for _, _, spec in outputs],
            scratch_shapes=list(scratch),
        ),
        out_shape=[jax.ShapeDtypeStruct(shape, dtype) for shape, dtype, _ in outputs],
        input_output_aliases={1 + taken + at: place for at, place in enumerate(places)},
        compiler_params=pltpu.CompilerParams(
            dimension_semantics=("arbitrary",) * len(grid), vmem_limit_bytes=VMEM
        ),
        cost_estimate=pl.CostEstimate(flops=1, bytes_accessed=1, transcendentals=0),
        name=name,
    )(ids, *[placed_for(array) for array, _ in inputs], *extra)


class Whole:
    def __init__(self, arrays, slots, relative, lanes=None):
        self.arrays, self.slots, self.relative = arrays, slots, relative
        self.cols, self.lane = lanes or (arrays[0].shape[3], 0)

    def specs(self, count, at):
        return [
            (
                array,
                pl.BlockSpec(
                    (array.shape[0], count, array.shape[2], self.cols),
                    lambda step, _: (0, at(step), 0, self.lane),
                ),
            )
            for array in self.arrays
        ]

    def load(self, refs, block, target, device):
        if not self.relative:
            return refs[0][:, block].reshape(target.shape)
        for ref, slots in zip(refs, self.slots):
            rows = ref.shape[2]
            for place, slot in enumerate(slots):
                target[aligned(lax.bitwise_xor(device, slot), rows), :] = ref[place, block]
        return target[...]


def combos(bits):
    found = [0]
    for bit in bits:
        found += [value | bit for value in found]
    return found


class Network:
    def __init__(self, size):
        bits = [1 << k for k in range(size.bit_length() - 1)]
        self.size = size
        self.near, self.far = bits[:2], bits[2:]
        self.rounds = [(bit,) for bit in bits]
        self.order = [0]
        for bits in reversed(self.rounds):
            self.order = [slot | mask for mask in combos(bits) for slot in self.order]

    def swap(self, array, mask):
        return lax.ppermute(array, "dp", [(at, at ^ mask) for at in range(self.size)])

    def gather(self, shard):
        combo = combos(self.far)
        first = [shard[None]] + [self.swap(shard[None], mask) for mask in combo[1:]]
        have = [(jnp.concatenate(first, axis=0), combo)]
        for mask in reversed(self.near):
            have = have + [(self.swap(array, mask), [slot | mask for slot in slots]) for array, slots in have]
        return Whole([array for array, _ in have], [slots for _, slots in have], True)

    def cut(self, slots, bits):
        mask = sum(bits)
        return [[slot for slot in slots if slot & mask == value] for value in combos(bits)]

    def first_cut(self):
        return self.cut(self.order, self.rounds[0])

    def scatter(self, parts, scale, joined=False):
        rounds = self.rounds[: len(self.near)] + [tuple(self.far)] if joined else self.rounds
        slots = self.first_cut()[0]
        terms, sends, marks = [parts[0]], parts[1:], []
        for step, bits in enumerate(rounds):
            marks.append(sends)
            terms += [self.swap(piece, mask) for piece, mask in zip(sends, combos(bits)[1:])]
            if step + 1 < len(rounds):
                lists = self.cut(slots, rounds[step + 1])
                spans = [(slots.index(members[0]), slots.index(members[-1]) + 1) for members in lists]
                sends = [sum(term[lo:hi].astype(F32) for term in terms).astype(BF16) for lo, hi in spans[1:]]
                terms = [term[spans[0][0] : spans[0][1]] for term in terms]
                slots = lists[0]
        result = sum(term[0].astype(F32) for term in terms) * scale
        return result, marks + [[result]]


def tiles(array, rows, cols, down, along, at):
    return [
        (
            array,
            pl.BlockSpec(
                (rows, cols),
                functools.partial(lambda row, col, step, _: (row, along * at(step) + col), row, col),
            ),
        )
        for row in range(down)
        for col in range(along)
    ]


def expand_kernel(weights, shifts, spans, group, inner, ids, *rest):
    x_refs, rest = rest[:2], rest[2:]
    w_refs, rest = rest[: len(weights.arrays)], rest[len(weights.arrays) :]
    outs, held = rest[:-1], rest[-1]
    blk = held.shape[1]
    halves = []
    for half in range(2):
        weight = weights.load(w_refs, half, held.at[half], ids[1])
        halves.append(dot(x_refs[half][...], weight, 1, 0).astype(BF16).T.astype(F32))
    width = blk // group
    for at, _ in enumerate(shifts):
        parts = [
            full[at * width : (at + 1) * width].reshape(width // inner, inner, -1) for full in halves
        ]
        piece = jnp.concatenate(parts, axis=1).astype(BF16)
        for place, (start, stop) in enumerate(spans):
            outs[at * len(spans) + place][...] = piece[start:stop]


def expand(ids, tokens, weights, shifts, spans, group, local, after=()):
    tok = tokens.shape[0]
    blk = tokens.shape[1] // local
    inner = blk // (local * group)
    cols = len(shifts) * (blk // group)
    shapes = [stop - start for _ in shifts for start, stop in spans]
    return call(
        functools.partial(expand_kernel, weights, shifts, spans, group, inner),
        "expand",
        ids,
        (local // 2,),
        tiles(tokens, tok, blk, 1, 2, lambda pair: pair)
        + weights.specs(2, lambda pair: pair),
        {},
        [
            (
                (count, local * inner, tok),
                BF16,
                pl.BlockSpec((count, 2 * inner, tok), lambda pair, _: (0, pair, 0)),
            )
            for count in shapes
        ],
        [pltpu.VMEM((2, blk, cols), BF16)],
        after,
    )


def order_matrix(blk, blocks, flip):
    inner = blk // blocks
    out = lax.broadcasted_iota(jnp.int32, (blk, blk), 1 if flip else 0)
    held = lax.broadcasted_iota(jnp.int32, (blk, blk), 0 if flip else 1)
    return (held == lax.rem(out, blocks) * inner + lax.div(out, blocks)).astype(F32).astype(BF16)


def store_term(term, slots_lists, relative, outs, scratch, device, block):
    if not relative:
        out = outs[0]
        out[:, block] = term.reshape(out.shape[0], out.shape[2], out.shape[3])
        return
    scratch[...] = term
    for out, slots in zip(outs, slots_lists):
        rows = out.shape[2]
        for place, slot in enumerate(slots):
            out[place, block] = scratch[aligned(lax.bitwise_xor(device, slot), rows), :].astype(out.dtype)


def mix_kernel(weights, cut, relative, group, blocks, backs, ids, own_ref, *rest):
    arrived, rest = rest[: group - 1], rest[group - 1 :]
    w_refs, rest = rest[: len(weights.arrays)], rest[len(weights.arrays) :]
    step = (len(rest) - 6 - len(cut) - len(backs) * (group - 1)) // 2
    x_refs, up_refs, rest = rest[:step], rest[step : 2 * step], rest[2 * step :]
    mixed_ref, back_own_ref = rest[:2]
    term_refs, rest = rest[2 : 2 + len(cut)], rest[2 + len(cut) :]
    back_refs, (moved, back, held, term) = rest[:-4], rest[-4:]
    me = ids[0]
    blk = held.shape[1]
    rows = blk // group
    there = order_matrix(blk, blocks, False)
    again = order_matrix(blk, blocks, True)
    for j in range(held.shape[0]):
        cols = slice(j * blk, (j + 1) * blk)
        moved[j, aligned(me, rows), :] = own_ref[j]
        for shift in range(1, group):
            moved[j, aligned(lax.rem(me - shift + group, group), rows), :] = arrived[shift - 1][j]
        weight = weights.load(w_refs, j, held.at[j], ids[1])
        ordered = dot(there, moved[j], 1, 0).astype(BF16)
        inner_out = dot(ordered.T, weight, 1, 0)
        cdf = 0.5 + 0.5 * lax.erf(inner_out * ROOT_HALF)
        mixed_ref[:, cols] = (x_refs[j][...].astype(F32) + inner_out * cdf).astype(BF16)
        slope = cdf + inner_out * (DENSITY * jnp.exp(-0.5 * inner_out * inner_out))
        grad_out = (up_refs[j][...].astype(F32) * slope).astype(BF16)
        store_term(dot(ordered, grad_out, 1, 0), cut, relative, term_refs, term.at[j], ids[1], j)
        returned = dot(weight, grad_out, 1, 1).astype(BF16)
        back[j] = dot(again, returned, 1, 0).astype(BF16)
        back_own_ref[j] = back[j, aligned(me, rows), :]
        for shift in range(1, group):
            piece = back[j, aligned(lax.rem(me + shift, group), rows), :]
            for at, (start, stop) in enumerate(backs):
                back_refs[(shift - 1) * len(backs) + at][j] = piece[start:stop]


def mix(ids, own, arrived, weights, tokens, upstream, held, span, group, local, cut, relative, term, backs):
    tok = tokens.shape[0]
    blk = tokens.shape[1] // local
    feat = blk // group
    per = feat // local
    first, last = span
    rows = blk // sum(len(slots) for slots in cut)
    step = math.gcd(2, math.gcd(first, last))
    lane = pl.BlockSpec((tok, step * blk), lambda j, _: (0, first // step + j))
    at = pl.BlockSpec((step, feat, tok), lambda j, _: (first // step + j, 0, 0))
    keys = ["mixed", "own"]
    outs = [(tokens.shape, BF16, lane), ((local, feat, tok), BF16, at)]
    term_key, (term_first, term_last) = term
    for place, slots in enumerate(cut):
        keys.append((term_key, place))
        outs.append(
            (
                (len(slots), term_last - term_first, rows, blk),
                F32 if place == 0 else BF16,
                pl.BlockSpec((len(slots), step, rows, blk), lambda j, _: (0, (first - term_first) // step + j, 0, 0)),
            )
        )
    for shift in range(1, group):
        for key, (b_first, b_last), (j_first, j_last) in backs:
            keys.append((key, shift))
            outs.append(
                (
                    (j_last - j_first, (b_last - b_first) * per, tok),
                    BF16,
                    pl.BlockSpec(
                        (step, (b_last - b_first) * per, tok),
                        functools.partial(lambda start, j, _: (start + j, 0, 0), (first - j_first) // step),
                    ),
                )
            )
    kept = {place: held[key] for place, key in enumerate(keys) if key in held}
    cuts = [(b_first * per, b_last * per) for _, (b_first, b_last), _ in backs]
    got = call(
        functools.partial(mix_kernel, weights, cut, relative, group, local * group, cuts),
        "mix",
        ids,
        ((last - first) // step,),
        [(own, at)]
        + [(array, pl.BlockSpec((step, feat, tok), lambda j, _: (j, 0, 0))) for array in arrived]
        + weights.specs(step, lambda j: first // step + j)
        + tiles(tokens, tok, blk, 1, step, lambda j: first // step + j)
        + tiles(upstream, tok, blk, 1, step, lambda j: first // step + j),
        kept,
        outs,
        [
            pltpu.VMEM((step, blk, tok), BF16),
            pltpu.VMEM((step, blk, tok), BF16),
            pltpu.VMEM((step, blk, blk), BF16),
            pltpu.VMEM((step, blk, blk), F32),
        ],
    )
    held.update(zip(keys, got))


def fold_kernel(columns, cut, relative, group, inner, pieces, ids, own_ref, *rest):
    arrived, rest = rest[: pieces * (group - 1)], rest[pieces * (group - 1) :]
    x_refs, up_refs, rest = rest[:2], rest[2:4], rest[4:]
    w_refs = []
    for weights in columns:
        w_refs.append(rest[: len(weights.arrays)])
        rest = rest[len(weights.arrays) :]
    out_ref, term_refs = rest[0], rest[1:-4]
    inner_grad, held, sorted_term, term = rest[-4:]
    me = ids[0]
    blk = held.shape[2]
    width = blk // group
    for shift in range(group):
        if shift == 0:
            piece = own_ref[...]
        else:
            refs = arrived[(shift - 1) * pieces : shift * pieces]
            piece = jnp.concatenate([ref[...] for ref in refs], axis=0)
        piece = piece.astype(F32)
        for half in range(2):
            part = piece[:, half * inner : (half + 1) * inner].reshape(width, -1)
            inner_grad[half, shift * width : (shift + 1) * width, :] = part.astype(BF16)
    for half in range(2):
        cols = slice(half * blk, (half + 1) * blk)
        if len(columns) == 1:
            weight = columns[0].load(w_refs[0], half, held.at[half], ids[1])
        else:
            start = 0
            for weights, refs in zip(columns, w_refs):
                size = weights.cols
                part = held.at[half, :, start : start + size]
                part[...] = weights.load(refs, half, part, ids[1])
                start += size
            weight = held[half]
        du = inner_grad[half]
        unsorted = dot(du, x_refs[half][...], 1, 0)
        for shift in range(group):
            source = lax.rem(me - shift + group, group)
            sorted_term[half, aligned(source, width), :] = unsorted[shift * width : (shift + 1) * width]
        store_term(sorted_term[half].T, cut, relative, term_refs, term.at[half], ids[1], half)
        back = dot(du.T, weight, 1, 1)
        out_ref[:, cols] = (up_refs[half][...].astype(F32) + back).astype(BF16)


def fold(ids, own, arrived, tokens, upstream, columns, grad_tokens, span, group, local, cut, relative, after):
    tok = tokens.shape[0]
    blk = tokens.shape[1] // local
    inner = blk // (local * group)
    first, last = span
    rows = blk // sum(len(slots) for slots in cut)
    start = first // 2
    lane = pl.BlockSpec((tok, 2 * blk), lambda pair, _: (0, start + pair))
    inputs = []
    for array, begin in [(own, 0)] + arrived:
        at = functools.partial(lambda skip, pair, _: (0, skip + pair, 0), start - begin // 2)
        inputs.append((array, pl.BlockSpec((array.shape[0], 2 * inner, tok), at)))
    for array in (tokens, upstream):
        inputs += tiles(array, tok, blk, 1, 2, lambda pair: start + pair)
    for weights in columns:
        inputs += weights.specs(2, lambda pair: start + pair)
    outs = [(tokens.shape, BF16, lane)] + [
        (
            (len(slots), last - first, rows, blk),
            F32 if place == 0 else BF16,
            pl.BlockSpec((len(slots), 2, rows, blk), lambda pair, _: (0, pair, 0, 0)),
        )
        for place, slots in enumerate(cut)
    ]
    pieces = len(arrived) // (group - 1)
    held = {} if grad_tokens is None else {0: grad_tokens}
    return call(
        functools.partial(fold_kernel, columns, cut, relative, group, inner, pieces),
        "fold",
        ids,
        ((last - first) // 2,),
        inputs,
        held,
        outs,
        [
            pltpu.VMEM((2, blk, tok), BF16),
            pltpu.VMEM((2, blk, blk), BF16),
            pltpu.VMEM((2, blk, blk), F32),
            pltpu.VMEM((2, blk, blk), F32),
        ],
        after,
    )


def send(array, shift, group):
    return lax.ppermute(array, "mp", [(at, (at + shift) % group) for at in range(group)])


def gather_plain(shard):
    local, rows, blk = shard.shape
    whole = lax.all_gather(shard, "dp", axis=0, tiled=False)
    if rows % 16:
        whole = jnp.transpose(whole, (1, 0, 2, 3)).reshape(1, local, whole.shape[0] * rows, blk)
    return Whole([whole], [list(range(whole.shape[0]))], False)


def scatter_plain(term, rows, scale):
    if term.shape[2] != rows:
        _, count, whole, blk = term.shape
        term = jnp.transpose(term.reshape(count, whole // rows, rows, blk), (1, 0, 2, 3))
    return lax.psum_scatter(term, "dp", scatter_dimension=0, tiled=False) * scale


def on_device(tokens, upstream, first_factor, second_factor):
    local, rows, blk = first_factor.shape
    group, size = lax.axis_size("mp"), lax.axis_size("dp")
    width = blk // group
    scale = 1.0 / math.sqrt(tokens.shape[0] * size)
    me, device = lax.axis_index("mp"), lax.axis_index("dp")
    ids = jnp.stack([me, device]).astype(jnp.int32)
    cube = group == 2 and size >= 8 and size & (size - 1) == 0 and rows % 16 == 0 and width % 128 == 0
    net = Network(size) if cube else None
    cut = net.first_cut() if cube else [[0]]
    plain_cut = [list(range(size))] if cube else [[0]]
    j_spans = split_by(local, (3, 3, 2)) if cube else split_even(local, 4)
    b_spans = [(2 * lo, 2 * hi) for lo, hi in split_by(local // 2, (3, 3, 2))]
    shifts = list(range(1, group))

    if cube:
        cols = [
            lax.dynamic_slice_in_dim(first_factor, lax.rem(me + shift, group) * width, width, 2)
            for shift in range(2)
        ]
        far = net.gather(cols[1])
        both = gather_plain(jnp.concatenate([second_factor, cols[0]], axis=2))
        second_whole = Whole(both.arrays, both.slots, False, (blk, 0))
        near = Whole(both.arrays, both.slots, False, (width, group))
        columns = [near, far]
    else:
        second_whole = gather_plain(second_factor)
        whole = gather_plain(first_factor).arrays[0]
        if whole.shape[0] > 1:
            whole = jnp.transpose(whole, (1, 0, 2, 3)).reshape(1, local, blk, blk)
        turned = jnp.roll(whole, -me * width, axis=3)
        near, far, turned = [
            Whole([array], [[0]], False) for array in (turned[..., :width], turned[..., width:], turned)
        ]
        columns = [turned]
    sends = expand(ids, tokens, far, shifts, j_spans, group, local)
    arrived = [
        [send(sends[(shift - 1) * len(j_spans) + at], shift, group) for shift in shifts]
        for at in range(len(j_spans))
    ]
    own = expand(ids, tokens, near, [0], [(0, local)], group, local)[0]

    held = {}
    backs = [(("back", place), b_span, (0, local)) for place, b_span in enumerate(b_spans)]
    for at, span in enumerate(j_spans):
        mix(
            ids, own, arrived[at], second_whole, tokens, upstream, held, span, group, local, cut, cube,
            ("term", (0, local)), backs,
        )
    returned = [[send(held[(key, shift)], shift, group) for shift in shifts] for key, _, _ in backs]
    parts = [held[("term", place)] for place in range(len(cut))]
    if cube:
        grad_second, marks = net.scatter(parts, scale, JOINED[0])
    else:
        grad_second, marks = scatter_plain(parts[0], rows, scale), []

    grad_tokens, sums, terms, chains = None, [], [], [marks]
    tie = lambda place: [array for chain, step in TIES.get(place, ()) if cube for array in chains[chain][step]]
    for place, b_span in enumerate(b_spans):
        grad_tokens, *parts = fold(
            ids, held["own"], [(array, b_span[0]) for array in returned[place]], tokens, upstream, columns,
            grad_tokens, b_span, group, local, cut, cube, tie(place),
        )
        if cube:
            total, marks = net.scatter(parts, scale, JOINED[1 + place])
            chains.append(marks)
            sums.append(total)
        else:
            terms.append(parts[0])
    if not cube:
        sums = [scatter_plain(jnp.concatenate(terms, axis=1), rows, scale)]
    return held["mixed"], grad_tokens, jnp.concatenate(sums), grad_second


def solution(mesh):
    placed = (P("dp", "mp"), P("dp", "mp"), P("mp", "dp", None), P("mp", "dp", None))
    return jax.shard_map(
        on_device, mesh=mesh, in_specs=placed, out_specs=placed, check_vma=False
    )
```

```python
import functools
import math

import jax
import jax.numpy as jnp
from jax import lax
from jax.experimental import pallas as pl
from jax.experimental.pallas import tpu as pltpu
from jax.sharding import PartitionSpec as P

BF16 = jnp.bfloat16
F32 = jnp.float32
ROOT_HALF = math.sqrt(0.5)
DENSITY = 1.0 / math.sqrt(2.0 * math.pi)
JOINED = (True, False, False, True)
TIES = {0: ((0, 2),), 1: ((1, 1),), 2: ((0, 3), (1, 3), (2, 2))}
VMEM = 20 * 1024 * 1024
LARGE = 1 << 20


def split_even(count, parts):
    parts = min(count, parts)
    edges = [count * step // parts for step in range(parts + 1)]
    return list(zip(edges[:-1], edges[1:]))


def split_by(count, weights):
    total, edges, run = sum(weights), [0], 0
    for weight in weights:
        run += weight
        edges.append(count * run // total)
    return [(lo, hi) for lo, hi in zip(edges[:-1], edges[1:]) if hi > lo]


def dot(left, right, left_dim, right_dim):
    return lax.dot_general(
        left, right, (((left_dim,), (right_dim,)), ((), ())), preferred_element_type=F32
    )


def aligned(index, size):
    return pl.ds(pl.multiple_of(index * size, size), size)


def placed_for(array):
    if array.ndim == 2 or array.ndim == 4 and array.size > LARGE:
        return pltpu.with_memory_space_constraint(array, pltpu.HBM)
    return array


def call(kernel, name, ids, grid, inputs, held, outputs, scratch=(), after=()):
    places = sorted(held)
    extra = [held[place] for place in places] + list(after)
    taken = len(inputs)

    def body(ids_ref, *refs):
        kernel(ids_ref, *refs[:taken], *refs[taken + len(extra) :])

    return pl.pallas_call(
        body,
        grid_spec=pltpu.PrefetchScalarGridSpec(
            num_scalar_prefetch=1,
            grid=grid,
            in_specs=[spec for _, spec in inputs] + [pl.BlockSpec(memory_space=pl.ANY)] * len(extra),
            out_specs=[spec for _, _, spec in outputs],
            scratch_shapes=list(scratch),
        ),
        out_shape=[jax.ShapeDtypeStruct(shape, dtype) for shape, dtype, _ in outputs],
        input_output_aliases={1 + taken + at: place for at, place in enumerate(places)},
        compiler_params=pltpu.CompilerParams(
            dimension_semantics=("arbitrary",) * len(grid), vmem_limit_bytes=VMEM
        ),
        cost_estimate=pl.CostEstimate(flops=1, bytes_accessed=1, transcendentals=0),
        name=name,
    )(ids, *[placed_for(array) for array, _ in inputs], *extra)


class Whole:
    def __init__(self, arrays, slots, relative, lanes=None):
        self.arrays, self.slots, self.relative = arrays, slots, relative
        self.cols, self.lane = lanes or (arrays[0].shape[3], 0)

    def specs(self, count, at):
        return [
            (
                array,
                pl.BlockSpec(
                    (array.shape[0], count, array.shape[2], self.cols),
                    lambda step, _: (0, at(step), 0, self.lane),
                ),
            )
            for array in self.arrays
        ]

    def load(self, refs, block, target, device):
        if not self.relative:
            return refs[0][:, block].reshape(target.shape)
        for ref, slots in zip(refs, self.slots):
            rows = ref.shape[2]
            for place, slot in enumerate(slots):
                target[aligned(lax.bitwise_xor(device, slot), rows), :] = ref[place, block]
        return target[...]


def combos(bits):
    found = [0]
    for bit in bits:
        found += [value | bit for value in found]
    return found


class Network:
    def __init__(self, size):
        bits = [1 << k for k in range(size.bit_length() - 1)]
        self.size = size
        self.near, self.far = bits[:2], bits[2:]
        self.rounds = [(bit,) for bit in bits]
        self.order = [0]
        for bits in reversed(self.rounds):
            self.order = [slot | mask for mask in combos(bits) for slot in self.order]

    def swap(self, array, mask):
        return lax.ppermute(array, "dp", [(at, at ^ mask) for at in range(self.size)])

    def gather(self, shard):
        combo = combos(self.far)
        first = [shard[None]] + [self.swap(shard[None], mask) for mask in combo[1:]]
        have = [(jnp.concatenate(first, axis=0), combo)]
        for mask in reversed(self.near):
            have = have + [(self.swap(array, mask), [slot | mask for slot in slots]) for array, slots in have]
        return Whole([array for array, _ in have], [slots for _, slots in have], True)

    def cut(self, slots, bits):
        mask = sum(bits)
        return [[slot for slot in slots if slot & mask == value] for value in combos(bits)]

    def first_cut(self):
        return self.cut(self.order, self.rounds[0])

    def scatter(self, parts, scale, joined=False):
        rounds = self.rounds[: len(self.near)] + [tuple(self.far)] if joined else self.rounds
        slots = self.first_cut()[0]
        terms, sends, marks = [parts[0]], parts[1:], []
        for step, bits in enumerate(rounds):
            marks.append(sends)
            terms += [self.swap(piece, mask) for piece, mask in zip(sends, combos(bits)[1:])]
            if step + 1 < len(rounds):
                lists = self.cut(slots, rounds[step + 1])
                spans = [(slots.index(members[0]), slots.index(members[-1]) + 1) for members in lists]
                sends = [sum(term[lo:hi].astype(F32) for term in terms).astype(BF16) for lo, hi in spans[1:]]
                terms = [term[spans[0][0] : spans[0][1]] for term in terms]
                slots = lists[0]
        result = sum(term[0].astype(F32) for term in terms) * scale
        return result, marks + [[result]]


def tiles(array, rows, cols, down, along, at):
    return [
        (
            array,
            pl.BlockSpec(
                (rows, cols),
                functools.partial(lambda row, col, step, _: (row, along * at(step) + col), row, col),
            ),
        )
        for row in range(down)
        for col in range(along)
    ]


def expand_kernel(weights, shifts, spans, group, inner, ids, *rest):
    x_refs, rest = rest[:2], rest[2:]
    w_refs, rest = rest[: len(weights.arrays)], rest[len(weights.arrays) :]
    outs, held = rest[:-1], rest[-1]
    blk = held.shape[1]
    halves = []
    for half in range(2):
        weight = weights.load(w_refs, half, held.at[half], ids[1])
        halves.append(dot(x_refs[half][...], weight, 1, 0).astype(BF16).T.astype(F32))
    width = blk // group
    for at, _ in enumerate(shifts):
        parts = [
            full[at * width : (at + 1) * width].reshape(width // inner, inner, -1) for full in halves
        ]
        piece = jnp.concatenate(parts, axis=1).astype(BF16)
        for place, (start, stop) in enumerate(spans):
            outs[at * len(spans) + place][...] = piece[start:stop]


def expand(ids, tokens, weights, shifts, spans, group, local, after=()):
    tok = tokens.shape[0]
    blk = tokens.shape[1] // local
    inner = blk // (local * group)
    cols = len(shifts) * (blk // group)
    shapes = [stop - start for _ in shifts for start, stop in spans]
    return call(
        functools.partial(expand_kernel, weights, shifts, spans, group, inner),
        "expand",
        ids,
        (local // 2,),
        tiles(tokens, tok, blk, 1, 2, lambda pair: pair)
        + weights.specs(2, lambda pair: pair),
        {},
        [
            (
                (count, local * inner, tok),
                BF16,
                pl.BlockSpec((count, 2 * inner, tok), lambda pair, _: (0, pair, 0)),
            )
            for count in shapes
        ],
        [pltpu.VMEM((2, blk, cols), BF16)],
        after,
    )


def order_matrix(blk, blocks, flip):
    inner = blk // blocks
    out = lax.broadcasted_iota(jnp.int32, (blk, blk), 1 if flip else 0)
    held = lax.broadcasted_iota(jnp.int32, (blk, blk), 0 if flip else 1)
    return (held == lax.rem(out, blocks) * inner + lax.div(out, blocks)).astype(F32).astype(BF16)


def store_term(term, slots_lists, relative, outs, scratch, device, block):
    if not relative:
        out = outs[0]
        out[:, block] = term.reshape(out.shape[0], out.shape[2], out.shape[3])
        return
    scratch[...] = term
    for out, slots in zip(outs, slots_lists):
        rows = out.shape[2]
        for place, slot in enumerate(slots):
            out[place, block] = scratch[aligned(lax.bitwise_xor(device, slot), rows), :].astype(out.dtype)


def mix_kernel(weights, cut, relative, group, blocks, backs, ids, own_ref, *rest):
    arrived, rest = rest[: group - 1], rest[group - 1 :]
    w_refs, rest = rest[: len(weights.arrays)], rest[len(weights.arrays) :]
    step = (len(rest) - 6 - len(cut) - len(backs) * (group - 1)) // 2
    x_refs, up_refs, rest = rest[:step], rest[step : 2 * step], rest[2 * step :]
    mixed_ref, back_own_ref = rest[:2]
    term_refs, rest = rest[2 : 2 + len(cut)], rest[2 + len(cut) :]
    back_refs, (moved, back, held, term) = rest[:-4], rest[-4:]
    me = ids[0]
    blk = held.shape[1]
    rows = blk // group
    there = order_matrix(blk, blocks, False)
    again = order_matrix(blk, blocks, True)
    for j in range(held.shape[0]):
        cols = slice(j * blk, (j + 1) * blk)
        moved[j, aligned(me, rows), :] = own_ref[j]
        for shift in range(1, group):
            moved[j, aligned(lax.rem(me - shift + group, group), rows), :] = arrived[shift - 1][j]
        weight = weights.load(w_refs, j, held.at[j], ids[1])
        ordered = dot(there, moved[j], 1, 0).astype(BF16)
        inner_out = dot(ordered.T, weight, 1, 0)
        cdf = 0.5 + 0.5 * lax.erf(inner_out * ROOT_HALF)
        mixed_ref[:, cols] = (x_refs[j][...].astype(F32) + inner_out * cdf).astype(BF16)
        slope = cdf + inner_out * (DENSITY * jnp.exp(-0.5 * inner_out * inner_out))
        grad_out = (up_refs[j][...].astype(F32) * slope).astype(BF16)
        store_term(dot(ordered, grad_out, 1, 0), cut, relative, term_refs, term.at[j], ids[1], j)
        returned = dot(weight, grad_out, 1, 1).astype(BF16)
        back[j] = dot(again, returned, 1, 0).astype(BF16)
        back_own_ref[j] = back[j, aligned(me, rows), :]
        for shift in range(1, group):
            piece = back[j, aligned(lax.rem(me + shift, group), rows), :]
            for at, (start, stop) in enumerate(backs):
                back_refs[(shift - 1) * len(backs) + at][j] = piece[start:stop]


def mix(ids, own, arrived, weights, tokens, upstream, held, span, group, local, cut, relative, term, backs):
    tok = tokens.shape[0]
    blk = tokens.shape[1] // local
    feat = blk // group
    per = feat // local
    first, last = span
    rows = blk // sum(len(slots) for slots in cut)
    step = math.gcd(2, math.gcd(first, last))
    lane = pl.BlockSpec((tok, step * blk), lambda j, _: (0, first // step + j))
    at = pl.BlockSpec((step, feat, tok), lambda j, _: (first // step + j, 0, 0))
    keys = ["mixed", "own"]
    outs = [(tokens.shape, BF16, lane), ((local, feat, tok), BF16, at)]
    term_key, (term_first, term_last) = term
    for place, slots in enumerate(cut):
        keys.append((term_key, place))
        outs.append(
            (
                (len(slots), term_last - term_first, rows, blk),
                F32 if place == 0 else BF16,
                pl.BlockSpec((len(slots), step, rows, blk), lambda j, _: (0, (first - term_first) // step + j, 0, 0)),
            )
        )
    for shift in range(1, group):
        for key, (b_first, b_last), (j_first, j_last) in backs:
            keys.append((key, shift))
            outs.append(
                (
                    (j_last - j_first, (b_last - b_first) * per, tok),
                    BF16,
                    pl.BlockSpec(
                        (step, (b_last - b_first) * per, tok),
                        functools.partial(lambda start, j, _: (start + j, 0, 0), (first - j_first) // step),
                    ),
                )
            )
    kept = {place: held[key] for place, key in enumerate(keys) if key in held}
    cuts = [(b_first * per, b_last * per) for _, (b_first, b_last), _ in backs]
    got = call(
        functools.partial(mix_kernel, weights, cut, relative, group, local * group, cuts),
        "mix",
        ids,
        ((last - first) // step,),
        [(own, at)]
        + [(array, pl.BlockSpec((step, feat, tok), lambda j, _: (j, 0, 0))) for array in arrived]
        + weights.specs(step, lambda j: first // step + j)
        + tiles(tokens, tok, blk, 1, step, lambda j: first // step + j)
        + tiles(upstream, tok, blk, 1, step, lambda j: first // step + j),
        kept,
        outs,
        [
            pltpu.VMEM((step, blk, tok), BF16),
            pltpu.VMEM((step, blk, tok), BF16),
            pltpu.VMEM((step, blk, blk), BF16),
            pltpu.VMEM((step, blk, blk), F32),
        ],
    )
    held.update(zip(keys, got))


def fold_kernel(columns, cut, relative, group, inner, pieces, ids, own_ref, *rest):
    arrived, rest = rest[: pieces * (group - 1)], rest[pieces * (group - 1) :]
    x_refs, up_refs, rest = rest[:2], rest[2:4], rest[4:]
    w_refs = []
    for weights in columns:
        w_refs.append(rest[: len(weights.arrays)])
        rest = rest[len(weights.arrays) :]
    out_ref, term_refs = rest[0], rest[1:-4]
    inner_grad, held, sorted_term, term = rest[-4:]
    me = ids[0]
    blk = held.shape[2]
    width = blk // group
    for shift in range(group):
        if shift == 0:
            piece = own_ref[...]
        else:
            refs = arrived[(shift - 1) * pieces : shift * pieces]
            piece = jnp.concatenate([ref[...] for ref in refs], axis=0)
        piece = piece.astype(F32)
        for half in range(2):
            part = piece[:, half * inner : (half + 1) * inner].reshape(width, -1)
            inner_grad[half, shift * width : (shift + 1) * width, :] = part.astype(BF16)
    for half in range(2):
        cols = slice(half * blk, (half + 1) * blk)
        if len(columns) == 1:
            weight = columns[0].load(w_refs[0], half, held.at[half], ids[1])
        else:
            start = 0
            for weights, refs in zip(columns, w_refs):
                size = weights.cols
                part = held.at[half, :, start : start + size]
                part[...] = weights.load(refs, half, part, ids[1])
                start += size
            weight = held[half]
        du = inner_grad[half]
        unsorted = dot(du, x_refs[half][...], 1, 0)
        for shift in range(group):
            source = lax.rem(me - shift + group, group)
            sorted_term[half, aligned(source, width), :] = unsorted[shift * width : (shift + 1) * width]
        store_term(sorted_term[half].T, cut, relative, term_refs, term.at[half], ids[1], half)
        back = dot(du.T, weight, 1, 1)
        out_ref[:, cols] = (up_refs[half][...].astype(F32) + back).astype(BF16)


def fold(ids, own, arrived, tokens, upstream, columns, grad_tokens, span, group, local, cut, relative, after):
    tok = tokens.shape[0]
    blk = tokens.shape[1] // local
    inner = blk // (local * group)
    first, last = span
    rows = blk // sum(len(slots) for slots in cut)
    start = first // 2
    lane = pl.BlockSpec((tok, 2 * blk), lambda pair, _: (0, start + pair))
    inputs = []
    for array, begin in [(own, 0)] + arrived:
        at = functools.partial(lambda skip, pair, _: (0, skip + pair, 0), start - begin // 2)
        inputs.append((array, pl.BlockSpec((array.shape[0], 2 * inner, tok), at)))
    for array in (tokens, upstream):
        inputs += tiles(array, tok, blk, 1, 2, lambda pair: start + pair)
    for weights in columns:
        inputs += weights.specs(2, lambda pair: start + pair)
    outs = [(tokens.shape, BF16, lane)] + [
        (
            (len(slots), last - first, rows, blk),
            F32 if place == 0 else BF16,
            pl.BlockSpec((len(slots), 2, rows, blk), lambda pair, _: (0, pair, 0, 0)),
        )
        for place, slots in enumerate(cut)
    ]
    pieces = len(arrived) // (group - 1)
    held = {} if grad_tokens is None else {0: grad_tokens}
    return call(
        functools.partial(fold_kernel, columns, cut, relative, group, inner, pieces),
        "fold",
        ids,
        ((last - first) // 2,),
        inputs,
        held,
        outs,
        [
            pltpu.VMEM((2, blk, tok), BF16),
            pltpu.VMEM((2, blk, blk), BF16),
            pltpu.VMEM((2, blk, blk), F32),
            pltpu.VMEM((2, blk, blk), F32),
        ],
        after,
    )


def send(array, shift, group):
    return lax.ppermute(array, "mp", [(at, (at + shift) % group) for at in range(group)])


def gather_plain(shard):
    local, rows, blk = shard.shape
    whole = lax.all_gather(shard, "dp", axis=0, tiled=False)
    if rows % 16:
        whole = jnp.transpose(whole, (1, 0, 2, 3)).reshape(1, local, whole.shape[0] * rows, blk)
    return Whole([whole], [list(range(whole.shape[0]))], False)


def scatter_plain(term, rows, scale):
    if term.shape[2] != rows:
        _, count, whole, blk = term.shape
        term = jnp.transpose(term.reshape(count, whole // rows, rows, blk), (1, 0, 2, 3))
    return lax.psum_scatter(term, "dp", scatter_dimension=0, tiled=False) * scale


def on_device(tokens, upstream, first_factor, second_factor):
    local, rows, blk = first_factor.shape
    group, size = lax.axis_size("mp"), lax.axis_size("dp")
    width = blk // group
    scale = 1.0 / math.sqrt(tokens.shape[0] * size)
    me, device = lax.axis_index("mp"), lax.axis_index("dp")
    ids = jnp.stack([me, device]).astype(jnp.int32)
    cube = group == 2 and size >= 8 and size & (size - 1) == 0 and rows % 16 == 0 and width % 128 == 0
    net = Network(size) if cube else None
    cut = net.first_cut() if cube else [[0]]
    plain_cut = [list(range(size))] if cube else [[0]]
    j_spans = split_by(local, (3, 2, 2, 1)) if cube else split_even(local, 4)
    b_spans = [(2 * lo, 2 * hi) for lo, hi in split_by(local // 2, (3, 3, 2))]
    shifts = list(range(1, group))

    if cube:
        cols = [
            lax.dynamic_slice_in_dim(first_factor, lax.rem(me + shift, group) * width, width, 2)
            for shift in range(2)
        ]
        far = net.gather(cols[1])
        both = gather_plain(jnp.concatenate([second_factor, cols[0]], axis=2))
        second_whole = Whole(both.arrays, both.slots, False, (blk, 0))
        near = Whole(both.arrays, both.slots, False, (width, group))
        columns = [near, far]
    else:
        second_whole = gather_plain(second_factor)
        whole = gather_plain(first_factor).arrays[0]
        if whole.shape[0] > 1:
            whole = jnp.transpose(whole, (1, 0, 2, 3)).reshape(1, local, blk, blk)
        turned = jnp.roll(whole, -me * width, axis=3)
        near, far, turned = [
            Whole([array], [[0]], False) for array in (turned[..., :width], turned[..., width:], turned)
        ]
        columns = [turned]
    sends = expand(ids, tokens, far, shifts, j_spans, group, local)
    arrived = [
        [send(sends[(shift - 1) * len(j_spans) + at], shift, group) for shift in shifts]
        for at in range(len(j_spans))
    ]
    own = expand(ids, tokens, near, [0], [(0, local)], group, local)[0]

    held = {}
    backs = [(("back", place), b_span, (0, local)) for place, b_span in enumerate(b_spans)]
    for at, span in enumerate(j_spans):
        mix(
            ids, own, arrived[at], second_whole, tokens, upstream, held, span, group, local, cut, cube,
            ("term", (0, local)), backs,
        )
    returned = [[send(held[(key, shift)], shift, group) for shift in shifts] for key, _, _ in backs]
    parts = [held[("term", place)] for place in range(len(cut))]
    if cube:
        grad_second, marks = net.scatter(parts, scale, JOINED[0])
    else:
        grad_second, marks = scatter_plain(parts[0], rows, scale), []

    grad_tokens, sums, terms, chains = None, [], [], [marks]
    tie = lambda place: [array for chain, step in TIES.get(place, ()) if cube for array in chains[chain][step]]
    for place, b_span in enumerate(b_spans):
        grad_tokens, *parts = fold(
            ids, held["own"], [(array, b_span[0]) for array in returned[place]], tokens, upstream, columns,
            grad_tokens, b_span, group, local, cut, cube, tie(place),
        )
        if cube:
            total, marks = net.scatter(parts, scale, JOINED[1 + place])
            chains.append(marks)
            sums.append(total)
        else:
            terms.append(parts[0])
    if not cube:
        sums = [scatter_plain(jnp.concatenate(terms, axis=1), rows, scale)]
    return held["mixed"], grad_tokens, jnp.concatenate(sums), grad_second


def solution(mesh):
    placed = (P("dp", "mp"), P("dp", "mp"), P("mp", "dp", None), P("mp", "dp", None))
    return jax.shard_map(
        on_device, mesh=mesh, in_specs=placed, out_specs=placed, check_vma=False
    )
```
